32 devices in a mesh: dp: 4 (over y, core), expert: 8 (over z, x).
Axes of the slice: x: 2, y: 2, z: 4, core: 2. Of those that a mesh axis runs over, the one named last changes fastest.
Arguments:
- block_input: bfloat16 [192, 196, 384], P(('dp', 'expert')), may hold values from -6 to 6
- routes: int32 [2, 192, 196, 1], P(None, ('dp', 'expert')), may hold values from 0 to 7, as said below
- first_gain: float32 [2, 384], replicated, may hold values from 0.5 to 1.5
- first_shift: float32 [2, 384], replicated, may hold values from -2.5 to 2.5
- attend_weight: bfloat16 [2, 384, 1152], replicated, may hold values from -0.3125 to 0.3125
- bias_table: float32 [2, 169, 12], replicated, may hold values from -4 to 4
- output_weight: bfloat16 [2, 384, 384], replicated, may hold values from -1.25 to 1.25
- second_gain: float32 [2, 384], replicated, may hold values from 0.5 to 1.5
- second_shift: float32 [2, 384], replicated, may hold values from -2.5 to 2.5
- router_weight: bfloat16 [2, 384, 8], replicated, may hold values from -0.21875 to 0.21875
- core_up: bfloat16 [2, 384, 1536], replicated, may hold values from -0.3125 to 0.3125
- core_down: bfloat16 [2, 1536, 384], replicated, may hold values from -2.5 to 2.5
- residual_up: bfloat16 [2, 384, 12288], P(None, None, 'expert'), may hold values from -0.15625 to 0.15625
- residual_down: bfloat16 [2, 12288, 384], P(None, 'expert'), may hold values from -1.25 to 1.25
- cotangent: bfloat16 [192, 196, 384], P(('dp', 'expert')), may hold values from -6 to 6
Outputs:
- block_output: bfloat16 [192, 196, 384], P(('dp', 'expert'))
- input_grad: bfloat16 [192, 196, 384], P(('dp', 'expert'))
- first_gain_grad: float32 [2, 384], replicated
- first_shift_grad: float32 [2, 384], replicated
- attend_weight_grad: float32 [2, 384, 1152], replicated
- bias_table_grad: float32 [2, 169, 12], replicated
- output_weight_grad: float32 [2, 384, 384], replicated
- second_gain_grad: float32 [2, 384], replicated
- second_shift_grad: float32 [2, 384], replicated
- router_weight_grad: float32 [2, 384, 8], replicated
- core_up_grad: float32 [2, 384, 1536], replicated
- core_down_grad: float32 [2, 1536, 384], replicated
- residual_up_grad: float32 [2, 384, 12288], P(None, None, 'expert')
- residual_down_grad: float32 [2, 12288, 384], P(None, 'expert')
The draws below stay inside these ranges and needn't reach their ends.
Inputs may be any that keep to these rules, and one draw needn't show every extreme that they name: `routes`: each token's expert in each block; every expert is named by some token; in each block one expert, drawn from the seed, is named by about two fifths of all tokens.
All inputs are finite; a program needn't handle non-finite values.
Results may differ from the reference program's by a relative error of at most 0.022.
Values may be sent and summed in bfloat16 or wider, within the bound.
No kernel may reach another device: no remote copies, remote signals or barrier semaphores. Data moves between devices by JAX's collectives and lax.ppermute only.
A program may use at most 256 MiB of HBM per device.

```python
import jax
import jax.numpy as jnp
from jax import lax

D = 384
HEADS = 12
HD = 32
FF = 1536
EXPERTS = 8
WIN = 7
SIDE = 14
SHIFT = 3
LAYERS = 2
IMG_DEV = 6
HW = 196
TOK_DEV = 1176
IMAGES = 192
CAP = 184
HSPLIT = 1
FFS = 1536
OFFSETS = 169


def draw_routes(key, part):
    key = jax.random.fold_in(key, 11)
    favoured = jax.random.randint(jax.random.fold_in(key, 1), (LAYERS,), 0, EXPERTS)
    chance = jax.random.randint(jax.random.fold_in(key, 2), (LAYERS, IMAGES, HW), 0, 1000)
    others = jax.random.randint(jax.random.fold_in(key, 3), (LAYERS, IMAGES, HW), 0, EXPERTS)
    picks = jnp.where(chance < 314, favoured[:, None, None], others)
    image_ids = jnp.arange(IMAGES, dtype=jnp.int32)[None, :, None]
    token_ids = jnp.arange(HW, dtype=jnp.int32)[None, None, :]
    forced = (image_ids == 0) & (token_ids < EXPERTS)
    picks = jnp.where(forced, token_ids, picks)
    return picks.astype(jnp.int32)[..., None]


def block_levels(rng, shape, cuts, least, largest):
    def one(dim, shards_of):
        steps = jax.random.uniform(jax.random.fold_in(jax.random.fold_in(rng, 6), dim), (shards_of,), jnp.float32, least / len(cuts), largest / len(cuts))
        return jnp.repeat(jnp.exp(steps), shape[dim] // shards_of).reshape((-1,) + (1,) * (len(shape) - dim - 1))

    level = one(*cuts[0])
    for cut in cuts[1:]:
        level = level * one(*cut)
    return level


def scatter_about(own_key, shape, scale, limit, split=(), kind=jnp.bfloat16):
    entries = scale * jax.random.normal(own_key, shape, jnp.float32)
    if split:
        entries = entries * block_levels(own_key, shape, split, -0.22, 0.18)
    return jnp.clip(entries, -limit, limit).astype(kind)


def setup_inputs(seed: int = 0) -> dict:
    key_of = jax.random.split(jax.random.key(seed), 16)
    return {
        "block_input": scatter_about(key_of[0], (IMAGES, HW, D), 1.0, 6.0, ((0, 32),)),
        "routes": draw_routes(jax.random.fold_in(key_of[15], 71), 0),
        "first_gain": jnp.clip(1.0 + 0.1 * jax.random.normal(key_of[2], (LAYERS, D), jnp.float32), 0.5, 1.5),
        "first_shift": scatter_about(key_of[3], (LAYERS, D), 0.3, 2.5, (), jnp.float32),
        "attend_weight": scatter_about(key_of[4], (LAYERS, D, 3 * D), D ** -0.5, 0.3125),
        "bias_table": scatter_about(key_of[5], (LAYERS, OFFSETS, HEADS), 1.0, 4.0, (), jnp.float32),
        "output_weight": scatter_about(key_of[6], (LAYERS, D, D), (max(D // 16, 1)) ** -0.5, 1.25),
        "second_gain": jnp.clip(1.0 + 0.1 * jax.random.normal(key_of[7], (LAYERS, D), jnp.float32), 0.5, 1.5),
        "second_shift": scatter_about(key_of[8], (LAYERS, D), 0.3, 2.5, (), jnp.float32),
        "router_weight": scatter_about(key_of[9], (LAYERS, D, EXPERTS), (2 * D) ** -0.5, 0.21875),
        "core_up": scatter_about(key_of[10], (LAYERS, D, FF), D ** -0.5, 0.3125),
        "core_down": scatter_about(key_of[11], (LAYERS, FF, D), (max(FF // 256, 1)) ** -0.5, 2.5),
        "residual_up": scatter_about(key_of[12], (LAYERS, D, EXPERTS * FF), (4 * D) ** -0.5, 0.15625, ((2, 8),)),
        "residual_down": scatter_about(key_of[13], (LAYERS, EXPERTS * FF, D), (max(FF // 64, 1)) ** -0.5, 1.25, ((1, 8),)),
        "cotangent": scatter_about(key_of[14], (IMAGES, HW, D), 1.0, 6.0, ((0, 32),)),
    }


@jax.custom_vjp
def low(v):
    return lax.optimization_barrier(v.astype(jnp.bfloat16)).astype(jnp.float32)

@jax.custom_vjp
def low_back(v):
    return v

def low_keep(v):
    return (low(v), None)

def low_pass(kept, grad):
    return (grad,)

def back_keep(v):
    return (v, None)

def back_low(kept, grad):
    return (low(grad),)
low.defvjp(low_keep, low_pass)
low_back.defvjp(back_keep, back_low)
eps_norm = 1e-05
mask_fill = -100.0
precise = lax.Precision.HIGHEST

def layer_norm(values, norm_gain, norm_shift):
    middle = lax.optimization_barrier(jnp.mean(values, axis=-1, keepdims=True))
    centred = values - middle
    spread = lax.optimization_barrier(jnp.mean(centred * centred, axis=-1, keepdims=True))
    return centred * lax.rsqrt(spread + eps_norm) * norm_gain + norm_shift

def to_windows(grid_in, window):
    images = grid_in.shape[0]
    grid_side = grid_in.shape[1]
    channels = grid_in.shape[3]
    per_side = grid_side // window
    pieces = grid_in.reshape(images, per_side, window, per_side, window, channels)
    return pieces.transpose(0, 1, 3, 2, 4, 5).reshape(images * per_side * per_side, window * window, channels)

def from_windows(blocks, images, grid_side, window):
    per_side = grid_side // window
    channels = blocks.shape[-1]
    pieces = blocks.reshape(images, per_side, per_side, window, window, channels)
    return pieces.transpose(0, 1, 3, 2, 4, 5).reshape(images, grid_side, grid_side, channels)

def relative_index(window):
    places = jnp.arange(window * window, dtype=jnp.int32)
    rows_at = places // window
    cols_at = places % window
    row_delta = rows_at[:, None] - rows_at[None, :] + window - 1
    col_delta = cols_at[:, None] - cols_at[None, :] + window - 1
    return row_delta * (2 * window - 1) + col_delta

def band_mask(grid_side, window, offset):
    coords = jnp.arange(grid_side, dtype=jnp.int32)
    bands = (coords >= grid_side - window).astype(jnp.int32) + (coords >= grid_side - offset).astype(jnp.int32)
    labels = bands[:, None] * 3 + bands[None, :]
    pieces = to_windows(labels[None, :, :, None], window)[:, :, 0]
    return jnp.where(pieces[:, :, None] == pieces[:, None, :], 0.0, mask_fill).astype(jnp.float32)

def attention(normed, attend_w, bias_rows, output_w, offset):
    images = normed.shape[0]
    length = WIN * WIN
    rolled = jnp.roll(normed, (-offset, -offset), axis=(1, 2))
    blocks = low(to_windows(rolled, WIN))
    count_windows = blocks.shape[0]
    joined = low(low_back(jnp.einsum('wld,de->wle', blocks, attend_w, precision=precise)))
    head_split = joined.reshape(count_windows, length, 3, HEADS, HD)
    queries = head_split[:, :, 0]
    key_heads = head_split[:, :, 1]
    value_heads = head_split[:, :, 2]
    position = jnp.take(bias_rows, relative_index(WIN).reshape(-1), axis=0).reshape(length, length, HEADS).transpose(2, 0, 1)
    scores = jnp.einsum('wqhd,wkhd->whqk', queries, key_heads, precision=precise) * HD ** (-0.5) + position[None]
    masked = scores.reshape(images, -1, HEADS, length, length) + band_mask(SIDE, WIN, offset)[None, :, None]
    scores = low_back(masked.reshape(count_windows, HEADS, length, length))
    weights = low(jax.nn.softmax(scores, axis=-1))
    mixed = jnp.einsum('whqk,wkhd->wqhd', weights, value_heads, precision=precise)
    mixed = low(low_back(mixed.reshape(count_windows, length, D)))
    result = low_back(jnp.einsum('wld,de->wle', mixed, output_w, precision=precise))
    return jnp.roll(from_windows(result, images, SIDE, WIN), (offset, offset), axis=(1, 2))

def one_layer(carried, params, route_ids, offset):
    gain_one, shift_one, attend_w, bias_rows, output_w, gain_two, shift_two, router_w, up_core, down_core, up_res, down_res = params
    grid_in = carried.reshape(IMG_DEV, SIDE, SIDE, D)
    middle = grid_in + attention(layer_norm(grid_in, gain_one, shift_one), attend_w, bias_rows, output_w, offset)
    tokens = middle.reshape(TOK_DEV, D)
    normed = low(layer_norm(tokens, gain_two, shift_two))
    logits = low_back(jnp.dot(normed, router_w, precision=precise))
    router_probs = jax.nn.softmax(logits, axis=-1)
    chosen = route_ids[:, None] == jnp.arange(EXPERTS, dtype=jnp.int32)[None, :]
    gate_values = lax.optimization_barrier(jnp.sum(jnp.where(chosen, router_probs, 0.0), axis=-1))
    rank_counts = jnp.cumsum(chosen.astype(jnp.int32), axis=0) - 1
    slot_index = lax.optimization_barrier(jnp.sum(jnp.where(chosen, rank_counts, 0), axis=-1))
    target = jnp.where(slot_index < CAP, route_ids * CAP + slot_index, EXPERTS * CAP)
    placing = (target[:, None] == jnp.arange(EXPERTS * CAP, dtype=jnp.int32)[None, :]).astype(jnp.float32)
    buffers = jnp.einsum('ts,td->sd', placing, normed, precision=precise).reshape(EXPERTS, 1, CAP, D)
    up_full = low(up_core[None] + up_res.reshape(D, EXPERTS, FF).transpose(1, 0, 2))
    down_full = low(down_core[None] + down_res.reshape(EXPERTS, FF, D))
    copies = low_back(jnp.broadcast_to(buffers, (EXPERTS, HSPLIT, CAP, D)))
    inner_act = low_back(jnp.einsum('escd,edsf->escf', copies, up_full.reshape(EXPERTS, D, HSPLIT, FFS), precision=precise))
    hidden = low(jax.nn.gelu(inner_act, approximate=False))
    part_out = low(low_back(jnp.einsum('escf,esfd->escd', hidden, down_full.reshape(EXPERTS, HSPLIT, FFS, D), precision=precise)))
    expert_out = lax.optimization_barrier(jnp.sum(part_out, axis=1)).reshape(EXPERTS * CAP, D)
    padded = jnp.concatenate([expert_out, jnp.zeros((1, D), jnp.float32)], axis=0)
    returned = jnp.take(padded, target, axis=0)
    return (tokens + gate_values[:, None] * returned).reshape(IMG_DEV, HW, D)

def reference(block_input, routes, first_gain, first_shift, attend_weight, bias_table, output_weight, second_gain, second_shift, router_weight, core_up, core_down, residual_up, residual_down, cotangent):
    block_count = IMAGES // IMG_DEV
    weights = tuple((array.astype(jnp.float32) for array in (first_gain, first_shift, attend_weight, bias_table, output_weight, second_gain, second_shift, router_weight, core_up, core_down, residual_up, residual_down)))
    inputs = block_input.astype(jnp.float32).reshape(block_count, IMG_DEV, HW, D)
    outward = cotangent.astype(jnp.float32).reshape(block_count, IMG_DEV, HW, D)
    route_blocks = routes.reshape(LAYERS, block_count, TOK_DEV).transpose(1, 0, 2)

    def block_step(running, pieces):
        block_in, block_routes, block_cot = pieces

        def forward(carried, params):
            for depth in range(LAYERS):
                carried = one_layer(carried, tuple((array[depth] for array in params)), block_routes[depth], SHIFT * (depth % 2))
            return carried
        result, pullback = jax.vjp(forward, block_in, weights)
        grad_in, grad_params = pullback(block_cot)
        running = tuple((before + addend for before, addend in zip(running, grad_params)))
        return (running, (result.astype(jnp.bfloat16), grad_in.astype(jnp.bfloat16)))
    start = tuple((jnp.zeros_like(array) for array in weights))
    totals, (results, grads) = lax.scan(block_step, start, (inputs, route_blocks, outward))
    gain_one_grad, shift_one_grad, attend_grad, table_grad, output_grad, gain_two_grad, shift_two_grad, router_grad, up_core_grad, down_core_grad, up_res_grad, down_res_grad = totals
    return (results.reshape(IMAGES, HW, D), grads.reshape(IMAGES, HW, D), gain_one_grad, shift_one_grad, attend_grad, table_grad, output_grad, gain_two_grad, shift_two_grad, router_grad, up_core_grad, down_core_grad, up_res_grad, down_res_grad)
```

```python
from functools import partial

import jax
import jax.numpy as jnp
import numpy as np
from jax import lax
from jax.experimental import pallas as pl
from jax.experimental.pallas import tpu as pltpu
from jax.sharding import PartitionSpec as P

D = 384
HEADS = 12
HD = 32
FF = 1536
EXPERTS = 8
WIN = 7
SIDE = 14
SHIFT = 3
LAYERS = 2
HW = 196
CAP = 184
OFFSETS = 169
SLOTS = EXPERTS * CAP

WINDOWS = (SIDE // WIN) * (SIDE // WIN)
LENGTH = WIN * WIN
LPAD = 64
WROWS = WINDOWS * LPAD
TPAD = 256
LANES = 128
GROUP = LANES // HD
GROUPS = HEADS // GROUP
GW = GROUP * LPAD
FCHUNK = 384

F32 = jnp.float32
BF16 = jnp.bfloat16
eps_norm = 1e-05
mask_fill = -100.0
pad_fill = -1e30
score_scale = HD ** (-0.5)
VMEM_BYTES = 56 * 1024 * 1024

NN = (((1,), (0,)), ((), ()))
NT = (((1,), (1,)), ((), ()))
TN = (((0,), (0,)), ((), ()))


def mm(a, b, dims=NN):
    return lax.dot_general(a, b, dims, preferred_element_type=F32)


def window_tokens(offset):
    rows = np.full((WINDOWS, LPAD), -1, np.int64)
    per_side = SIDE // WIN
    for w in range(WINDOWS):
        for i in range(LENGTH):
            r = (w // per_side) * WIN + i // WIN
            c = (w % per_side) * WIN + i % WIN
            rows[w, i] = ((r + offset) % SIDE) * SIDE + (c + offset) % SIDE
    return rows.reshape(-1)


def permutation(offset):
    rows = window_tokens(offset)
    return (rows[:, None] == np.arange(HW)[None, :]).astype(np.float32)


def score_mask(offset):
    coords = np.arange(SIDE)
    bands = (coords >= SIDE - WIN).astype(int) + (coords >= SIDE - offset).astype(int)
    labels = bands[:, None] * 3 + bands[None, :]
    per_side = SIDE // WIN
    out = np.zeros((WINDOWS, LPAD, LPAD), np.float32)
    for w in range(WINDOWS):
        r0, c0 = (w // per_side) * WIN, (w % per_side) * WIN
        flat = labels[r0 : r0 + WIN, c0 : c0 + WIN].reshape(-1)
        out[w, :LENGTH, :LENGTH] = np.where(flat[:, None] == flat[None, :], 0.0, mask_fill)
        out[w, LENGTH:, :] = pad_fill
    return np.tile(out, (1, 1, GROUP))


def offset_table():
    i = np.arange(LENGTH)
    r, c = i // WIN, i % WIN
    index = np.full((LPAD, LPAD), -1, np.int64)
    index[:LENGTH, :LENGTH] = (
        (r[None, :] - r[:, None] + WIN - 1) * (2 * WIN - 1) + c[None, :] - c[:, None] + WIN - 1
    )
    return index.reshape(-1)


def norm_parts(x):
    centred = x - jnp.mean(x, axis=-1, keepdims=True)
    inverse = lax.rsqrt(jnp.mean(centred * centred, axis=-1, keepdims=True) + eps_norm)
    return centred * inverse, inverse


def norm_back(grad, unit, inverse, gain):
    scaled = grad * gain
    return inverse * (
        scaled
        - jnp.mean(scaled, axis=-1, keepdims=True)
        - unit * jnp.mean(scaled * unit, axis=-1, keepdims=True)
    )


def one_hot(cond):
    return jnp.where(cond, 1.0, 0.0).astype(BF16)


def head_masks():
    lane = lax.broadcasted_iota(jnp.int32, (1, LANES), 1) // HD
    return [jnp.where(lane == h, 1.0, 0.0) for h in range(GROUP)]


def spread_heads(block, masks):
    return jnp.concatenate([block * m.astype(BF16) for m in masks], axis=0)


def fold_heads(tall, masks):
    total = tall[0:LPAD] * masks[0]
    for h in range(1, GROUP):
        total = total + tall[h * LPAD : (h + 1) * LPAD] * masks[h]
    return total


def as_column(row, count):
    wide = jnp.broadcast_to(row.astype(F32), (8, TPAD))
    return wide.T[:count, 0:1].astype(jnp.int32)


def pick_rows(target_row, parts):
    column = as_column(target_row, HW)
    place = one_hot(lax.broadcasted_iota(jnp.int32, (HW, SLOTS), 1) == column)
    total = mm(place, parts[0])
    for k in range(1, parts.shape[0]):
        total = total + mm(place, parts[k])
    return total


def send_rows(out_ref, target_all, rows):
    step = SLOTS // 4
    for c in range(4):
        slot = lax.broadcasted_iota(jnp.int32, (step, rows.shape[0]), 0) + c * step
        out_ref[c * step : (c + 1) * step] = mm(one_hot(slot == target_all), rows).astype(BF16)


def gelu_parts(u):
    x = jnp.abs(u) * (0.5**0.5)
    t = 1.0 / (1.0 + 0.3275911 * x)
    bell = jnp.exp(-0.5 * u * u)
    poly = t * (
        0.254829592
        + t * (-0.284496736 + t * (1.421413741 + t * (-1.453152027 + t * 1.061405429)))
    )
    tail = 0.5 * poly * bell
    cdf = jnp.where(u >= 0.0, 1.0 - tail, tail)
    return u * cdf, cdf + u * bell * 0.3989422804014327


def routing_kernel(routes_ref, target_ref):
    before = one_hot(
        lax.broadcasted_iota(jnp.int32, (TPAD, TPAD), 0)
        <= lax.broadcasted_iota(jnp.int32, (TPAD, TPAD), 1)
    )
    expert = lax.broadcasted_iota(jnp.int32, (16, TPAD), 0)
    for depth in range(LAYERS):
        carry = jnp.zeros((16, 1), F32)
        for i in range(routes_ref.shape[1]):
            row = routes_ref[depth, i : i + 1, :]
            chosen = jnp.where(expert == row, 1.0, 0.0)
            counts = mm(chosen.astype(BF16), before) + carry
            carry = counts[:, TPAD - 1 : TPAD]
            slot = jnp.sum(chosen * counts, axis=0, keepdims=True).astype(jnp.int32) - 1
            kept = (slot >= 0) & (slot < CAP)
            target_ref[depth, i : i + 1, :] = jnp.where(kept, row * CAP + slot, -1)


def run_routing(routes):
    return pl.pallas_call(
        routing_kernel,
        out_shape=jax.ShapeDtypeStruct(routes.shape, jnp.int32),
        name="routing",
    )(routes)


def transposed_scores(qkv, w, g, bias_ref, mask_ref, masks):
    rows = slice(w * LPAD, (w + 1) * LPAD)
    q = qkv[rows, g * LANES : (g + 1) * LANES]
    k = qkv[rows, D + g * LANES : D + (g + 1) * LANES]
    v = qkv[rows, 2 * D + g * LANES : 2 * D + (g + 1) * LANES]
    q_wide = spread_heads(q, masks)
    scores = (
        mm(k, q_wide, NT) * score_scale
        + bias_ref[:, g * GW : (g + 1) * GW]
        + mask_ref[w]
    )
    raised = jnp.exp(scores - jnp.max(scores, axis=0, keepdims=True))
    return q_wide, k, v, raised * (1.0 / jnp.sum(raised, axis=0, keepdims=True))


def forward_kernel(depth, images, *refs):
    last = depth == LAYERS - 1
    refs = list(refs)
    take = lambda: refs.pop(0)
    x_ref = take()
    if depth:
        back_ref, gate_in_ref, target_in_ref = take(), take(), take()
    if last:
        cot_ref = take()
    (route_ref, target_ref, g1_ref, s1_ref, g2_ref, s2_ref, attend_ref, out_w_ref) = refs[:8]
    (router_ref, bias_ref, mask_ref, perm_ref, perm_back_ref) = refs[8:13]
    refs = refs[13:]
    (qkv_ref, a_ref, mixed_ref, mid_ref, n_ref, probs_ref, gate_ref, buf_ref) = refs[:8]
    refs = refs[8:]
    if depth:
        x_out_ref, picked_ref = take(), take()
    if last:
        dy_buf_ref = take()
    rows_ref = take()
    if last:
        dy_rows_ref = take()

    step = pl.program_id(0)

    @pl.when(step == 0)
    def _():
        rows_ref[...] = jnp.zeros_like(rows_ref)
        if last:
            dy_rows_ref[...] = jnp.zeros_like(dy_rows_ref)

    x = x_ref[0].astype(F32)
    if depth:
        picked = pick_rows(target_in_ref[0], back_ref)
        picked_ref[0] = picked.astype(picked_ref.dtype)
        x = x + gate_in_ref[0][:, 0:1] * picked
        x_out_ref[0] = x
    unit, _ = norm_parts(x)
    normed = (unit * g1_ref[depth : depth + 1] + s1_ref[depth : depth + 1]).astype(BF16)
    a = mm(perm_ref[...], normed).astype(BF16)
    a_ref[0] = a
    qkv_ref[0] = mm(a, attend_ref[0]).astype(BF16)
    masks = head_masks()
    for w in range(WINDOWS):
        for g in range(GROUPS):
            _, _, v, probs = transposed_scores(qkv_ref.at[0], w, g, bias_ref, mask_ref, masks)
            mixed = fold_heads(mm(probs.astype(BF16), v, TN), masks)
            mixed_ref[0, w * LPAD : (w + 1) * LPAD, g * LANES : (g + 1) * LANES] = mixed.astype(
                BF16
            )
    mixed = mm(perm_back_ref[...], mixed_ref[0]).astype(BF16)
    mid = x + mm(mixed, out_w_ref[0])
    mid_ref[0] = mid
    unit, _ = norm_parts(mid)
    n = (unit * g2_ref[depth : depth + 1] + s2_ref[depth : depth + 1]).astype(BF16)
    n_ref[0] = n
    lane = lax.broadcasted_iota(jnp.int32, (HW, LANES), 1)
    logits = jnp.where(lane < EXPERTS, mm(n, router_ref[0]), pad_fill)
    raised = jnp.exp(logits - jnp.max(logits, axis=-1, keepdims=True))
    router = raised / jnp.sum(raised, axis=-1, keepdims=True)
    probs_ref[0] = router
    chosen = lane == as_column(route_ref[0], HW)
    gate = jnp.sum(jnp.where(chosen, router, 0.0), axis=-1, keepdims=True)
    gate_ref[0] = jnp.broadcast_to(gate, (HW, LANES))
    rows_ref[pl.ds(step, 1), 0:HW, :] = n[None]
    if last:
        dy_rows_ref[pl.ds(step, 1), 0:HW, :] = (gate * cot_ref[0].astype(F32)).astype(BF16)[None]

    @pl.when(step == images - 1)
    def _():
        target_all = target_ref[...]
        send_rows(buf_ref, target_all, rows_ref[...].reshape(images * TPAD, D))
        if last:
            send_rows(dy_buf_ref, target_all, dy_rows_ref[...].reshape(images * TPAD, D))


def whole(shape):
    return pl.BlockSpec(shape, lambda i: (0,) * len(shape))


def by_image(shape):
    return pl.BlockSpec((1,) + shape[1:], lambda i: (i,) + (0,) * (len(shape) - 1))


def layer_of(shape, depth):
    return pl.BlockSpec((1,) + shape[1:], lambda i: (depth,) + (0,) * (len(shape) - 1))


def run_forward(depth, x, earlier, cotangent, route_rows, target_rows, target_all, shared):
    images = x.shape[0]
    last = depth == LAYERS - 1
    args, specs = [x], [by_image(x.shape)]
    if depth:
        back, gate_in, target_in, picked_type = earlier
        args += [back, gate_in, target_in]
        specs += [whole(back.shape), by_image(gate_in.shape), by_image(target_in.shape)]
    if last:
        args.append(cotangent)
        specs.append(by_image(cotangent.shape))
    args += [route_rows, target_all]
    specs += [by_image(route_rows.shape), whole(target_all.shape)]
    for name in ("first_gain", "first_shift", "second_gain", "second_shift"):
        args.append(shared[name])
        specs.append(whole(shared[name].shape))
    for name in ("attend_weight", "output_weight", "router"):
        args.append(shared[name])
        specs.append(layer_of(shared[name].shape, depth))
    for name in ("bias", "mask", "perm", "perm_back"):
        args.append(shared[name][depth])
        specs.append(whole(shared[name][depth].shape))
    outs = [
        ((images, WROWS, 3 * D), BF16),
        ((images, WROWS, D), BF16),
        ((images, WROWS, D), BF16),
        ((images, HW, D), F32),
        ((images, HW, D), BF16),
        ((images, HW, LANES), F32),
        ((images, HW, LANES), F32),
    ]
    out_specs = [by_image(s) for s, _ in outs]
    outs.append(((SLOTS, D), BF16))
    out_specs.append(whole((SLOTS, D)))
    if depth:
        outs += [((images, HW, D), F32), ((images, HW, D), picked_type)]
        out_specs += [by_image((images, HW, D))] * 2
    if last:
        outs.append(((SLOTS, D), BF16))
        out_specs.append(whole((SLOTS, D)))
    scratch = [pltpu.VMEM((images, TPAD, D), BF16)] * (2 if last else 1)
    return pl.pallas_call(
        partial(forward_kernel, depth, images),
        grid=(images,),
        in_specs=specs,
        out_specs=out_specs,
        out_shape=[jax.ShapeDtypeStruct(s, t) for s, t in outs],
        scratch_shapes=scratch,
        compiler_params=pltpu.CompilerParams(vmem_limit_bytes=VMEM_BYTES),
        name="forward_%d" % depth,
    )(*args)


def expert_forward_kernel(n_ref, up_ref, down_ref, y_ref, hidden_ref, slope_ref):
    u = mm(n_ref[...], up_ref[...])
    value, slope = gelu_parts(u)
    hidden = value.astype(BF16)
    hidden_ref[...] = hidden
    slope_ref[...] = slope.astype(BF16)
    y_ref[...] = mm(hidden, down_ref[...]).astype(BF16)


def run_expert_forward(arrived, up, down):
    rows, width = arrived.shape[0], up.shape[1]
    block = CAP * 2
    row_spec = pl.BlockSpec((block, D), lambda i: (i, 0))
    wide_spec = pl.BlockSpec((block, width), lambda i: (i, 0))
    return pl.pallas_call(
        expert_forward_kernel,
        grid=(rows // block,),
        in_specs=[row_spec, whole(up.shape), whole(down.shape)],
        out_specs=[row_spec, wide_spec, wide_spec],
        out_shape=[
            jax.ShapeDtypeStruct((rows, D), BF16),
            jax.ShapeDtypeStruct((rows, width), BF16),
            jax.ShapeDtypeStruct((rows, width), BF16),
        ],
        compiler_params=pltpu.CompilerParams(vmem_limit_bytes=VMEM_BYTES),
        name="expert_forward",
    )(arrived, up, down)


def expert_inner_kernel(dy_ref, slope_ref, up_ref, down_ref, dn_ref, du_ref):
    dh = mm(dy_ref[...], down_ref[...], NT)
    du = (dh * slope_ref[...].astype(F32)).astype(BF16)
    du_ref[...] = du
    dn_ref[...] = mm(du, up_ref[...], NT).astype(BF16)


def run_expert_inner(dy, slope, up, down):
    rows, width = dy.shape[0], up.shape[1]
    block = CAP * 2
    row_spec = pl.BlockSpec((block, D), lambda i: (i, 0))
    wide_spec = pl.BlockSpec((block, width), lambda i: (i, 0))
    return pl.pallas_call(
        expert_inner_kernel,
        grid=(rows // block,),
        in_specs=[row_spec, wide_spec, whole(up.shape), whole(down.shape)],
        out_specs=[row_spec, wide_spec],
        out_shape=[
            jax.ShapeDtypeStruct((rows, D), BF16),
            jax.ShapeDtypeStruct((rows, width), BF16),
        ],
        compiler_params=pltpu.CompilerParams(vmem_limit_bytes=VMEM_BYTES),
        name="expert_inner",
    )(dy, slope, up, down)


def expert_weights_kernel(n_ref, dy_ref, hidden_ref, du_ref, out_ref):
    out_ref[0:D] = mm(n_ref[...], du_ref[...], TN).astype(BF16)
    out_ref[D : 2 * D] = mm(hidden_ref[...], dy_ref[...], TN).astype(BF16)


def run_expert_weights(arrived, dy, hidden, du):
    rows, width = hidden.shape
    wide_spec = pl.BlockSpec((rows, FCHUNK), lambda i: (0, i))
    return pl.pallas_call(
        expert_weights_kernel,
        grid=(width // FCHUNK,),
        in_specs=[whole(arrived.shape), whole(dy.shape), wide_spec, wide_spec],
        out_specs=pl.BlockSpec((2 * D, FCHUNK), lambda i: (0, i)),
        out_shape=jax.ShapeDtypeStruct((2 * D, width), BF16),
        compiler_params=pltpu.CompilerParams(vmem_limit_bytes=VMEM_BYTES),
        name="expert_weights",
    )(arrived, dy, hidden, du)


def backward_kernel(depth, images, *refs):
    last = depth == LAYERS - 1
    refs = list(refs)
    take = lambda: refs.pop(0)
    g_ref, dn_ref = take(), take()
    if last:
        y_ref, before_gate_ref, before_target_ref = take(), take(), take()
    else:
        picked_ref = take()
    (x_ref, qkv_ref, a_ref, mixed_ref, mid_ref, n_ref, probs_ref, gate_ref) = refs[:8]
    (route_ref, target_ref, g1_ref, g2_ref, attend_ref, out_w_ref) = refs[8:14]
    (router_ref, bias_ref, mask_ref, perm_ref, perm_back_ref) = refs[14:19]
    refs = refs[19:]
    g_out_ref, mats_ref, vecs_ref, table_ref = take(), take(), take(), take()
    if last:
        result_ref, dy_buf_ref = take(), take()
    attend_acc, out_acc, dqkv_ref = take(), take(), take()
    if last:
        dy_rows_ref = take()

    step = pl.program_id(0)

    @pl.when(step == 0)
    def _():
        attend_acc[...] = jnp.zeros_like(attend_acc)
        out_acc[...] = jnp.zeros_like(out_acc)
        vecs_ref[...] = jnp.zeros_like(vecs_ref)
        table_ref[...] = jnp.zeros_like(table_ref)
        if last:
            dy_rows_ref[...] = jnp.zeros_like(dy_rows_ref)

    grad = g_ref[0].astype(F32)
    mid = mid_ref[0]
    gate = gate_ref[0][:, 0:1]
    if last:
        picked = pick_rows(target_ref[0], y_ref)
        result_ref[0] = (mid + gate * picked).astype(BF16)
    else:
        picked = picked_ref[0].astype(F32)
    gate_grad = jnp.sum(grad * picked, axis=-1, keepdims=True)
    lane = lax.broadcasted_iota(jnp.int32, (HW, LANES), 1)
    chosen = jnp.where(lane == as_column(route_ref[0], HW), 1.0, 0.0)
    logit_grad = ((gate * gate_grad) * (chosen - probs_ref[0])).astype(BF16)
    router_grad = mm(logit_grad, n_ref[0], TN)
    grad_n = pick_rows(target_ref[0], dn_ref) + mm(logit_grad, router_ref[0], NT)
    unit, inverse = norm_parts(mid)
    vecs_ref[2:3] += jnp.sum(grad_n * unit, axis=0, keepdims=True)
    vecs_ref[3:4] += jnp.sum(grad_n, axis=0, keepdims=True)
    vecs_ref[8:16] += router_grad[0:8]
    grad_mid = grad + norm_back(grad_n, unit, inverse, g2_ref[depth : depth + 1])
    dz = mm(perm_ref[...], grad_mid.astype(BF16)).astype(BF16)
    out_acc[...] += mm(mixed_ref[0], dz, TN)
    dmixed_all = mm(dz, out_w_ref[0], NT).astype(BF16)
    masks = head_masks()
    for w in range(WINDOWS):
        rows = slice(w * LPAD, (w + 1) * LPAD)
        for g in range(GROUPS):
            cols = slice(g * LANES, (g + 1) * LANES)
            q_wide, k, v, probs = transposed_scores(
                qkv_ref.at[0], w, g, bias_ref, mask_ref, masks
            )
            dm_wide = spread_heads(dmixed_all[rows, cols], masks)
            dprobs = mm(v, dm_wide, NT)
            dv = mm(probs.astype(BF16), dm_wide)
            row_dot = jnp.sum(probs * dprobs, axis=0, keepdims=True)
            dscores = (probs * (dprobs - row_dot)).astype(BF16)
            table_ref[:, g * GW : (g + 1) * GW] += dscores.astype(F32)
            dk = mm(dscores, q_wide) * score_scale
            dq = fold_heads(mm(dscores, k, TN), masks) * score_scale
            dqkv_ref[rows, cols] = dq.astype(BF16)
            dqkv_ref[rows, D + g * LANES : D + (g + 1) * LANES] = dk.astype(BF16)
            dqkv_ref[rows, 2 * D + g * LANES : 2 * D + (g + 1) * LANES] = dv.astype(BF16)
    dqkv = dqkv_ref[...]
    attend_acc[...] += mm(a_ref[0], dqkv, TN)
    dqkv_tokens = mm(perm_back_ref[...], dqkv).astype(BF16)
    grad_normed = mm(dqkv_tokens, attend_ref[0], NT)
    unit, inverse = norm_parts(x_ref[0].astype(F32))
    vecs_ref[0:1] += jnp.sum(grad_normed * unit, axis=0, keepdims=True)
    vecs_ref[1:2] += jnp.sum(grad_normed, axis=0, keepdims=True)
    grad_x = grad_mid + norm_back(grad_normed, unit, inverse, g1_ref[depth : depth + 1])
    g_out_ref[0] = grad_x.astype(g_out_ref.dtype)
    if last:
        dy = (before_gate_ref[0][:, 0:1] * grad_x).astype(BF16)
        dy_rows_ref[pl.ds(step, 1), 0:HW, :] = dy[None]

    @pl.when(step == images - 1)
    def _():
        mats_ref[:, 0 : 3 * D] = attend_acc[...].astype(BF16)
        mats_ref[:, 3 * D : 4 * D] = out_acc[...].astype(BF16)
        if last:
            send_rows(
                dy_buf_ref, before_target_ref[...], dy_rows_ref[...].reshape(images * TPAD, D)
            )


def run_backward(depth, grad, dn_back, extra, saved, route_rows, target_rows, shared):
    images = grad.shape[0]
    last = depth == LAYERS - 1
    args, specs = [grad, dn_back], [by_image(grad.shape), whole(dn_back.shape)]
    if last:
        y_back, before_gate, before_target = extra
        args += [y_back, before_gate, before_target]
        specs += [whole(y_back.shape), by_image(before_gate.shape), whole(before_target.shape)]
    else:
        args.append(extra)
        specs.append(by_image(extra.shape))
    for array in saved + [route_rows, target_rows]:
        args.append(array)
        specs.append(by_image(array.shape))
    for name in ("first_gain", "second_gain"):
        args.append(shared[name])
        specs.append(whole(shared[name].shape))
    for name in ("attend_weight", "output_weight", "router"):
        args.append(shared[name])
        specs.append(layer_of(shared[name].shape, depth))
    for name in ("bias", "mask", "perm", "perm_back"):
        args.append(shared[name][depth])
        specs.append(whole(shared[name][depth].shape))
    token_shape = (images, HW, D)
    outs = [
        (token_shape, F32 if last else BF16, by_image(token_shape)),
        ((D, 4 * D), BF16, whole((D, 4 * D))),
        ((16, D), F32, whole((16, D))),
        ((LPAD, GROUPS * GW), F32, whole((LPAD, GROUPS * GW))),
    ]
    if last:
        outs.append((token_shape, BF16, by_image(token_shape)))
        outs.append(((SLOTS, D), BF16, whole((SLOTS, D))))
    scratch = [
        pltpu.VMEM((D, 3 * D), F32),
        pltpu.VMEM((D, D), F32),
        pltpu.VMEM((WROWS, 3 * D), BF16),
    ]
    if last:
        scratch.append(pltpu.VMEM((images, TPAD, D), BF16))
    return pl.pallas_call(
        partial(backward_kernel, depth, images),
        grid=(images,),
        in_specs=specs,
        out_specs=[o[2] for o in outs],
        out_shape=[jax.ShapeDtypeStruct(o[0], o[1]) for o in outs],
        scratch_shapes=scratch,
        compiler_params=pltpu.CompilerParams(vmem_limit_bytes=VMEM_BYTES),
        name="backward_%d" % depth,
    )(*args)


def bits_of(axis, low, high):
    steps = []
    bit = low
    while bit < high:
        steps.append((axis, bit))
        bit *= 2
    return steps


def swap(x, step):
    axis, bit = step
    size = lax.axis_size(axis)
    return lax.ppermute(x, axis, [(i, i ^ bit) for i in range(size)])


def bit_at(step):
    axis, bit = step
    return (lax.axis_index(axis) // bit) % 2


def halved(rows, steps, least):
    count = 0
    while count < len(steps) and rows % 2 == 0 and rows // 2 >= least:
        rows //= 2
        count += 1
    return count


def sum_over(x, steps, least=24):
    count = halved(x.shape[0], steps, least)
    x = sum_all(scatter_sum(x, steps[:count]), steps[count:])
    return gather_all(x, steps[:count])


def scatter_sum(x, steps):
    for step in steps:
        half = x.shape[0] // 2
        mine = bit_at(step)
        keep = lax.dynamic_slice_in_dim(x, mine * half, half, 0)
        away = lax.dynamic_slice_in_dim(x, (1 - mine) * half, half, 0)
        x = (keep.astype(F32) + swap(away, step).astype(F32)).astype(x.dtype)
    return x


def gather_all(x, steps, dim=0):
    for step in reversed(steps):
        other = swap(x, step)
        mine = bit_at(step)
        first = jnp.where(mine == 0, x, other)
        second = jnp.where(mine == 0, other, x)
        x = jnp.concatenate([first, second], axis=dim)
    return x


def sum_all(x, steps):
    for step in steps:
        x = (x.astype(F32) + swap(x, step).astype(F32)).astype(x.dtype)
    return x


def exchange(buffers, slices):
    groups = lax.axis_size("expert")
    out = lax.all_to_all(
        buffers.reshape(groups, CAP, D), "expert", split_axis=0, concat_axis=0, tiled=True
    )
    return out.reshape(groups * CAP, D)


def to_experts(buffers, slices):
    if slices > 1:
        buffers = jnp.repeat(buffers.reshape(EXPERTS, CAP, D), slices, axis=0)
    return exchange(buffers, slices)


def from_experts(rows, slices):
    back = exchange(rows, slices)
    return back.reshape(EXPERTS, slices, CAP, D).transpose(1, 0, 2, 3).reshape(slices, SLOTS, D)


def unpack_down(packed):
    width = packed.shape[1]
    return jnp.concatenate(
        [packed[:, j * D : (j + 1) * D] for j in range(width // D)], axis=0
    )


def body(
    block_input,
    routes,
    first_gain,
    first_shift,
    attend_weight,
    bias_table,
    output_weight,
    second_gain,
    second_shift,
    router_weight,
    core_up,
    core_down,
    residual_up,
    residual_down,
    cotangent,
):
    groups = lax.axis_size("expert")
    slices = groups // EXPERTS
    group_part = lax.axis_index("expert") % slices
    images = block_input.shape[0]
    width = residual_up.shape[2]

    routes_rows = jnp.pad(
        routes.reshape(LAYERS, images, HW), ((0, 0), (0, 0), (0, TPAD - HW)), constant_values=-1
    )
    targets = run_routing(routes_rows)

    table_index = jnp.asarray(offset_table(), jnp.int32)
    picker = (jnp.arange(OFFSETS, dtype=jnp.int32)[:, None] == table_index[None, :]).astype(F32)
    flat_table = bias_table.transpose(0, 2, 1).reshape(LAYERS * HEADS, OFFSETS)
    bias = jnp.dot(flat_table, picker, precision=lax.Precision.HIGHEST)
    bias = (
        bias.reshape(LAYERS, HEADS, LPAD, LPAD)
        .transpose(0, 2, 1, 3)
        .reshape(LAYERS, LPAD, HEADS * LPAD)
    )
    offsets = [SHIFT * (depth % 2) for depth in range(LAYERS)]
    shared = {
        "first_gain": first_gain,
        "first_shift": first_shift,
        "second_gain": second_gain,
        "second_shift": second_shift,
        "attend_weight": attend_weight,
        "output_weight": output_weight,
        "router": jnp.pad(router_weight, ((0, 0), (0, 0), (0, LANES - EXPERTS))),
        "bias": [bias[depth] for depth in range(LAYERS)],
        "mask": [jnp.asarray(score_mask(o)) for o in offsets],
        "perm": [jnp.asarray(permutation(o), BF16) for o in offsets],
        "perm_back": [jnp.asarray(permutation(o).T, BF16) for o in offsets],
    }
    route_rows = [routes_rows[d].reshape(images, 1, TPAD) for d in range(LAYERS)]
    target_rows = [targets[d].reshape(images, 1, TPAD) for d in range(LAYERS)]
    target_all = [targets[d].reshape(1, images * TPAD) for d in range(LAYERS)]
    ups, downs = [], []
    for d in range(LAYERS):
        up_core = lax.dynamic_slice_in_dim(core_up[d], group_part * width, width, 1)
        down_core = lax.dynamic_slice_in_dim(core_down[d], group_part * width, width, 0)
        ups.append((up_core.astype(F32) + residual_up[d].astype(F32)).astype(BF16))
        downs.append((down_core.astype(F32) + residual_down[d].astype(F32)).astype(BF16))

    picked_type = BF16 if slices == 1 else F32
    saved, inner, gates, xs, picks = [], [], [], [block_input], []
    x, earlier = block_input, None
    dy_arrived = None
    for d in range(LAYERS):
        outs = run_forward(
            d, x, earlier, cotangent, route_rows[d], target_rows[d], target_all[d], shared
        )
        qkv, a, mixed, mid, n, probs, gate, buffers = outs[:8]
        if d:
            xs.append(outs[8])
            picks.append(outs[9])
        arrived = to_experts(buffers, slices)
        if d == LAYERS - 1:
            dy_arrived = to_experts(outs[10], slices)
        y, hidden, slope = run_expert_forward(arrived, ups[d], downs[d])
        back = from_experts(y, slices)
        earlier = (back, gate, target_rows[d], picked_type)
        x = mid
        gates.append(gate)
        saved.append([xs[d], qkv, a, mixed, mid, n, probs, gate])
        inner.append((arrived, hidden, slope))

    grad = cotangent
    mats, vecs, tables, experts = [None] * 2, [None] * 2, [None] * 2, [None] * 2
    block_output = None
    for d in reversed(range(LAYERS)):
        arrived, hidden, slope = inner[d]
        dn, du = run_expert_inner(dy_arrived, slope, ups[d], downs[d])
        dn_back = from_experts(dn, slices)
        experts[d] = run_expert_weights(arrived, dy_arrived, hidden, du)
        if d == LAYERS - 1:
            extra = (earlier[0], gates[d - 1], target_all[d - 1])
        else:
            extra = picks[d]
        outs = run_backward(
            d, grad, dn_back, extra, saved[d], route_rows[d], target_rows[d], shared
        )
        grad, mats[d], vecs[d], tables[d] = outs[:4]
        if d == LAYERS - 1:
            block_output = outs[4]
            dy_arrived = to_experts(outs[5], slices)
    input_grad = grad

    dp_steps = bits_of("dp", 1, lax.axis_size("dp"))
    slice_steps = bits_of("expert", 1, slices)
    sum_steps = bits_of("expert", slices, groups)
    all_steps = dp_steps + slice_steps + sum_steps
    residual, core, full = [], [], []
    for d in reversed(range(LAYERS)):
        part = scatter_sum(experts[d], dp_steps)
        residual.insert(0, gather_all(part, dp_steps))
        total = sum_over(part, sum_steps)
        total = gather_all(total, dp_steps)
        core.insert(0, gather_all(total, slice_steps, dim=1))
        full.insert(0, sum_over(mats[d], all_steps))
    table_grad = jnp.stack(tables).reshape(LAYERS, LPAD, HEADS, LPAD).transpose(0, 2, 1, 3)
    table_grad = jnp.dot(
        table_grad.reshape(LAYERS * HEADS, LPAD * LPAD), picker.T, precision=lax.Precision.HIGHEST
    )
    small = jnp.concatenate(
        [
            jnp.stack(vecs).reshape(LAYERS * 16, D),
            jnp.pad(table_grad, ((0, 0), (0, D - OFFSETS))),
        ],
        axis=0,
    )
    small = sum_all(small, all_steps)
    vec = small[: LAYERS * 16].reshape(LAYERS, 16, D)
    table = small[LAYERS * 16 :, :OFFSETS].reshape(LAYERS, HEADS, OFFSETS).transpose(0, 2, 1)
    full = jnp.stack(full).astype(F32)
    residual_up_grad = jnp.stack([r[:D] for r in residual]).astype(F32)
    residual_down_grad = jnp.stack([unpack_down(r[D:]) for r in residual]).astype(F32)
    core_up_grad = jnp.stack([c[:D] for c in core]).astype(F32)
    core_down_grad = jnp.stack([unpack_down(c[D:]) for c in core]).astype(F32)
    return (
        block_output,
        input_grad,
        vec[:, 0],
        vec[:, 1],
        full[:, :, : 3 * D],
        table,
        full[:, :, 3 * D :],
        vec[:, 2],
        vec[:, 3],
        vec[:, 8:16].transpose(0, 2, 1),
        core_up_grad,
        core_down_grad,
        residual_up_grad,
        residual_down_grad,
    )


def solution(mesh):
    placed = (
        P(("dp", "expert"), None, None),
        P(None, ("dp", "expert"), None, None),
        P(),
        P(),
        P(),
        P(),
        P(),
        P(),
        P(),
        P(),
        P(),
        P(),
        P(None, None, "expert"),
        P(None, "expert", None),
        P(("dp", "expert"), None, None),
    )
    return jax.shard_map(
        body,
        mesh=mesh,
        in_specs=placed,
        out_specs=(
            P(("dp", "expert"), None, None),
            P(("dp", "expert"), None, None),
            P(),
            P(),
            P(),
            P(),
            P(),
            P(),
            P(),
            P(),
            P(),
            P(),
            P(None, None, "expert"),
            P(None, "expert", None),
        ),
        check_vma=False,
    )
```

```python
from functools import partial

import jax
import jax.numpy as jnp
import numpy as np
from jax import lax
from jax.experimental import pallas as pl
from jax.experimental.pallas import tpu as pltpu
from jax.sharding import PartitionSpec as P

D = 384
HEADS = 12
HD = 32
FF = 1536
EXPERTS = 8
WIN = 7
SIDE = 14
SHIFT = 3
LAYERS = 2
HW = 196
CAP = 184
OFFSETS = 169
ROWS = 192
SLOTS = EXPERTS * ROWS

WINDOWS = (SIDE // WIN) * (SIDE // WIN)
LENGTH = WIN * WIN
LPAD = 64
WROWS = WINDOWS * LPAD
TPAD = 256
LANES = 128
GROUP = LANES // HD
GROUPS = HEADS // GROUP
GW = GROUP * LPAD
FCHUNK = 384
JOIN = 2
FTILE = 512
EXPERT_VMEM = 32 * 1024 * 1024
BLOCK = 48
PAIRS_AT_ONCE = 2
SEND_ORDER = (4, 5, 6, 7, 2, 3, 1)
PART = 4
STEP_IMAGES = 3

F32 = jnp.float32
BF16 = jnp.bfloat16
eps_norm = 1e-05
mask_fill = -100.0
pad_fill = -1e30
score_scale = HD ** (-0.5)
VMEM_BYTES = 56 * 1024 * 1024

NN = (((1,), (0,)), ((), ()))
NT = (((1,), (1,)), ((), ()))
TN = (((0,), (0,)), ((), ()))


def mm(a, b, dims=NN):
    return lax.dot_general(a, b, dims, preferred_element_type=F32)


def window_tokens(offset):
    rows = np.full((WINDOWS, LPAD), -1, np.int64)
    per_side = SIDE // WIN
    for w in range(WINDOWS):
        for i in range(LENGTH):
            r = (w // per_side) * WIN + i // WIN
            c = (w % per_side) * WIN + i % WIN
            rows[w, i] = ((r + offset) % SIDE) * SIDE + (c + offset) % SIDE
    return rows.reshape(-1)


def permutation(offset):
    rows = window_tokens(offset)
    return (rows[:, None] == np.arange(HW)[None, :]).astype(np.float32)


def score_mask(offset):
    coords = np.arange(SIDE)
    bands = (coords >= SIDE - WIN).astype(int) + (coords >= SIDE - offset).astype(int)
    labels = bands[:, None] * 3 + bands[None, :]
    per_side = SIDE // WIN
    out = np.zeros((WINDOWS, LPAD, LPAD), np.float32)
    for w in range(WINDOWS):
        r0, c0 = (w // per_side) * WIN, (w % per_side) * WIN
        flat = labels[r0 : r0 + WIN, c0 : c0 + WIN].reshape(-1)
        out[w, :LENGTH, :LENGTH] = np.where(flat[:, None] == flat[None, :], 0.0, mask_fill)
        out[w, LENGTH:, :] = pad_fill
    return np.tile(out, (1, 1, GROUP))


def offset_table():
    i = np.arange(LENGTH)
    r, c = i // WIN, i % WIN
    index = np.full((LPAD, LPAD), -1, np.int64)
    index[:LENGTH, :LENGTH] = (
        (r[None, :] - r[:, None] + WIN - 1) * (2 * WIN - 1) + c[None, :] - c[:, None] + WIN - 1
    )
    return index.reshape(-1)


def norm_parts(x):
    centred = x - jnp.mean(x, axis=-1, keepdims=True)
    inverse = lax.rsqrt(jnp.mean(centred * centred, axis=-1, keepdims=True) + eps_norm)
    return centred * inverse, inverse


def norm_back(grad, unit, inverse, gain):
    scaled = grad * gain
    return inverse * (
        scaled
        - jnp.mean(scaled, axis=-1, keepdims=True)
        - unit * jnp.mean(scaled * unit, axis=-1, keepdims=True)
    )


def one_hot(cond):
    return jnp.where(cond, 1.0, 0.0).astype(BF16)


def head_masks():
    lane = lax.broadcasted_iota(jnp.int32, (1, LANES), 1) // HD
    return [jnp.where(lane == h, 1.0, 0.0) for h in range(GROUP)]


def spread_heads(block, masks):
    return jnp.concatenate([block * m.astype(BF16) for m in masks], axis=0)


def fold_heads(tall, masks):
    total = tall[0:LPAD] * masks[0]
    for h in range(1, GROUP):
        total = total + tall[h * LPAD : (h + 1) * LPAD] * masks[h]
    return total


def as_column(row, count):
    wide = jnp.broadcast_to(row.astype(F32), (8, TPAD))
    return wide.T[:count, 0:1].astype(jnp.int32)


def pick_rows(target_row, rows_ref):
    column = as_column(target_row, HW)
    place = one_hot(lax.broadcasted_iota(jnp.int32, (HW, SLOTS), 1) == column)
    total = mm(place, rows_ref[0])
    for k in range(1, rows_ref.shape[0]):
        total = total + mm(place, rows_ref[k])
    return total


def join_chunks(rows_ref, chunks):
    parts = rows_ref.shape[0]
    for i, chunk in enumerate(chunks):
        rows_ref[i % parts, (i // parts) * ROWS : (i // parts + 1) * ROWS] = chunk[...]


def send_rows(out_refs, target_all, rows):
    step = SLOTS // 4
    for c in range(4):
        slot = lax.broadcasted_iota(jnp.int32, (step, rows.shape[0]), 0) + c * step
        block = mm(one_hot(slot == target_all), rows).astype(BF16)
        for group, refs in enumerate(out_refs):
            for k in range(step // ROWS):
                refs[c * (step // ROWS) + k][...] = block[
                    k * ROWS : (k + 1) * ROWS, group * D : (group + 1) * D
                ]


def gelu_parts(u):
    cdf = 0.5 + 0.5 * lax.erf(u * (0.5**0.5))
    bell = jnp.exp(-0.5 * u * u)
    return u * cdf, cdf + u * (bell * 0.3989422804014327)


def cost(microseconds):
    return pl.CostEstimate(
        flops=int(microseconds * 9e8), bytes_accessed=1000, transcendentals=0
    )


def routing_kernel(flip_ref, routes_ref, target_ref):
    before = one_hot(
        lax.broadcasted_iota(jnp.int32, (TPAD, TPAD), 0)
        <= lax.broadcasted_iota(jnp.int32, (TPAD, TPAD), 1)
    )
    expert = lax.broadcasted_iota(jnp.int32, (16, TPAD), 0)
    for depth in range(LAYERS):
        carry = jnp.zeros((16, 1), F32)
        for i in range(routes_ref.shape[1]):
            row = routes_ref[depth, i : i + 1, :]
            chosen = jnp.where(expert == row, 1.0, 0.0)
            counts = mm(chosen.astype(BF16), before) + carry
            carry = counts[:, TPAD - 1 : TPAD]
            slot = jnp.sum(chosen * counts, axis=0, keepdims=True).astype(jnp.int32) - 1
            kept = (slot >= 0) & (slot < CAP)
            target_ref[depth, i : i + 1, :] = jnp.where(
                kept, jnp.bitwise_xor(row, flip_ref[0]) * ROWS + slot, -1
            )


def run_routing(routes, flip):
    return pl.pallas_call(
        routing_kernel,
        in_specs=[
            pl.BlockSpec(memory_space=pltpu.SMEM),
            pl.BlockSpec(memory_space=pltpu.VMEM),
        ],
        out_shape=jax.ShapeDtypeStruct(routes.shape, jnp.int32),
        name="routing",
    )(flip, routes)


def group_cols(part, g):
    return slice(part * D + g * LANES, part * D + (g + 1) * LANES)


def softmax_down(scores):
    raised = jnp.exp(scores - jnp.max(scores, axis=0, keepdims=True))
    return raised * (1.0 / jnp.sum(raised, axis=0, keepdims=True))


def window_items(some):
    pairs = [(w, g) for w in range(WINDOWS) for g in range(GROUPS)]
    runs = []
    for first in range(0, len(pairs), PAIRS_AT_ONCE):
        runs.append([(w, g, b) for w, g in pairs[first : first + PAIRS_AT_ONCE] for b in some])
    return runs


def raw_scores(qkv_ref, items, masks):
    wide, scores = [], []
    for w, g, b in items:
        rows = slice(w * LPAD, (w + 1) * LPAD)
        wide.append(spread_heads(qkv_ref[b, rows, group_cols(0, g)], masks))
    for (w, g, b), q_wide in zip(items, wide):
        rows = slice(w * LPAD, (w + 1) * LPAD)
        scores.append(mm(qkv_ref[b, rows, group_cols(1, g)], q_wide, NT))
    return wide, scores


def to_probs(items, scores, bias_ref, mask_ref):
    probs = []
    for (w, g, b), score in zip(items, scores):
        probs.append(
            softmax_down(
                score * score_scale + bias_ref[:, g * GW : (g + 1) * GW] + mask_ref[w]
            )
        )
    return probs


def forward_kernel(depth, images, chunks, *refs):
    last = depth == LAYERS - 1
    refs = list(refs)
    take = lambda: refs.pop(0)
    x_ref = take()
    if depth:
        back = [take() for _ in range(chunks)]
        gate_in_ref, target_in_ref = take(), take()
    if last:
        cot_ref = take()
    (route_ref, target_ref, g1_ref, s1_ref, g2_ref, s2_ref, attend_ref, out_w_ref) = refs[:8]
    (router_ref, bias_ref, mask_ref, perm_ref, perm_back_ref) = refs[8:13]
    refs = refs[13:]
    (qkv_ref, a_ref, mixed_ref, mid_ref, n_ref, probs_ref, gate_ref) = refs[:7]
    refs = refs[7:]
    if depth:
        x_out_ref, picked_ref = take(), take()
    outgoing = [[take() for _ in range(EXPERTS)] for _ in range(2 if last else 1)]
    rows_ref = take()
    if depth:
        back_ref = take()

    step = pl.program_id(0)

    @pl.when(step == 0)
    def _():
        rows_ref[...] = jnp.zeros_like(rows_ref)
        if depth:
            join_chunks(back_ref, back)

    some = range(x_ref.shape[0])
    xs = []
    for b in some:
        x = x_ref[b].astype(F32)
        if depth:
            picked = pick_rows(target_in_ref[b], back_ref)
            picked_ref[b] = picked.astype(picked_ref.dtype)
            x = x + gate_in_ref[b][:, 0:1] * picked
            x_out_ref[b] = x
        xs.append(x)
    for b in some:
        unit, _ = norm_parts(xs[b])
        normed = (unit * g1_ref[depth : depth + 1] + s1_ref[depth : depth + 1]).astype(BF16)
        a_ref[b] = mm(perm_ref[...], normed).astype(BF16)
    qkv = mm(a_ref[...].reshape(len(some) * WROWS, D), attend_ref[0]).astype(BF16)
    qkv_ref[...] = qkv.reshape(len(some), WROWS, 3 * D)
    masks = head_masks()
    runs = window_items(some)
    ready = raw_scores(qkv_ref, runs[0], masks)
    for at, items in enumerate(runs):
        _, scores = ready
        if at + 1 < len(runs):
            ready = raw_scores(qkv_ref, runs[at + 1], masks)
        probs = to_probs(items, scores, bias_ref, mask_ref)
        tall = []
        for (w, g, b), p in zip(items, probs):
            rows = slice(w * LPAD, (w + 1) * LPAD)
            tall.append(mm(p.astype(BF16), qkv_ref[b, rows, group_cols(2, g)], TN))
        for (w, g, b), t in zip(items, tall):
            rows = slice(w * LPAD, (w + 1) * LPAD)
            mixed_ref[b, rows, group_cols(0, g)] = fold_heads(t, masks).astype(BF16)
    lane = lax.broadcasted_iota(jnp.int32, (HW, LANES), 1)
    for b in some:
        mixed = mm(perm_back_ref[...], mixed_ref[b]).astype(BF16)
        mid = xs[b] + mm(mixed, out_w_ref[0])
        mid_ref[b] = mid
        unit, _ = norm_parts(mid)
        n = (unit * g2_ref[depth : depth + 1] + s2_ref[depth : depth + 1]).astype(BF16)
        n_ref[b] = n
        logits = jnp.where(lane < EXPERTS, mm(n, router_ref[0]), pad_fill)
        raised = jnp.exp(logits - jnp.max(logits, axis=-1, keepdims=True))
        router = raised / jnp.sum(raised, axis=-1, keepdims=True)
        probs_ref[b] = router
        chosen = lane == as_column(route_ref[b], HW)
        gate = jnp.sum(jnp.where(chosen, router, 0.0), axis=-1, keepdims=True)
        gate_ref[b] = jnp.broadcast_to(gate, (HW, LANES))
        at = step * len(some) + b
        rows_ref[pl.ds(at, 1), 0:HW, 0:D] = n[None]
        if last:
            dy = (gate * cot_ref[b].astype(F32)).astype(BF16)
            rows_ref[pl.ds(at, 1), 0:HW, D : 2 * D] = dy[None]

    @pl.when(step == pl.num_programs(0) - 1)
    def _():
        rows = rows_ref[...].reshape(images * TPAD, rows_ref.shape[2])
        send_rows(outgoing, target_ref[...], rows)


def whole(shape):
    return pl.BlockSpec(shape, lambda i: (0,) * len(shape))


def images_of(images):
    return STEP_IMAGES if images % STEP_IMAGES == 0 else 1


def by_image(shape):
    return pl.BlockSpec(
        (images_of(shape[0]),) + shape[1:], lambda i: (i,) + (0,) * (len(shape) - 1)
    )


def layer_of(shape, depth):
    return pl.BlockSpec((1,) + shape[1:], lambda i: (depth,) + (0,) * (len(shape) - 1))


def run_forward(depth, x, earlier, cotangent, route_rows, target_rows, target_all, shared):
    images = x.shape[0]
    last = depth == LAYERS - 1
    args, specs = [x], [by_image(x.shape)]
    if depth:
        back, gate_in, target_in, picked_type = earlier
        args += list(back) + [gate_in, target_in]
        specs += [whole(chunk.shape) for chunk in back]
        specs += [by_image(gate_in.shape), by_image(target_in.shape)]
    if last:
        args.append(cotangent)
        specs.append(by_image(cotangent.shape))
    args += [route_rows, target_all]
    specs += [by_image(route_rows.shape), whole(target_all.shape)]
    for name in ("first_gain", "first_shift", "second_gain", "second_shift"):
        args.append(shared[name])
        specs.append(whole(shared[name].shape))
    for name in ("attend_weight", "output_weight", "router"):
        args.append(shared[name])
        specs.append(layer_of(shared[name].shape, depth))
    for name in ("bias", "mask", "perm", "perm_back"):
        args.append(shared[name][depth])
        specs.append(whole(shared[name][depth].shape))
    outs = [
        ((images, WROWS, 3 * D), BF16),
        ((images, WROWS, D), BF16),
        ((images, WROWS, D), BF16),
        ((images, HW, D), F32),
        ((images, HW, D), BF16),
        ((images, HW, LANES), F32),
        ((images, HW, LANES), F32),
    ]
    out_specs = [by_image(s) for s, _ in outs]
    if depth:
        outs += [((images, HW, D), F32), ((images, HW, D), picked_type)]
        out_specs += [by_image((images, HW, D))] * 2
    count = EXPERTS * (2 if last else 1)
    outs += [((ROWS, D), BF16)] * count
    out_specs += [whole((ROWS, D))] * count
    scratch = [pltpu.VMEM((images, TPAD, 2 * D if last else D), BF16)]
    if depth:
        scratch.append(pltpu.VMEM((len(back) // EXPERTS, SLOTS, D), BF16))
    results = pl.pallas_call(
        partial(forward_kernel, depth, images, len(back) if depth else 0),
        grid=(images // images_of(images),),
        in_specs=specs,
        out_specs=out_specs,
        out_shape=[jax.ShapeDtypeStruct(s, t) for s, t in outs],
        scratch_shapes=scratch,
        compiler_params=pltpu.CompilerParams(vmem_limit_bytes=VMEM_BYTES),
        cost_estimate=cost(24 if last else 18),
        name="forward_%d" % depth,
    )(*args)
    return results[:-count], [results[-count:][i : i + EXPERTS] for i in range(0, count, EXPERTS)]


def expert_forward_kernel(chunks, *refs):
    sources, refs = refs[:chunks], refs[chunks:]
    up_ref, down_ref, refs = refs[0], refs[1], refs[2:]
    returns, refs = refs[:chunks], refs[chunks:]
    hidden_ref, slope_ref = refs
    width = up_ref.shape[1]
    tile = FTILE if width % FTILE == 0 else FCHUNK
    tiles = [(k, f) for k in range(0, chunks, JOIN) for f in range(0, width, tile)]
    joined = [
        jnp.concatenate([r[...] for r in sources[k : k + JOIN]], axis=0)
        for k in range(0, chunks, JOIN)
    ]
    first = lambda k, f: mm(joined[k // JOIN], up_ref[:, f : f + tile])
    ready = first(*tiles[0])
    for at, (k, f) in enumerate(tiles):
        u = ready
        if at + 1 < len(tiles):
            ready = first(*tiles[at + 1])
        rows = slice(k * ROWS, (k + JOIN) * ROWS)
        value, slope = gelu_parts(u)
        hidden_ref[rows, f : f + tile] = value.astype(BF16)
        slope_ref[rows, f : f + tile] = slope.astype(BF16)
        if f + tile >= width:
            y = mm(hidden_ref[rows], down_ref[...]).astype(BF16)
            for j in range(JOIN):
                returns[k + j][...] = y[j * ROWS : (j + 1) * ROWS]


def expert_inner_kernel(chunks, *refs):
    sources, refs = refs[:chunks], refs[chunks:]
    slope_ref, up_ref, down_ref, refs = refs[0], refs[1], refs[2], refs[3:]
    returns, refs = refs[:chunks], refs[chunks:]
    (du_ref,) = refs
    width = up_ref.shape[1]
    tile = FTILE if width % FTILE == 0 else FCHUNK
    tiles = [(k, f) for k in range(chunks) for f in range(0, width, tile)]
    first = lambda k, f: mm(sources[k][...], down_ref[f : f + tile], NT)
    ready = first(*tiles[0])
    for at, (k, f) in enumerate(tiles):
        dh = ready
        if at + 1 < len(tiles):
            ready = first(*tiles[at + 1])
        rows = slice(k * ROWS, (k + 1) * ROWS)
        du_ref[rows, f : f + tile] = (dh * slope_ref[rows, f : f + tile].astype(F32)).astype(
            BF16
        )
        if f + tile >= width:
            returns[k][...] = mm(du_ref[rows], up_ref[...], NT).astype(BF16)


def run_expert(kernel, name, sources, slopes, up, down, wides, time):
    rows, width = ROWS * len(sources), up.shape[1]
    results = pl.pallas_call(
        partial(kernel, len(sources)),
        out_shape=[jax.ShapeDtypeStruct((ROWS, D), BF16)] * len(sources)
        + [jax.ShapeDtypeStruct((rows, width), BF16)] * wides,
        compiler_params=pltpu.CompilerParams(vmem_limit_bytes=EXPERT_VMEM),
        cost_estimate=cost(time),
        name=name,
    )(*sources, *slopes, up, down)
    return results[: len(sources)], results[len(sources) :]


def run_expert_forward(sources, up, down):
    return run_expert(expert_forward_kernel, "expert_forward", sources, [], up, down, 2, 5.5)


def run_expert_inner(sources, slope, up, down):
    return run_expert(expert_inner_kernel, "expert_inner", sources, [slope], up, down, 1, 4)


def expert_weights_kernel(chunks, parts, order, *refs):
    if order:
        order_ref, refs = refs[0], refs[1:]
    ns, refs = refs[:chunks], refs[chunks:]
    dys, refs = refs[:chunks], refs[chunks:]
    hiddens, refs = refs[:parts], refs[parts:]
    dus, refs = refs[:parts], refs[parts:]
    if order:
        keep_ref, send_ref, n_rows, dy_rows, sum_ref = refs
    else:
        out_ref, n_rows, dy_rows = refs
    for k in range(chunks):
        n_rows[k * ROWS : (k + 1) * ROWS] = ns[k][...]
        dy_rows[k * ROWS : (k + 1) * ROWS] = dys[k][...]
    for f in range(0, hiddens[0].shape[1], FCHUNK):
        columns = slice(f, f + FCHUNK)
        up, down, at = 0.0, 0.0, 0
        for hidden, du in zip(hiddens, dus):
            rows = slice(at, at + du.shape[0])
            at += du.shape[0]
            up = up + mm(n_rows[rows], du[:, columns], TN)
            down = down + mm(hidden[:, columns], dy_rows[rows], TN)
        if order:
            sum_ref[0:D] = up
            sum_ref[D : 2 * D] = down
            spread_blocks(order_ref, sum_ref, keep_ref, send_ref, columns)
        else:
            out_ref[0:D, columns] = up.astype(BF16)
            out_ref[D : 2 * D, columns] = down.astype(BF16)


def spread_blocks(order_ref, sum_ref, keep_ref, send_ref, columns):
    count = sum_ref.shape[0] // BLOCK
    for j in range(count):
        start = pl.multiple_of(jnp.bitwise_xor(order_ref[0], j) * BLOCK, BLOCK)
        block = sum_ref[pl.ds(start, BLOCK)].astype(BF16)
        ref = keep_ref if j < count // 2 else send_ref
        at = (j % (count // 2)) * BLOCK
        ref[at : at + BLOCK, columns] = block


def run_expert_weights(ns, dys, hiddens, dus, order=None):
    width = hiddens[0].shape[1]
    rows = ROWS * len(ns)
    scratch = [pltpu.VMEM((rows, D), BF16)] * 2
    shape, leading, specs = jax.ShapeDtypeStruct((2 * D, width), BF16), [], None
    if order is not None:
        shape = [jax.ShapeDtypeStruct((D, width), BF16)] * 2
        leading = [order]
        scratch.append(pltpu.VMEM((2 * D, FCHUNK), F32))
    vmem = pl.BlockSpec(memory_space=pltpu.VMEM)
    return pl.pallas_call(
        partial(expert_weights_kernel, len(ns), len(hiddens), order is not None),
        in_specs=[pl.BlockSpec(memory_space=pltpu.SMEM)] * len(leading)
        + [vmem] * (2 * len(ns) + 2 * len(hiddens)),
        out_shape=shape,
        scratch_shapes=scratch,
        compiler_params=pltpu.CompilerParams(vmem_limit_bytes=EXPERT_VMEM),
        cost_estimate=cost(6.5),
        name="expert_weights",
    )(*leading, *ns, *dys, *hiddens, *dus)


def backward_kernel(depth, images, chunks, order, *refs):
    last = depth == LAYERS - 1
    refs = list(refs)
    take = lambda: refs.pop(0)
    if order:
        order_ref = take()
    g_ref = take()
    dn_back = [take() for _ in range(chunks)]
    if last:
        y_back = [take() for _ in range(chunks)]
        before_gate_ref, before_target_ref = take(), take()
    else:
        picked_ref = take()
    (x_ref, qkv_ref, a_ref, mixed_ref, mid_ref, n_ref, probs_ref, gate_ref) = refs[:8]
    (route_ref, target_ref, g1_ref, g2_ref, attend_ref, out_w_ref) = refs[8:14]
    (router_ref, bias_ref, mask_ref, perm_ref, perm_back_ref) = refs[14:19]
    refs = refs[19:]
    g_out_ref = take()
    mats_refs = [take() for _ in range(2 if order else 1)]
    vecs_ref, table_ref = take(), take()
    if last:
        result_ref = take()
        outgoing = [take() for _ in range(EXPERTS)]
    attend_acc, out_acc, dqkv_ref, dz_ref, dn_ref = (take() for _ in range(5))
    if last:
        y_ref, dy_rows_ref = take(), take()

    step = pl.program_id(0)

    @pl.when(step == 0)
    def _():
        attend_acc[...] = jnp.zeros_like(attend_acc)
        out_acc[...] = jnp.zeros_like(out_acc)
        vecs_ref[...] = jnp.zeros_like(vecs_ref)
        table_ref[...] = jnp.zeros_like(table_ref)
        join_chunks(dn_ref, dn_back)
        if last:
            join_chunks(y_ref, y_back)
            dy_rows_ref[...] = jnp.zeros_like(dy_rows_ref)

    some = range(g_ref.shape[0])
    lane = lax.broadcasted_iota(jnp.int32, (HW, LANES), 1)
    grad_mids, dmixed_all = [], []
    for b in some:
        grad = g_ref[b].astype(F32)
        mid = mid_ref[b]
        gate = gate_ref[b][:, 0:1]
        if last:
            picked = pick_rows(target_ref[b], y_ref)
            result_ref[b] = (mid + gate * picked).astype(BF16)
        else:
            picked = picked_ref[b].astype(F32)
        gate_grad = jnp.sum(grad * picked, axis=-1, keepdims=True)
        chosen = jnp.where(lane == as_column(route_ref[b], HW), 1.0, 0.0)
        logit_grad = ((gate * gate_grad) * (chosen - probs_ref[b])).astype(BF16)
        router_grad = mm(logit_grad, n_ref[b], TN)
        grad_n = pick_rows(target_ref[b], dn_ref) + mm(logit_grad, router_ref[0], NT)
        unit, inverse = norm_parts(mid)
        vecs_ref[2:3] += jnp.sum(grad_n * unit, axis=0, keepdims=True)
        vecs_ref[3:4] += jnp.sum(grad_n, axis=0, keepdims=True)
        vecs_ref[8:16] += router_grad[0:8]
        grad_mid = grad + norm_back(grad_n, unit, inverse, g2_ref[depth : depth + 1])
        grad_mids.append(grad_mid)
        dz = mm(perm_ref[...], grad_mid.astype(BF16)).astype(BF16)
        dz_ref[b] = dz
    dz = dz_ref[...].reshape(len(some) * WROWS, D)
    out_acc[...] += mm(mixed_ref[...].reshape(len(some) * WROWS, D), dz, TN)
    dmixed_all = mm(dz, out_w_ref[0], NT).astype(BF16)
    masks = head_masks()
    def first_part(items):
        dm_wide, dprobs = [], []
        for w, g, b in items:
            start = b * WROWS + w * LPAD
            dm_wide.append(
                spread_heads(dmixed_all[start : start + LPAD, group_cols(0, g)], masks)
            )
        for (w, g, b), dm in zip(items, dm_wide):
            rows = slice(w * LPAD, (w + 1) * LPAD)
            dprobs.append(mm(qkv_ref[b, rows, group_cols(2, g)], dm, NT))
        return raw_scores(qkv_ref, items, masks) + (dm_wide, dprobs)

    runs = window_items(some)
    ready = first_part(runs[0])
    for at, items in enumerate(runs):
        places = [(b, slice(w * LPAD, (w + 1) * LPAD), g) for w, g, b in items]
        q_wide, scores, dm_wide, dprobs = ready
        if at + 1 < len(runs):
            ready = first_part(runs[at + 1])
        probs = to_probs(items, scores, bias_ref, mask_ref)
        dscores, tables = [], {}
        for (b, rows, g), p, dp in zip(places, probs, dprobs):
            row_dot = jnp.sum(p * dp, axis=0, keepdims=True)
            dscores.append((p * (dp - row_dot)).astype(BF16))
            wide = dscores[-1].astype(F32)
            tables[g] = tables[g] + wide if g in tables else wide
        for g, total in tables.items():
            table_ref[:, g * GW : (g + 1) * GW] += total
        dv, dk, tall = [], [], []
        for p, dm in zip(probs, dm_wide):
            dv.append(mm(p.astype(BF16), dm))
        for ds, q in zip(dscores, q_wide):
            dk.append(mm(ds, q))
        for (b, rows, g), ds in zip(places, dscores):
            tall.append(mm(ds, qkv_ref[b, rows, group_cols(1, g)], TN))
        for i, (b, rows, g) in enumerate(places):
            dq = fold_heads(tall[i], masks) * score_scale
            dqkv_ref[b, rows, group_cols(0, g)] = dq.astype(BF16)
            dqkv_ref[b, rows, group_cols(1, g)] = (dk[i] * score_scale).astype(BF16)
            dqkv_ref[b, rows, group_cols(2, g)] = dv[i].astype(BF16)
    dqkv = dqkv_ref[...].reshape(len(some) * WROWS, 3 * D)
    attend_acc[...] += mm(a_ref[...].reshape(len(some) * WROWS, D), dqkv, TN)
    for b in some:
        dqkv_tokens = mm(perm_back_ref[...], dqkv_ref[b]).astype(BF16)
        grad_normed = mm(dqkv_tokens, attend_ref[0], NT)
        unit, inverse = norm_parts(x_ref[b].astype(F32))
        vecs_ref[0:1] += jnp.sum(grad_normed * unit, axis=0, keepdims=True)
        vecs_ref[1:2] += jnp.sum(grad_normed, axis=0, keepdims=True)
        grad_x = grad_mids[b] + norm_back(grad_normed, unit, inverse, g1_ref[depth : depth + 1])
        g_out_ref[b] = grad_x.astype(g_out_ref.dtype)
        if last:
            dy = (before_gate_ref[b][:, 0:1] * grad_x).astype(BF16)
            dy_rows_ref[pl.ds(step * len(some) + b, 1), 0:HW, :] = dy[None]

    @pl.when(step == pl.num_programs(0) - 1)
    def _():
        for acc, columns in ((attend_acc, slice(0, 3 * D)), (out_acc, slice(3 * D, 4 * D))):
            if order:
                spread_blocks(order_ref, acc, *mats_refs, columns)
            else:
                mats_refs[0][:, columns] = acc[...].astype(BF16)
        if last:
            rows = dy_rows_ref[...].reshape(images * TPAD, D)
            send_rows([outgoing], before_target_ref[...], rows)


def run_backward(
    depth, grad, dn_back, extra, saved, route_rows, target_rows, shared, order=None
):
    images = grad.shape[0]
    last = depth == LAYERS - 1
    args, specs = [], []
    if order is not None:
        args.append(order)
        specs.append(pl.BlockSpec(memory_space=pltpu.SMEM))
    args += [grad] + list(dn_back)
    specs += [by_image(grad.shape)] + [whole(chunk.shape) for chunk in dn_back]
    if last:
        y_back, before_gate, before_target = extra
        args += list(y_back) + [before_gate, before_target]
        specs += [whole(chunk.shape) for chunk in y_back]
        specs += [by_image(before_gate.shape), whole(before_target.shape)]
    else:
        args.append(extra)
        specs.append(by_image(extra.shape))
    for array in saved + [route_rows, target_rows]:
        args.append(array)
        specs.append(by_image(array.shape))
    for name in ("first_gain", "second_gain"):
        args.append(shared[name])
        specs.append(whole(shared[name].shape))
    for name in ("attend_weight", "output_weight", "router"):
        args.append(shared[name])
        specs.append(layer_of(shared[name].shape, depth))
    for name in ("bias", "mask", "perm", "perm_back"):
        args.append(shared[name][depth])
        specs.append(whole(shared[name][depth].shape))
    token_shape = (images, HW, D)
    outs = [
        (token_shape, F32 if last else BF16, by_image(token_shape)),
    ]
    if order is None:
        outs.append(((D, 4 * D), BF16, whole((D, 4 * D))))
    else:
        outs += [((D // 2, 4 * D), BF16, whole((D // 2, 4 * D)))] * 2
    outs += [
        ((16, D), F32, whole((16, D))),
        ((LPAD, GROUPS * GW), F32, whole((LPAD, GROUPS * GW))),
    ]
    if last:
        outs.append((token_shape, BF16, by_image(token_shape)))
        outs += [((ROWS, D), BF16, whole((ROWS, D)))] * EXPERTS
    some = images_of(images)
    scratch = [
        pltpu.VMEM((D, 3 * D), F32),
        pltpu.VMEM((D, D), F32),
        pltpu.VMEM((some, WROWS, 3 * D), BF16),
        pltpu.VMEM((some, WROWS, D), BF16),
        pltpu.VMEM((len(dn_back) // EXPERTS, SLOTS, D), BF16),
    ]
    if last:
        scratch.append(pltpu.VMEM((len(y_back) // EXPERTS, SLOTS, D), BF16))
        scratch.append(pltpu.VMEM((images, TPAD, D), BF16))
    return pl.pallas_call(
        partial(backward_kernel, depth, images, len(dn_back), order is not None),
        grid=(images // images_of(images),),
        in_specs=specs,
        out_specs=[o[2] for o in outs],
        out_shape=[jax.ShapeDtypeStruct(o[0], o[1]) for o in outs],
        scratch_shapes=scratch,
        compiler_params=pltpu.CompilerParams(vmem_limit_bytes=VMEM_BYTES),
        cost_estimate=cost(33 if last else 24),
        name="backward_%d" % depth,
    )(*args)


def bits_of(axis, low, high):
    steps = []
    bit = low
    while bit < high:
        steps.append((axis, bit))
        bit *= 2
    return steps


def swap(x, step):
    axis, bit = step
    size = lax.axis_size(axis)
    return lax.ppermute(x, axis, [(i, i ^ bit) for i in range(size)])


def bit_at(step):
    axis, bit = step
    return (lax.axis_index(axis) // bit) % 2


def halved(rows, steps, least):
    count = 0
    while count < len(steps) and rows % 2 == 0 and rows // 2 >= least:
        rows //= 2
        count += 1
    return count


def sum_over(x, steps, least=24):
    count = halved(x.shape[0], steps, least)
    x = sum_all(scatter_sum(x, steps[:count]), steps[count:])
    return gather_all(x, steps[:count])


def scatter_sum(x, steps):
    for step in steps:
        half = x.shape[0] // 2
        mine = bit_at(step)
        keep = lax.dynamic_slice_in_dim(x, mine * half, half, 0)
        away = lax.dynamic_slice_in_dim(x, (1 - mine) * half, half, 0)
        x = (keep.astype(F32) + swap(away, step).astype(F32)).astype(x.dtype)
    return x


def gather_all(x, steps, dim=0):
    for step in reversed(steps):
        other = swap(x, step)
        mine = bit_at(step)
        first = jnp.where(mine == 0, x, other)
        second = jnp.where(mine == 0, other, x)
        x = jnp.concatenate([first, second], axis=dim)
    return x


def sum_all(x, steps):
    for step in steps:
        x = (x.astype(F32) + swap(x, step).astype(F32)).astype(x.dtype)
    return x


def exchange(chunks):
    groups = lax.axis_size("expert")
    if groups > EXPERTS:
        rows = jnp.stack(chunks)
        rows = lax.all_to_all(rows, "expert", split_axis=0, concat_axis=0, tiled=True)
        return [rows[k] for k in range(groups)]
    out = list(chunks)
    for k in SEND_ORDER:
        out[k] = lax.ppermute(chunks[k], "expert", [(i, i ^ k) for i in range(groups)])
    return out


def to_experts(chunks, slices):
    return exchange([chunk for chunk in chunks for _ in range(slices)])


def unpack_down(packed):
    width = packed.shape[1]
    return jnp.concatenate(
        [packed[:, j * D : (j + 1) * D] for j in range(width // D)], axis=0
    )


def add_kernel(cuts, keep_ref, got_ref, *outs):
    total = keep_ref[...].astype(F32) + got_ref[...].astype(F32)
    for (start, stop), out in zip(cuts, outs):
        out[...] = total[start:stop].astype(out.dtype)


def add_rows(keep, got, cuts):
    rows, width = got.shape
    return pl.pallas_call(
        partial(add_kernel, cuts),
        grid=(1,),
        in_specs=[pl.BlockSpec((rows, width), lambda i: (0, 0))] * 2,
        out_specs=[pl.BlockSpec((b - a, width), lambda i: (0, 0)) for a, b in cuts],
        out_shape=[jax.ShapeDtypeStruct((b - a, width), keep.dtype) for a, b in cuts],
        compiler_params=pltpu.CompilerParams(vmem_limit_bytes=12 * 1024 * 1024),
        cost_estimate=cost(1),
        name="add_rows",
    )(keep, got)


def join_kernel(first_ref, second_ref, out_ref):
    rows = first_ref.shape[0]
    out_ref[0:rows] = first_ref[...]
    out_ref[rows:] = second_ref[...]


def join_rows(first, second):
    rows, width = first.shape
    return pl.pallas_call(
        join_kernel,
        out_shape=jax.ShapeDtypeStruct((2 * rows, width), first.dtype),
        compiler_params=pltpu.CompilerParams(vmem_limit_bytes=8 * 1024 * 1024),
        cost_estimate=cost(1),
        name="join_rows",
    )(first, second)


def expert_outputs_kernel(earlier, order_ref, *refs):
    pieces, refs = refs[:8], refs[8:]
    refs = refs[4 if earlier else 0 :]
    outs, (rows_ref,) = refs[:4], refs[4:]
    step = pl.program_id(0)
    quarter = pieces[0].shape[0]

    @pl.when(step == 0)
    def _():
        for kind in range(2):
            for r in range(4):
                rows_ref[kind, r * quarter : (r + 1) * quarter] = pieces[kind * 4 + r][...]

    half = pl.num_programs(0)
    for kind in range(2):
        for part in range(2):
            place = jnp.bitwise_xor(order_ref[0], step + part * half)
            start = pl.multiple_of(place * BLOCK, BLOCK)
            block = rows_ref[kind, pl.ds(start, BLOCK)].astype(F32)
            out = outs[kind * 2 + part]
            if part == 0:
                out[0] = block
            else:
                for c in range(out.shape[1]):
                    out[0, c] = block[:, c * D : (c + 1) * D]


def expert_outputs(depth, order, residual, core, earlier):
    width = residual[0].shape[1]
    half = D // BLOCK
    count = width // D
    up = jax.ShapeDtypeStruct((LAYERS, D, width), F32)
    down = jax.ShapeDtypeStruct((LAYERS, count, D, D), F32)
    up_spec = pl.BlockSpec((1, BLOCK, width), lambda i: (depth, i, 0))
    down_spec = pl.BlockSpec((1, count, BLOCK, D), lambda i: (depth, 0, i, 0))
    pieces = residual + core
    earlier = list(earlier or [])
    return pl.pallas_call(
        partial(expert_outputs_kernel, bool(earlier)),
        grid=(half,),
        in_specs=[pl.BlockSpec(memory_space=pltpu.SMEM)]
        + [whole(p.shape) for p in pieces]
        + [pl.BlockSpec(memory_space=pl.ANY)] * len(earlier),
        out_specs=[up_spec, down_spec] * 2,
        out_shape=[up, down] * 2,
        scratch_shapes=[pltpu.VMEM((2, 2 * D, width), BF16)],
        input_output_aliases={9 + i: i for i in range(len(earlier))},
        compiler_params=pltpu.CompilerParams(vmem_limit_bytes=32 * 1024 * 1024),
        cost_estimate=cost(4),
        name="expert_outputs",
    )(order, *pieces, *earlier)


def attend_outputs_kernel(earlier, order_ref, *refs):
    pieces, refs = refs[:2], refs[2:]
    refs = refs[2 if earlier else 0 :]
    attend_ref, out_ref, rows_ref = refs
    half = pieces[0].shape[0]
    for r in range(2):
        rows_ref[r * half : (r + 1) * half] = pieces[r][...].astype(F32)
    for j in range(D // BLOCK):
        start = pl.multiple_of(jnp.bitwise_xor(order_ref[0], j) * BLOCK, BLOCK)
        block = rows_ref[pl.ds(start, BLOCK)]
        attend_ref[0, j * BLOCK : (j + 1) * BLOCK] = block[:, : 3 * D]
        out_ref[0, j * BLOCK : (j + 1) * BLOCK] = block[:, 3 * D :]


def attend_outputs(depth, order, pieces, earlier):
    earlier = list(earlier or [])
    shapes = [(LAYERS, D, 3 * D), (LAYERS, D, D)]
    return pl.pallas_call(
        partial(attend_outputs_kernel, bool(earlier)),
        grid=(1,),
        in_specs=[pl.BlockSpec(memory_space=pltpu.SMEM)]
        + [whole(p.shape) for p in pieces]
        + [pl.BlockSpec(memory_space=pl.ANY)] * len(earlier),
        out_specs=[layer_of(shape, depth) for shape in shapes],
        out_shape=[jax.ShapeDtypeStruct(shape, F32) for shape in shapes],
        scratch_shapes=[pltpu.VMEM((D, 4 * D), F32)],
        input_output_aliases={3 + i: i for i in range(len(earlier))},
        compiler_params=pltpu.CompilerParams(vmem_limit_bytes=24 * 1024 * 1024),
        cost_estimate=cost(2),
        name="attend_outputs",
    )(order, *pieces, *earlier)


CORE, ROW = ("dp", 1), ("dp", 2)
NEAR_X, NEAR_Z, FAR_Z = ("expert", 1), ("expert", 2), ("expert", 4)


def place_order(steps):
    order = 0
    for step in steps:
        order = order * 2 + bit_at(step)
    return jnp.full((1,), order, jnp.int32)


class ExpertSum:
    def __init__(self, keep, send):
        self.keep, self.send = keep, send
        self.steps = iter(
            (self.core, self.row, self.near_x, self.near_z, self.far_z, self.back_z, self.back_x)
        )

    def run(self, count):
        for _ in range(count):
            next(self.steps)()
        return self.done

    def core(self):
        quarter = self.keep.shape[0] // 2
        cuts = ((0, quarter), (quarter, 2 * quarter))
        self.keep, self.send = add_rows(self.keep, swap(self.send, CORE), cuts)
        self.done = [self.keep, self.send]

    def row(self):
        quarter = self.keep.shape[0]
        cuts = ((0, quarter), (quarter // 2, quarter))
        self.mine, self.send = add_rows(self.keep, swap(self.send, ROW), cuts)
        self.done = [self.mine, self.send]

    def near_x(self):
        rows = self.send.shape[0]
        cuts = ((0, rows // 2), (rows // 2, rows))
        self.keep, self.send = add_rows(self.mine, swap(self.send, NEAR_X), cuts)
        self.done = [self.keep, self.send]

    def near_z(self):
        rows = self.send.shape[0]
        (self.total,) = add_rows(self.keep, swap(self.send, NEAR_Z), ((0, rows),))
        self.done = [self.total]

    def far_z(self):
        rows = self.total.shape[0]
        (self.total,) = add_rows(self.total, swap(self.total, FAR_Z), ((0, rows),))
        self.done = [self.total]

    def back_z(self):
        self.total = join_rows(self.total, swap(self.total, NEAR_Z))
        self.done = [self.total]

    def back_x(self):
        self.total = join_rows(self.total, swap(self.total, NEAR_X))
        self.done = [self.total]

    def residual_row(self):
        self.mine_row = swap(self.mine, ROW)
        return [self.mine_row]

    def residual_core(self):
        self.residual = [self.mine, self.mine_row, swap(self.mine, CORE), swap(self.mine_row, CORE)]
        return self.residual[2:]

    def core_row(self):
        self.total_row = swap(self.total, ROW)
        return [self.total_row]

    def core_core(self):
        self.whole = [self.total, self.total_row, swap(self.total, CORE), swap(self.total_row, CORE)]
        return self.whole[2:]


class AttendSum:
    def __init__(self, keep, send):
        self.keep, self.send = keep, send
        self.steps = iter(
            [lambda step=step: self.halve(step) for step in (CORE, ROW, NEAR_X)]
            + [lambda step=step: self.add(step) for step in (NEAR_Z, FAR_Z)]
            + [lambda step=step: self.join(step) for step in (NEAR_X, ROW)]
            + [self.last]
        )

    def run(self, count):
        for _ in range(count):
            next(self.steps)()
        return self.done

    def halve(self, step):
        rows = self.send.shape[0]
        got = swap(self.send, step)
        if step == NEAR_X:
            (self.keep,) = add_rows(self.keep, got, ((0, rows),))
            self.done = [self.keep]
        else:
            cuts = ((0, rows // 2), (rows // 2, rows))
            self.keep, self.send = add_rows(self.keep, got, cuts)
            self.done = [self.keep, self.send]

    def add(self, step):
        (self.keep,) = add_rows(self.keep, swap(self.keep, step), ((0, self.keep.shape[0]),))
        self.done = [self.keep]

    def join(self, step):
        self.keep = join_rows(self.keep, swap(self.keep, step))
        self.done = [self.keep]

    def last(self):
        self.pieces = [self.keep, swap(self.keep, CORE)]
        self.done = self.pieces


def after(value, *done):
    return lax.optimization_barrier((value,) + done)[0]


def body(
    block_input,
    routes,
    first_gain,
    first_shift,
    attend_weight,
    bias_table,
    output_weight,
    second_gain,
    second_shift,
    router_weight,
    core_up,
    core_down,
    residual_up,
    residual_down,
    cotangent,
):
    groups = lax.axis_size("expert")
    slices = groups // EXPERTS
    group_part = lax.axis_index("expert") % slices
    images = block_input.shape[0]
    width = residual_up.shape[2]

    routes_rows = jnp.pad(
        routes.reshape(LAYERS, images, HW), ((0, 0), (0, 0), (0, TPAD - HW)), constant_values=-1
    )
    flip = lax.axis_index("expert") if slices == 1 else 0
    targets = run_routing(routes_rows, jnp.full((1,), flip, jnp.int32))

    table_index = jnp.asarray(offset_table(), jnp.int32)
    picker = (jnp.arange(OFFSETS, dtype=jnp.int32)[:, None] == table_index[None, :]).astype(F32)
    flat_table = bias_table.transpose(0, 2, 1).reshape(LAYERS * HEADS, OFFSETS)
    bias = jnp.dot(flat_table, picker, precision=lax.Precision.HIGHEST)
    bias = (
        bias.reshape(LAYERS, HEADS, LPAD, LPAD)
        .transpose(0, 2, 1, 3)
        .reshape(LAYERS, LPAD, HEADS * LPAD)
    )
    offsets = [SHIFT * (depth % 2) for depth in range(LAYERS)]
    shared = {
        "first_gain": first_gain,
        "first_shift": first_shift,
        "second_gain": second_gain,
        "second_shift": second_shift,
        "attend_weight": attend_weight,
        "output_weight": output_weight,
        "router": jnp.pad(router_weight, ((0, 0), (0, 0), (0, LANES - EXPERTS))),
        "bias": [bias[depth] for depth in range(LAYERS)],
        "mask": [jnp.asarray(score_mask(o)) for o in offsets],
        "perm": [jnp.asarray(permutation(o), BF16) for o in offsets],
        "perm_back": [jnp.asarray(permutation(o).T, BF16) for o in offsets],
    }
    route_rows = [routes_rows[d].reshape(images, 1, TPAD) for d in range(LAYERS)]
    target_rows = [targets[d].reshape(images, 1, TPAD) for d in range(LAYERS)]
    target_all = [targets[d].reshape(1, images * TPAD) for d in range(LAYERS)]
    ups, downs = [], []
    for d in range(LAYERS):
        up_core = lax.dynamic_slice_in_dim(core_up[d], group_part * width, width, 1)
        down_core = lax.dynamic_slice_in_dim(core_down[d], group_part * width, width, 0)
        ups.append((up_core.astype(F32) + residual_up[d].astype(F32)).astype(BF16))
        downs.append((down_core.astype(F32) + residual_down[d].astype(F32)).astype(BF16))

    picked_type = BF16 if slices == 1 else F32
    saved, inner, gates, xs, picks = [], [], [], [block_input], []
    x, earlier = block_input, None
    dy_arrived = None
    def in_parts(chunks):
        return [chunks[i : i + PART] for i in range(0, len(chunks), PART)]

    for d in range(LAYERS):
        outs, outgoing = run_forward(
            d, x, earlier, cotangent, route_rows[d], target_rows[d], target_all[d], shared
        )
        qkv, a, mixed, mid, n, probs, gate = outs[:7]
        if d:
            xs.append(outs[7])
            picks.append(outs[8])
        arrived = to_experts(outgoing[0], slices)
        if d == LAYERS - 1:
            dy_arrived = to_experts(outgoing[1], slices)
        ys, hiddens, slopes = [], [], []
        for part in in_parts(arrived):
            y, (hidden, slope) = run_expert_forward(part, ups[d], downs[d])
            ys += y
            hiddens.append(hidden)
            slopes.append(slope)
        back = exchange(ys)
        earlier = (back, gate, target_rows[d], picked_type)
        x = mid
        gates.append(gate)
        saved.append([xs[d], qkv, a, mixed, mid, n, probs, gate])
        inner.append((arrived, hiddens, slopes))

    grad = cotangent
    vecs, tables = [None] * 2, [None] * 2
    block_output = None
    alone = slices == 1
    expert_order = place_order((CORE, ROW, NEAR_X, NEAR_Z)) if alone else None
    attend_order = place_order((CORE, ROW, NEAR_X)) if alone else None
    expert_sums, attend_sums = [None] * 2, [None] * 2
    for d in reversed(range(LAYERS)):
        arrived, hiddens, slopes = inner[d]
        dns, dus = [], []
        for at, (part, slope) in enumerate(zip(in_parts(dy_arrived), slopes)):
            if alone and d == 0:
                if at == 0:
                    slope = after(slope, *expert_sums[1].run(1))
                    expert_sums[1].residual_row()
                else:
                    slope = after(slope, *expert_sums[1].run(1), *attend_sums[1].run(1))
            dn, (du,) = run_expert_inner(part, slope, ups[d], downs[d])
            dns += dn
            dus.append(du)
        dn_back = exchange(dns)
        grads = run_expert_weights(arrived, dy_arrived, hiddens, dus, expert_order)
        expert_sums[d] = ExpertSum(*grads) if alone else grads
        if d == LAYERS - 1:
            extra = (earlier[0], gates[d - 1], target_all[d - 1])
        else:
            extra = picks[d]
        if alone:
            done = expert_sums[d].run(1 if d else 2)
            if d == 0:
                done = done + expert_sums[1].run(4) + [expert_sums[1].mine_row]
                done = done + attend_sums[1].run(4)
            grad = after(grad, *done)
        outs = run_backward(
            d,
            grad,
            dn_back,
            extra,
            saved[d],
            route_rows[d],
            target_rows[d],
            shared,
            attend_order,
        )
        if alone:
            grad, keep, send, vecs[d], tables[d] = outs[:5]
            attend_sums[d] = AttendSum(keep, send)
            outs = outs[5:]
        else:
            grad, attend_sums[d], vecs[d], tables[d] = outs[:4]
            outs = outs[4:]
        if d == LAYERS - 1:
            block_output = outs[0]
            dy_arrived = to_experts(outs[1:], slices)
    input_grad = grad

    dp_steps = bits_of("dp", 1, lax.axis_size("dp"))
    slice_steps = bits_of("expert", 1, slices)
    sum_steps = bits_of("expert", slices, groups)
    all_steps = dp_steps + slice_steps + sum_steps
    if alone:
        experts, full = None, None
        for d in reversed(range(LAYERS)):
            sums, attend = expert_sums[d], attend_sums[d]
            if d:
                sums.residual_core()
                sums.core_row()
                sums.core_core()
                attend.run(3)
            else:
                sums.residual_row()
                sums.run(5)
                sums.residual_core()
                sums.core_row()
                sums.core_core()
                attend.run(8)
            experts = expert_outputs(d, expert_order, sums.residual, sums.whole, experts)
            full = attend_outputs(d, attend_order, attend.pieces, full)
        residual_up_grad, residual_down_grad, core_up_grad, core_down_grad = experts
        residual_down_grad = residual_down_grad.reshape(LAYERS, width, D)
        core_down_grad = core_down_grad.reshape(LAYERS, width, D)
        attend_weight_grad, output_weight_grad = full
    else:
        residual, core, full = [], [], []
        for d in range(LAYERS):
            part = scatter_sum(expert_sums[d], dp_steps)
            residual.append(gather_all(part, dp_steps))
            total = gather_all(sum_over(part, sum_steps), dp_steps)
            core.append(gather_all(total, slice_steps, dim=1))
            full.append(sum_over(attend_sums[d], all_steps))
        full = jnp.stack(full).astype(F32)
        attend_weight_grad, output_weight_grad = full[:, :, : 3 * D], full[:, :, 3 * D :]
        residual_up_grad = jnp.stack([r[:D] for r in residual]).astype(F32)
        residual_down_grad = jnp.stack([unpack_down(r[D:]) for r in residual]).astype(F32)
        core_up_grad = jnp.stack([c[:D] for c in core]).astype(F32)
        core_down_grad = jnp.stack([unpack_down(c[D:]) for c in core]).astype(F32)
    table_grad = jnp.stack(tables).reshape(LAYERS, LPAD, HEADS, LPAD).transpose(0, 2, 1, 3)
    table_grad = jnp.dot(
        table_grad.reshape(LAYERS * HEADS, LPAD * LPAD), picker.T, precision=lax.Precision.HIGHEST
    )
    small = jnp.concatenate(
        [
            jnp.stack(vecs).reshape(LAYERS * 16, D),
            jnp.pad(table_grad, ((0, 0), (0, D - OFFSETS))),
        ],
        axis=0,
    )
    small = sum_all(small, all_steps)
    vec = small[: LAYERS * 16].reshape(LAYERS, 16, D)
    table = small[LAYERS * 16 :, :OFFSETS].reshape(LAYERS, HEADS, OFFSETS).transpose(0, 2, 1)
    return (
        block_output,
        input_grad,
        vec[:, 0],
        vec[:, 1],
        attend_weight_grad,
        table,
        output_weight_grad,
        vec[:, 2],
        vec[:, 3],
        vec[:, 8:16].transpose(0, 2, 1),
        core_up_grad,
        core_down_grad,
        residual_up_grad,
        residual_down_grad,
    )


def solution(mesh):
    placed = (
        P(("dp", "expert"), None, None),
        P(None, ("dp", "expert"), None, None),
        P(),
        P(),
        P(),
        P(),
        P(),
        P(),
        P(),
        P(),
        P(),
        P(),
        P(None, None, "expert"),
        P(None, "expert", None),
        P(("dp", "expert"), None, None),
    )
    return jax.shard_map(
        body,
        mesh=mesh,
        in_specs=placed,
        out_specs=(
            P(("dp", "expert"), None, None),
            P(("dp", "expert"), None, None),
            P(),
            P(),
            P(),
            P(),
            P(),
            P(),
            P(),
            P(),
            P(),
            P(),
            P(None, None, "expert"),
            P(None, "expert", None),
        ),
        check_vma=False,
    )
```

```python
from functools import partial

import jax
import jax.numpy as jnp
import numpy as np
from jax import lax
from jax.experimental import pallas as pl
from jax.experimental.pallas import tpu as pltpu
from jax.sharding import PartitionSpec as P

D = 384
HEADS = 12
HD = 32
FF = 1536
EXPERTS = 8
WIN = 7
SIDE = 14
SHIFT = 3
LAYERS = 2
HW = 196
CAP = 184
OFFSETS = 169
ROWS = 192
SLOTS = EXPERTS * ROWS

WINDOWS = (SIDE // WIN) * (SIDE // WIN)
LENGTH = WIN * WIN
LPAD = 64
WROWS = WINDOWS * LPAD
TPAD = 256
LANES = 128
GROUP = LANES // HD
GROUPS = HEADS // GROUP
GW = GROUP * LPAD
FCHUNK = 384
SOURCES = 2
FTILE = 512
EXPERT_VMEM = 32 * 1024 * 1024
BLOCK = 48
PAIRS_AT_ONCE = 2
TEAM = 4
STEP_IMAGES = 3

F32 = jnp.float32
BF16 = jnp.bfloat16
eps_norm = 1e-05
mask_fill = -100.0
pad_fill = -1e30
score_scale = HD ** (-0.5)
VMEM_BYTES = 56 * 1024 * 1024

NN = (((1,), (0,)), ((), ()))
NT = (((1,), (1,)), ((), ()))
TN = (((0,), (0,)), ((), ()))


def mm(a, b, dims=NN):
    return lax.dot_general(a, b, dims, preferred_element_type=F32)


def window_tokens(offset):
    rows = np.full((WINDOWS, LPAD), -1, np.int64)
    per_side = SIDE // WIN
    for w in range(WINDOWS):
        for i in range(LENGTH):
            r = (w // per_side) * WIN + i // WIN
            c = (w % per_side) * WIN + i % WIN
            rows[w, i] = ((r + offset) % SIDE) * SIDE + (c + offset) % SIDE
    return rows.reshape(-1)


def permutation(offset):
    rows = window_tokens(offset)
    return (rows[:, None] == np.arange(HW)[None, :]).astype(np.float32)


def score_mask(offset):
    coords = np.arange(SIDE)
    bands = (coords >= SIDE - WIN).astype(int) + (coords >= SIDE - offset).astype(int)
    labels = bands[:, None] * 3 + bands[None, :]
    per_side = SIDE // WIN
    out = np.zeros((WINDOWS, LPAD, LPAD), np.float32)
    for w in range(WINDOWS):
        r0, c0 = (w // per_side) * WIN, (w % per_side) * WIN
        flat = labels[r0 : r0 + WIN, c0 : c0 + WIN].reshape(-1)
        out[w, :LENGTH, :LENGTH] = np.where(flat[:, None] == flat[None, :], 0.0, mask_fill)
        out[w, LENGTH:, :] = pad_fill
    return np.tile(out, (1, 1, GROUP))


def offset_table():
    i = np.arange(LENGTH)
    r, c = i // WIN, i % WIN
    index = np.full((LPAD, LPAD), -1, np.int64)
    index[:LENGTH, :LENGTH] = (
        (r[None, :] - r[:, None] + WIN - 1) * (2 * WIN - 1) + c[None, :] - c[:, None] + WIN - 1
    )
    return index.reshape(-1)


def norm_parts(x):
    centred = x - jnp.mean(x, axis=-1, keepdims=True)
    inverse = lax.rsqrt(jnp.mean(centred * centred, axis=-1, keepdims=True) + eps_norm)
    return centred * inverse, inverse


def norm_back(grad, unit, inverse, gain):
    scaled = grad * gain
    return inverse * (
        scaled
        - jnp.mean(scaled, axis=-1, keepdims=True)
        - unit * jnp.mean(scaled * unit, axis=-1, keepdims=True)
    )


def one_hot(cond):
    return jnp.where(cond, 1.0, 0.0).astype(BF16)


def head_masks():
    lane = lax.broadcasted_iota(jnp.int32, (1, LANES), 1) // HD
    return [jnp.where(lane == h, 1.0, 0.0) for h in range(GROUP)]


def spread_heads(block, masks):
    return jnp.concatenate([block * m.astype(BF16) for m in masks], axis=0)


def fold_heads(tall, masks):
    total = tall[0:LPAD] * masks[0]
    for h in range(1, GROUP):
        total = total + tall[h * LPAD : (h + 1) * LPAD] * masks[h]
    return total


def as_column(row, count):
    wide = jnp.broadcast_to(row.astype(F32), (8, TPAD))
    return wide.T[:count, 0:1].astype(jnp.int32)


def pick_rows(target_row, rows_ref):
    column = as_column(target_row, HW)
    place = one_hot(lax.broadcasted_iota(jnp.int32, (HW, SLOTS), 1) == column)
    total = mm(place, rows_ref[0])
    for k in range(1, rows_ref.shape[0]):
        total = total + mm(place, rows_ref[k])
    return total


def send_rows(out_ref, target_all, rows):
    step = SLOTS // 4
    for c in range(4):
        slot = lax.broadcasted_iota(jnp.int32, (step, rows.shape[0]), 0) + c * step
        out_ref[c * step : (c + 1) * step] = mm(one_hot(slot == target_all), rows).astype(BF16)


def gelu_parts(u):
    cdf = 0.5 + 0.5 * lax.erf(u * (0.5**0.5))
    bell = jnp.exp(-0.5 * u * u)
    return u * cdf, cdf + u * (bell * 0.3989422804014327)


def cost(microseconds):
    return pl.CostEstimate(
        flops=int(microseconds * 9e8), bytes_accessed=1000, transcendentals=0
    )


def routing_kernel(paired, half_ref, routes_ref, target_ref):
    before = one_hot(
        lax.broadcasted_iota(jnp.int32, (TPAD, TPAD), 0)
        <= lax.broadcasted_iota(jnp.int32, (TPAD, TPAD), 1)
    )
    expert = lax.broadcasted_iota(jnp.int32, (16, TPAD), 0)
    for depth in range(LAYERS):
        carry = jnp.zeros((16, 1), F32)
        for i in range(routes_ref.shape[1]):
            row = routes_ref[depth, i : i + 1, :]
            chosen = jnp.where(expert == row, 1.0, 0.0)
            counts = mm(chosen.astype(BF16), before) + carry
            carry = counts[:, TPAD - 1 : TPAD]
            slot = jnp.sum(chosen * counts, axis=0, keepdims=True).astype(jnp.int32) - 1
            kept = (slot >= 0) & (slot < CAP)
            place = row
            if paired:
                place = (row % TEAM) * 2 + jnp.bitwise_xor(row // TEAM, half_ref[0])
            target_ref[depth, i : i + 1, :] = jnp.where(kept, place * ROWS + slot, -1)


def run_routing(routes, half, paired):
    return pl.pallas_call(
        partial(routing_kernel, paired),
        in_specs=[
            pl.BlockSpec(memory_space=pltpu.SMEM),
            pl.BlockSpec(memory_space=pltpu.VMEM),
        ],
        out_shape=jax.ShapeDtypeStruct(routes.shape, jnp.int32),
        name="routing",
    )(half, routes)


def group_cols(part, g):
    return slice(part * D + g * LANES, part * D + (g + 1) * LANES)


def softmax_down(scores):
    raised = jnp.exp(scores - jnp.max(scores, axis=0, keepdims=True))
    return raised * (1.0 / jnp.sum(raised, axis=0, keepdims=True))


def window_items(some):
    pairs = [(w, g) for w in range(WINDOWS) for g in range(GROUPS)]
    runs = []
    for first in range(0, len(pairs), PAIRS_AT_ONCE):
        runs.append([(w, g, b) for w, g in pairs[first : first + PAIRS_AT_ONCE] for b in some])
    return runs


def raw_scores(qkv_ref, items, masks):
    wide, scores = [], []
    for w, g, b in items:
        rows = slice(w * LPAD, (w + 1) * LPAD)
        wide.append(spread_heads(qkv_ref[b, rows, group_cols(0, g)], masks))
    for (w, g, b), q_wide in zip(items, wide):
        rows = slice(w * LPAD, (w + 1) * LPAD)
        scores.append(mm(qkv_ref[b, rows, group_cols(1, g)], q_wide, NT))
    return wide, scores


def to_probs(items, scores, bias_ref, mask_ref):
    probs = []
    for (w, g, b), score in zip(items, scores):
        probs.append(
            softmax_down(
                score * score_scale + bias_ref[:, g * GW : (g + 1) * GW] + mask_ref[w]
            )
        )
    return probs


def forward_kernel(depth, images, *refs):
    last = depth == LAYERS - 1
    refs = list(refs)
    take = lambda: refs.pop(0)
    x_ref = take()
    if depth:
        back_ref, gate_in_ref, target_in_ref = take(), take(), take()
    if last:
        cot_ref = take()
    (route_ref, target_ref, g1_ref, s1_ref, g2_ref, s2_ref, attend_ref, out_w_ref) = refs[:8]
    (router_ref, bias_ref, mask_ref, perm_ref, perm_back_ref) = refs[8:13]
    refs = refs[13:]
    (qkv_ref, a_ref, mixed_ref, mid_ref, n_ref, probs_ref, gate_ref) = refs[:7]
    refs = refs[7:]
    if depth:
        x_out_ref, picked_ref = take(), take()
    out_ref, rows_ref = take(), take()

    step = pl.program_id(0)

    @pl.when(step == 0)
    def _():
        rows_ref[...] = jnp.zeros_like(rows_ref)

    some = range(x_ref.shape[0])
    xs = []
    for b in some:
        x = x_ref[b].astype(F32)
        if depth:
            picked = pick_rows(target_in_ref[b], back_ref)
            picked_ref[b] = picked.astype(picked_ref.dtype)
            x = x + gate_in_ref[b][:, 0:1] * picked
            x_out_ref[b] = x
        xs.append(x)
    for b in some:
        unit, _ = norm_parts(xs[b])
        normed = (unit * g1_ref[depth : depth + 1] + s1_ref[depth : depth + 1]).astype(BF16)
        a_ref[b] = mm(perm_ref[...], normed).astype(BF16)
    qkv = mm(a_ref[...].reshape(len(some) * WROWS, D), attend_ref[0]).astype(BF16)
    qkv_ref[...] = qkv.reshape(len(some), WROWS, 3 * D)
    masks = head_masks()
    runs = window_items(some)
    ready = raw_scores(qkv_ref, runs[0], masks)
    for at, items in enumerate(runs):
        _, scores = ready
        if at + 1 < len(runs):
            ready = raw_scores(qkv_ref, runs[at + 1], masks)
        probs = to_probs(items, scores, bias_ref, mask_ref)
        tall = []
        for (w, g, b), p in zip(items, probs):
            rows = slice(w * LPAD, (w + 1) * LPAD)
            tall.append(mm(p.astype(BF16), qkv_ref[b, rows, group_cols(2, g)], TN))
        for (w, g, b), t in zip(items, tall):
            rows = slice(w * LPAD, (w + 1) * LPAD)
            mixed_ref[b, rows, group_cols(0, g)] = fold_heads(t, masks).astype(BF16)
    lane = lax.broadcasted_iota(jnp.int32, (HW, LANES), 1)
    for b in some:
        mixed = mm(perm_back_ref[...], mixed_ref[b]).astype(BF16)
        mid = xs[b] + mm(mixed, out_w_ref[0])
        mid_ref[b] = mid
        unit, _ = norm_parts(mid)
        n = (unit * g2_ref[depth : depth + 1] + s2_ref[depth : depth + 1]).astype(BF16)
        n_ref[b] = n
        logits = jnp.where(lane < EXPERTS, mm(n, router_ref[0]), pad_fill)
        raised = jnp.exp(logits - jnp.max(logits, axis=-1, keepdims=True))
        router = raised / jnp.sum(raised, axis=-1, keepdims=True)
        probs_ref[b] = router
        chosen = lane == as_column(route_ref[b], HW)
        gate = jnp.sum(jnp.where(chosen, router, 0.0), axis=-1, keepdims=True)
        gate_ref[b] = jnp.broadcast_to(gate, (HW, LANES))
        at = step * len(some) + b
        rows_ref[pl.ds(at, 1), 0:HW, 0:D] = n[None]
        if last:
            dy = (gate * cot_ref[b].astype(F32)).astype(BF16)
            rows_ref[pl.ds(at, 1), 0:HW, D : 2 * D] = dy[None]

    @pl.when(step == pl.num_programs(0) - 1)
    def _():
        rows = rows_ref[...].reshape(images * TPAD, rows_ref.shape[2])
        send_rows(out_ref, target_ref[...], rows)


def whole(shape):
    return pl.BlockSpec(shape, lambda i: (0,) * len(shape))


def images_of(images):
    return STEP_IMAGES if images % STEP_IMAGES == 0 else 1


def by_image(shape):
    return pl.BlockSpec(
        (images_of(shape[0]),) + shape[1:], lambda i: (i,) + (0,) * (len(shape) - 1)
    )


def layer_of(shape, depth):
    return pl.BlockSpec((1,) + shape[1:], lambda i: (depth,) + (0,) * (len(shape) - 1))


def run_forward(depth, x, earlier, cotangent, route_rows, target_rows, target_all, shared):
    images = x.shape[0]
    last = depth == LAYERS - 1
    args, specs = [x], [by_image(x.shape)]
    if depth:
        back, gate_in, target_in, picked_type = earlier
        args += [back, gate_in, target_in]
        specs += [whole(back.shape), by_image(gate_in.shape), by_image(target_in.shape)]
    if last:
        args.append(cotangent)
        specs.append(by_image(cotangent.shape))
    args += [route_rows, target_all]
    specs += [by_image(route_rows.shape), whole(target_all.shape)]
    for name in ("first_gain", "first_shift", "second_gain", "second_shift"):
        args.append(shared[name])
        specs.append(whole(shared[name].shape))
    for name in ("attend_weight", "output_weight", "router"):
        args.append(shared[name])
        specs.append(layer_of(shared[name].shape, depth))
    for name in ("bias", "mask", "perm", "perm_back"):
        args.append(shared[name][depth])
        specs.append(whole(shared[name][depth].shape))
    outs = [
        ((images, WROWS, 3 * D), BF16),
        ((images, WROWS, D), BF16),
        ((images, WROWS, D), BF16),
        ((images, HW, D), F32),
        ((images, HW, D), BF16),
        ((images, HW, LANES), F32),
        ((images, HW, LANES), F32),
    ]
    out_specs = [by_image(s) for s, _ in outs]
    if depth:
        outs += [((images, HW, D), F32), ((images, HW, D), picked_type)]
        out_specs += [by_image((images, HW, D))] * 2
    sent = 2 * D if last else D
    outs.append(((SLOTS, sent), BF16))
    out_specs.append(whole((SLOTS, sent)))
    scratch = [pltpu.VMEM((images, TPAD, sent), BF16)]
    results = pl.pallas_call(
        partial(forward_kernel, depth, images),
        grid=(images // images_of(images),),
        in_specs=specs,
        out_specs=out_specs,
        out_shape=[jax.ShapeDtypeStruct(s, t) for s, t in outs],
        scratch_shapes=scratch,
        compiler_params=pltpu.CompilerParams(vmem_limit_bytes=VMEM_BYTES),
        cost_estimate=cost(24 if last else 18),
        name="forward_%d" % depth,
    )(*args)
    return results[:-1], results[-1]


def joined(ref, columns=slice(None)):
    return jnp.concatenate([ref[s, 0, :, columns] for s in range(ref.shape[0])], axis=0)


def spread(ref, value, columns=slice(None)):
    for s in range(ref.shape[0]):
        ref[s, 0, :, columns] = value[s * ROWS : (s + 1) * ROWS]


def hidden_tiles(width):
    tile = FTILE if width % FTILE == 0 else FCHUNK
    return [slice(f, f + tile) for f in range(0, width, tile)]


def expert_forward_kernel(n_ref, up_ref, down_ref, y_ref, hidden_ref):
    n = joined(n_ref)
    tiles = hidden_tiles(up_ref.shape[2])
    ready = mm(n, up_ref[0, :, tiles[0]])
    for at, tile in enumerate(tiles):
        u = ready
        if at + 1 < len(tiles):
            ready = mm(n, up_ref[0, :, tiles[at + 1]])
        hidden_ref[:, tile] = gelu_parts(u)[0].astype(BF16)
    spread(y_ref, mm(hidden_ref[...], down_ref[0]).astype(BF16))


def by_expert(shape):
    return pl.BlockSpec((1,) + shape[1:], lambda k, i: (k,) + (0,) * (len(shape) - 1))


def by_sources(array):
    return pl.BlockSpec((SOURCES, 1) + array.shape[2:], lambda k, i: (i, k, 0, 0))


def run_expert_forward(arrived, up, down):
    total, width = up.shape[0], up.shape[2]
    return pl.pallas_call(
        expert_forward_kernel,
        grid=(total, arrived.shape[0] // SOURCES),
        in_specs=[by_sources(arrived), by_expert(up.shape), by_expert(down.shape)],
        out_specs=by_sources(arrived),
        out_shape=jax.ShapeDtypeStruct(arrived.shape, BF16),
        scratch_shapes=[pltpu.VMEM((SOURCES * ROWS, width), BF16)],
        compiler_params=pltpu.CompilerParams(vmem_limit_bytes=VMEM_BYTES),
        cost_estimate=cost(4 * total),
        name="expert_forward",
    )(arrived, up, down)


def expert_both_kernel(joint, *refs):
    n_ref, refs = refs[0], refs[1:]
    if joint:
        dy = joined(n_ref, slice(D, 2 * D))
    else:
        dy, refs = joined(refs[0]), refs[1:]
    up_ref, down_ref, out_ref, hidden_ref, du_ref = refs
    n = joined(n_ref, slice(0, D))
    tiles = hidden_tiles(up_ref.shape[2])

    def first(tile):
        return mm(n, up_ref[0, :, tile]), mm(dy, down_ref[0, tile], NT)

    ready = first(tiles[0])
    for at, tile in enumerate(tiles):
        u, dh = ready
        if at + 1 < len(tiles):
            ready = first(tiles[at + 1])
        value, slope = gelu_parts(u)
        hidden_ref[0, :, tile] = value.astype(BF16)
        du_ref[0, :, tile] = (dh * slope).astype(BF16)
    dn = mm(du_ref[0], up_ref[0], NT).astype(BF16)
    if joint:
        spread(out_ref, mm(hidden_ref[0], down_ref[0]).astype(BF16), slice(0, D))
        spread(out_ref, dn, slice(D, 2 * D))
    else:
        spread(out_ref, dn)


def run_expert_both(n, dy, up, down):
    total, width, joint = up.shape[0], up.shape[2], dy is None
    args = [n] if joint else [n, dy]
    wide = jax.ShapeDtypeStruct((total, n.shape[0] * ROWS, width), BF16)
    wide_spec = pl.BlockSpec((1, SOURCES * ROWS, width), lambda k, i: (k, i, 0))
    return pl.pallas_call(
        partial(expert_both_kernel, joint),
        grid=(total, n.shape[0] // SOURCES),
        in_specs=[by_sources(array) for array in args]
        + [by_expert(up.shape), by_expert(down.shape)],
        out_specs=[by_sources(n), wide_spec, wide_spec],
        out_shape=[jax.ShapeDtypeStruct(n.shape, BF16), wide, wide],
        compiler_params=pltpu.CompilerParams(vmem_limit_bytes=VMEM_BYTES),
        cost_estimate=cost(6 * total),
        name="expert_both",
    )(*args, up, down)


def expert_weights_kernel(joint, order, *refs):
    if order:
        order_ref, refs = refs[0], refs[1:]
    n_ref, refs = refs[0], refs[1:]
    dy_ref, dy_columns = n_ref, slice(D, 2 * D)
    if not joint:
        dy_ref, dy_columns, refs = refs[0], slice(0, D), refs[1:]
    hidden_ref, du_ref, refs = refs[0], refs[1], refs[2:]
    if order:
        keep_ref, send_ref, n_rows, dy_rows, sum_ref = refs
    else:
        out_ref, n_rows, dy_rows = refs

    @pl.when(pl.program_id(1) == 0)
    def _():
        n_rows[...] = joined(n_ref, slice(0, D))
        dy_rows[...] = joined(dy_ref, dy_columns)

    up = mm(n_rows[...], du_ref[0], TN)
    down = mm(hidden_ref[0], dy_rows[...], TN)
    if order:
        sum_ref[0:D] = up
        sum_ref[D : 2 * D] = down
        spread_experts(order_ref, sum_ref, keep_ref, send_ref)
    else:
        out_ref[0, 0:D] = up.astype(BF16)
        out_ref[0, D : 2 * D] = down.astype(BF16)


def spread_experts(order_ref, sum_ref, keep_ref, send_ref):
    run = sum_ref.shape[0] // BLOCK // 4
    for j in range(4 * run):
        start = pl.multiple_of(jnp.bitwise_xor(order_ref[0], j) * BLOCK, BLOCK)
        block = sum_ref[pl.ds(start, BLOCK)].astype(BF16)
        ref = keep_ref if j < 2 * run else send_ref
        at = j % run * BLOCK
        ref[j // run % 2, 0, at : at + BLOCK] = block


def spread_blocks(order_ref, sum_ref, keep_ref, send_ref, columns):
    count = sum_ref.shape[0] // BLOCK
    for j in range(count):
        start = pl.multiple_of(jnp.bitwise_xor(order_ref[0], j) * BLOCK, BLOCK)
        block = sum_ref[pl.ds(start, BLOCK)].astype(BF16)
        ref = keep_ref if j < count // 2 else send_ref
        at = (j % (count // 2)) * BLOCK
        ref[at : at + BLOCK, columns] = block


def run_expert_weights(n, dy, hidden, du, order=None):
    total, rows, width = hidden.shape
    args = [n] if dy is None else [n, dy]
    specs = [
        pl.BlockSpec((array.shape[0], 1) + array.shape[2:], lambda k, f: (0, k, 0, 0))
        for array in args
    ]
    scratch = [pltpu.VMEM((rows, D), BF16)] * 2
    if order is None:
        shape = jax.ShapeDtypeStruct((total, 2 * D, width), BF16)
        out_specs = pl.BlockSpec((1, 2 * D, FCHUNK), lambda k, f: (k, 0, f))
        leading = []
    else:
        shape = [jax.ShapeDtypeStruct((2, total, D // 2, width), BF16)] * 2
        out_specs = [pl.BlockSpec((2, 1, D // 2, FCHUNK), lambda k, f: (0, k, 0, f))] * 2
        leading = [order]
        scratch.append(pltpu.VMEM((2 * D, FCHUNK), F32))
    wide_spec = pl.BlockSpec((1, rows, FCHUNK), lambda k, f: (k, 0, f))
    results = pl.pallas_call(
        partial(expert_weights_kernel, dy is None, order is not None),
        grid=(total, width // FCHUNK),
        in_specs=[pl.BlockSpec(memory_space=pltpu.SMEM)] * len(leading)
        + specs
        + [wide_spec] * 2,
        out_specs=out_specs,
        out_shape=shape,
        scratch_shapes=scratch,
        compiler_params=pltpu.CompilerParams(vmem_limit_bytes=EXPERT_VMEM),
        cost_estimate=cost(4 * total),
        name="expert_weights",
    )(*leading, *args, hidden, du)
    if order is None:
        return results[0]
    return [r.reshape(total * D, width) for r in results]


def backward_kernel(depth, images, order, *refs):
    last = depth == LAYERS - 1
    refs = list(refs)
    take = lambda: refs.pop(0)
    if order:
        order_ref = take()
    g_ref, back_ref = take(), take()
    if last:
        before_gate_ref, before_target_ref = take(), take()
    else:
        picked_ref = take()
    (x_ref, qkv_ref, a_ref, mixed_ref, mid_ref, n_ref, probs_ref, gate_ref) = refs[:8]
    (route_ref, target_ref, g1_ref, g2_ref, attend_ref, out_w_ref) = refs[8:14]
    (router_ref, bias_ref, mask_ref, perm_ref, perm_back_ref) = refs[14:19]
    refs = refs[19:]
    g_out_ref = take()
    mats_refs = [take() for _ in range(2 if order else 1)]
    vecs_ref, table_ref = take(), take()
    if last:
        result_ref, dy_out_ref = take(), take()
    attend_acc, out_acc, dqkv_ref, dz_ref = (take() for _ in range(4))
    if last:
        dy_rows_ref = take()

    step = pl.program_id(0)

    @pl.when(step == 0)
    def _():
        attend_acc[...] = jnp.zeros_like(attend_acc)
        out_acc[...] = jnp.zeros_like(out_acc)
        vecs_ref[...] = jnp.zeros_like(vecs_ref)
        table_ref[...] = jnp.zeros_like(table_ref)
        if last:
            dy_rows_ref[...] = jnp.zeros_like(dy_rows_ref)

    some = range(g_ref.shape[0])
    lane = lax.broadcasted_iota(jnp.int32, (HW, LANES), 1)
    grad_mids, dmixed_all = [], []
    for b in some:
        grad = g_ref[b].astype(F32)
        mid = mid_ref[b]
        gate = gate_ref[b][:, 0:1]
        rows_back = pick_rows(target_ref[b], back_ref)
        if last:
            picked, rows_back = rows_back[:, 0:D], rows_back[:, D : 2 * D]
            result_ref[b] = (mid + gate * picked).astype(BF16)
        else:
            picked = picked_ref[b].astype(F32)
        gate_grad = jnp.sum(grad * picked, axis=-1, keepdims=True)
        chosen = jnp.where(lane == as_column(route_ref[b], HW), 1.0, 0.0)
        logit_grad = ((gate * gate_grad) * (chosen - probs_ref[b])).astype(BF16)
        router_grad = mm(logit_grad, n_ref[b], TN)
        grad_n = rows_back + mm(logit_grad, router_ref[0], NT)
        unit, inverse = norm_parts(mid)
        vecs_ref[2:3] += jnp.sum(grad_n * unit, axis=0, keepdims=True)
        vecs_ref[3:4] += jnp.sum(grad_n, axis=0, keepdims=True)
        vecs_ref[8:16] += router_grad[0:8]
        grad_mid = grad + norm_back(grad_n, unit, inverse, g2_ref[depth : depth + 1])
        grad_mids.append(grad_mid)
        dz = mm(perm_ref[...], grad_mid.astype(BF16)).astype(BF16)
        dz_ref[b] = dz
    dz = dz_ref[...].reshape(len(some) * WROWS, D)
    out_acc[...] += mm(mixed_ref[...].reshape(len(some) * WROWS, D), dz, TN)
    dmixed_all = mm(dz, out_w_ref[0], NT).astype(BF16)
    masks = head_masks()
    def first_part(items):
        dm_wide, dprobs = [], []
        for w, g, b in items:
            start = b * WROWS + w * LPAD
            dm_wide.append(
                spread_heads(dmixed_all[start : start + LPAD, group_cols(0, g)], masks)
            )
        for (w, g, b), dm in zip(items, dm_wide):
            rows = slice(w * LPAD, (w + 1) * LPAD)
            dprobs.append(mm(qkv_ref[b, rows, group_cols(2, g)], dm, NT))
        return raw_scores(qkv_ref, items, masks) + (dm_wide, dprobs)

    runs = window_items(some)
    ready = first_part(runs[0])
    for at, items in enumerate(runs):
        places = [(b, slice(w * LPAD, (w + 1) * LPAD), g) for w, g, b in items]
        q_wide, scores, dm_wide, dprobs = ready
        if at + 1 < len(runs):
            ready = first_part(runs[at + 1])
        probs = to_probs(items, scores, bias_ref, mask_ref)
        dscores, tables = [], {}
        for (b, rows, g), p, dp in zip(places, probs, dprobs):
            row_dot = jnp.sum(p * dp, axis=0, keepdims=True)
            dscores.append((p * (dp - row_dot)).astype(BF16))
            wide = dscores[-1].astype(F32)
            tables[g] = tables[g] + wide if g in tables else wide
        for g, total in tables.items():
            table_ref[:, g * GW : (g + 1) * GW] += total
        dv, dk, tall = [], [], []
        for p, dm in zip(probs, dm_wide):
            dv.append(mm(p.astype(BF16), dm))
        for ds, q in zip(dscores, q_wide):
            dk.append(mm(ds, q))
        for (b, rows, g), ds in zip(places, dscores):
            tall.append(mm(ds, qkv_ref[b, rows, group_cols(1, g)], TN))
        for i, (b, rows, g) in enumerate(places):
            dq = fold_heads(tall[i], masks) * score_scale
            dqkv_ref[b, rows, group_cols(0, g)] = dq.astype(BF16)
            dqkv_ref[b, rows, group_cols(1, g)] = (dk[i] * score_scale).astype(BF16)
            dqkv_ref[b, rows, group_cols(2, g)] = dv[i].astype(BF16)
    dqkv = dqkv_ref[...].reshape(len(some) * WROWS, 3 * D)
    attend_acc[...] += mm(a_ref[...].reshape(len(some) * WROWS, D), dqkv, TN)
    for b in some:
        dqkv_tokens = mm(perm_back_ref[...], dqkv_ref[b]).astype(BF16)
        grad_normed = mm(dqkv_tokens, attend_ref[0], NT)
        unit, inverse = norm_parts(x_ref[b].astype(F32))
        vecs_ref[0:1] += jnp.sum(grad_normed * unit, axis=0, keepdims=True)
        vecs_ref[1:2] += jnp.sum(grad_normed, axis=0, keepdims=True)
        grad_x = grad_mids[b] + norm_back(grad_normed, unit, inverse, g1_ref[depth : depth + 1])
        g_out_ref[b] = grad_x.astype(g_out_ref.dtype)
        if last:
            dy = (before_gate_ref[b][:, 0:1] * grad_x).astype(BF16)
            dy_rows_ref[pl.ds(step * len(some) + b, 1), 0:HW, :] = dy[None]

    @pl.when(step == pl.num_programs(0) - 1)
    def _():
        for acc, columns in ((attend_acc, slice(0, 3 * D)), (out_acc, slice(3 * D, 4 * D))):
            if order:
                spread_blocks(order_ref, acc, *mats_refs, columns)
            else:
                mats_refs[0][:, columns] = acc[...].astype(BF16)
        if last:
            rows = dy_rows_ref[...].reshape(images * TPAD, D)
            send_rows(dy_out_ref, before_target_ref[...], rows)


def run_backward(
    depth, grad, dn_back, extra, saved, route_rows, target_rows, shared, order=None
):
    images = grad.shape[0]
    last = depth == LAYERS - 1
    args, specs = [], []
    if order is not None:
        args.append(order)
        specs.append(pl.BlockSpec(memory_space=pltpu.SMEM))
    args += [grad, dn_back]
    specs += [by_image(grad.shape), whole(dn_back.shape)]
    if last:
        before_gate, before_target = extra
        args += [before_gate, before_target]
        specs += [by_image(before_gate.shape), whole(before_target.shape)]
    else:
        args.append(extra)
        specs.append(by_image(extra.shape))
    for array in saved + [route_rows, target_rows]:
        args.append(array)
        specs.append(by_image(array.shape))
    for name in ("first_gain", "second_gain"):
        args.append(shared[name])
        specs.append(whole(shared[name].shape))
    for name in ("attend_weight", "output_weight", "router"):
        args.append(shared[name])
        specs.append(layer_of(shared[name].shape, depth))
    for name in ("bias", "mask", "perm", "perm_back"):
        args.append(shared[name][depth])
        specs.append(whole(shared[name][depth].shape))
    token_shape = (images, HW, D)
    outs = [
        (token_shape, F32 if last else BF16, by_image(token_shape)),
    ]
    if order is None:
        outs.append(((D, 4 * D), BF16, whole((D, 4 * D))))
    else:
        outs += [((D // 2, 4 * D), BF16, whole((D // 2, 4 * D)))] * 2
    outs += [
        ((16, D), F32, whole((16, D))),
        ((LPAD, GROUPS * GW), F32, whole((LPAD, GROUPS * GW))),
    ]
    if last:
        outs.append((token_shape, BF16, by_image(token_shape)))
        outs.append(((SLOTS, D), BF16, whole((SLOTS, D))))
    some = images_of(images)
    scratch = [
        pltpu.VMEM((D, 3 * D), F32),
        pltpu.VMEM((D, D), F32),
        pltpu.VMEM((some, WROWS, 3 * D), BF16),
        pltpu.VMEM((some, WROWS, D), BF16),
    ]
    if last:
        scratch.append(pltpu.VMEM((images, TPAD, D), BF16))
    return pl.pallas_call(
        partial(backward_kernel, depth, images, order is not None),
        grid=(images // images_of(images),),
        in_specs=specs,
        out_specs=[o[2] for o in outs],
        out_shape=[jax.ShapeDtypeStruct(o[0], o[1]) for o in outs],
        scratch_shapes=scratch,
        compiler_params=pltpu.CompilerParams(vmem_limit_bytes=VMEM_BYTES),
        cost_estimate=cost(33 if last else 24),
        name="backward_%d" % depth,
    )(*args)


def bits_of(axis, low, high):
    steps = []
    bit = low
    while bit < high:
        steps.append((axis, bit))
        bit *= 2
    return steps


def swap(x, step):
    axis, bit = step
    size = lax.axis_size(axis)
    return lax.ppermute(x, axis, [(i, i ^ bit) for i in range(size)])


def bit_at(step):
    axis, bit = step
    return (lax.axis_index(axis) // bit) % 2


def halved(rows, steps, least):
    count = 0
    while count < len(steps) and rows % 2 == 0 and rows // 2 >= least:
        rows //= 2
        count += 1
    return count


def sum_over(x, steps, least=24):
    count = halved(x.shape[0], steps, least)
    x = sum_all(scatter_sum(x, steps[:count]), steps[count:])
    return gather_all(x, steps[:count])


def scatter_sum(x, steps):
    for step in steps:
        half = x.shape[0] // 2
        mine = bit_at(step)
        keep = lax.dynamic_slice_in_dim(x, mine * half, half, 0)
        away = lax.dynamic_slice_in_dim(x, (1 - mine) * half, half, 0)
        x = (keep.astype(F32) + swap(away, step).astype(F32)).astype(x.dtype)
    return x


def gather_all(x, steps, dim=0):
    for step in reversed(steps):
        other = swap(x, step)
        mine = bit_at(step)
        first = jnp.where(mine == 0, x, other)
        second = jnp.where(mine == 0, other, x)
        x = jnp.concatenate([first, second], axis=dim)
    return x


def sum_all(x, steps):
    for step in steps:
        x = (x.astype(F32) + swap(x, step).astype(F32)).astype(x.dtype)
    return x


def exchange(rows):
    groups = lax.axis_size("expert")
    if groups > EXPERTS:
        teams, size = None, groups
    else:
        teams = [list(range(first, first + TEAM)) for first in range(0, groups, TEAM)]
        size = TEAM
    width = rows.shape[-1]
    runs = rows.reshape(size, -1, width)
    runs = lax.all_to_all(
        runs, "expert", split_axis=0, concat_axis=0, tiled=True, axis_index_groups=teams
    )
    return runs.reshape(size, -1, ROWS, width)


def to_experts(rows, slices):
    if slices > 1:
        runs = rows.reshape(EXPERTS, ROWS, rows.shape[1])
        rows = jnp.repeat(runs, slices, axis=0)
    return exchange(rows)


def from_experts(rows, slices):
    width = rows.shape[-1]
    rows = exchange(rows).reshape(EXPERTS, slices, ROWS, width)
    return rows.transpose(1, 0, 2, 3).reshape(slices, SLOTS, width)


def unpack_down(packed):
    width = packed.shape[1]
    return jnp.concatenate(
        [packed[:, j * D : (j + 1) * D] for j in range(width // D)], axis=0
    )


def add_kernel(cuts, keep_ref, got_ref, *outs):
    total = keep_ref[...].astype(F32) + got_ref[...].astype(F32)
    for (start, stop), out in zip(cuts, outs):
        out[...] = total[start:stop].astype(out.dtype)


def add_rows(keep, got, cuts):
    rows, width = got.shape
    return pl.pallas_call(
        partial(add_kernel, cuts),
        grid=(1,),
        in_specs=[pl.BlockSpec((rows, width), lambda i: (0, 0))] * 2,
        out_specs=[pl.BlockSpec((b - a, width), lambda i: (0, 0)) for a, b in cuts],
        out_shape=[jax.ShapeDtypeStruct((b - a, width), keep.dtype) for a, b in cuts],
        compiler_params=pltpu.CompilerParams(vmem_limit_bytes=12 * 1024 * 1024),
        cost_estimate=cost(1),
        name="add_rows",
    )(keep, got)


def add_last_kernel(keep_ref, got_ref, own_ref, partner_ref, low_ref, high_ref):
    total = keep_ref[...].astype(F32) + got_ref[...].astype(F32)
    half = total.shape[0] // 2
    own, partner = total[0:half].astype(BF16), total[half:].astype(BF16)
    own_ref[...] = own
    partner_ref[...] = partner
    both = (own.astype(F32) + partner.astype(F32)).astype(BF16)
    low_ref[...] = both[0 : half // 2]
    high_ref[...] = both[half // 2 :]


def add_last(keep, got):
    rows, width = got.shape
    return pl.pallas_call(
        add_last_kernel,
        out_shape=[
            jax.ShapeDtypeStruct((count, width), BF16)
            for count in (rows // 2, rows // 2, rows // 4, rows // 4)
        ],
        compiler_params=pltpu.CompilerParams(vmem_limit_bytes=12 * 1024 * 1024),
        cost_estimate=cost(1),
        name="add_last",
    )(keep, got)


def join_kernel(first_ref, second_ref, out_ref):
    rows = first_ref.shape[0]
    out_ref[0:rows] = first_ref[...]
    out_ref[rows:] = second_ref[...]


def join_rows(first, second):
    rows, width = first.shape
    return pl.pallas_call(
        join_kernel,
        out_shape=jax.ShapeDtypeStruct((2 * rows, width), first.dtype),
        compiler_params=pltpu.CompilerParams(vmem_limit_bytes=8 * 1024 * 1024),
        cost_estimate=cost(1),
        name="join_rows",
    )(first, second)


def pack_kernel(order_ref, up_a, up_b, down_a, down_b, up_ref, down_ref, quarter_ref, rows_ref):
    up = (up_a[0].astype(F32) + up_b[0].astype(F32)).astype(BF16)
    down = (down_a[0].astype(F32) + down_b[0].astype(F32)).astype(BF16)
    up_ref[...] = up
    down_ref[...] = down
    step, steps = pl.program_id(0), pl.num_programs(0)
    some, width = up.shape
    rows_ref[pl.ds(pl.multiple_of(step * some, some), some)] = up
    for c in range(down.shape[0] // D):
        rows_ref[D : 2 * D, c * D : (c + 1) * D] = down[c * D : (c + 1) * D]

    @pl.when(step == steps - 1)
    def _():
        quarter = quarter_ref.shape[0]
        start = pl.multiple_of(order_ref[0] * quarter, quarter)
        quarter_ref[...] = rows_ref[pl.ds(start, quarter)]


def pack_weights(depth, order, core_up, residual_up, core_down, residual_down):
    width = residual_up.shape[2]
    arrays = [core_up, residual_up, core_down, residual_down]
    shapes = [(D, width), (width, D), (D // 2, width)]
    return pl.pallas_call(
        pack_kernel,
        grid=(1,),
        in_specs=[pl.BlockSpec(memory_space=pltpu.SMEM)]
        + [layer_of(array.shape, depth) for array in arrays],
        out_specs=[whole(shape) for shape in shapes],
        out_shape=[jax.ShapeDtypeStruct(shape, BF16) for shape in shapes],
        scratch_shapes=[pltpu.VMEM((2 * D, width), BF16)],
        compiler_params=pltpu.CompilerParams(vmem_limit_bytes=VMEM_BYTES),
        cost_estimate=cost(4),
        name="pack_weights",
    )(order, *arrays)


def unpack_kernel(order_ref, *refs):
    pieces, (own_up, own_down, up_ref, down_ref, rows_ref) = refs[:4], refs[4:]
    quarter = pieces[0].shape[0]
    for r, piece in enumerate(pieces):
        start = pl.multiple_of(jnp.bitwise_xor(order_ref[0], r) * quarter, quarter)
        rows_ref[pl.ds(start, quarter)] = piece[...]
    up_ref[0] = own_up[...]
    down_ref[0] = own_down[...]
    up_ref[1] = rows_ref[0:D]
    for c in range(down_ref.shape[1] // D):
        down_ref[1, c * D : (c + 1) * D] = rows_ref[D : 2 * D, c * D : (c + 1) * D]


def unpack_weights(order, pieces, own_up, own_down):
    width = pieces[0].shape[1]
    shapes = [(2, D, width), (2, width, D)]
    args = [*pieces, own_up, own_down]
    return pl.pallas_call(
        unpack_kernel,
        grid=(1,),
        in_specs=[pl.BlockSpec(memory_space=pltpu.SMEM)] + [whole(a.shape) for a in args],
        out_specs=[whole(shape) for shape in shapes],
        out_shape=[jax.ShapeDtypeStruct(shape, BF16) for shape in shapes],
        scratch_shapes=[pltpu.VMEM((2 * D, width), BF16)],
        compiler_params=pltpu.CompilerParams(vmem_limit_bytes=EXPERT_VMEM),
        cost_estimate=cost(3),
        name="unpack_weights",
    )(order, *args)


def expert_outputs_kernel(earlier, order_ref, *refs):
    pieces, refs = refs[:8], refs[8:]
    refs = refs[4 if earlier else 0 :]
    outs, (rows_ref,) = refs[:4], refs[4:]
    step = pl.program_id(0)
    quarter = pieces[0].shape[0]

    @pl.when(step == 0)
    def _():
        for kind in range(2):
            for r in range(4):
                rows_ref[kind, r * quarter : (r + 1) * quarter] = pieces[kind * 4 + r][...]

    half = pl.num_programs(0)
    for kind in range(2):
        for part in range(2):
            place = jnp.bitwise_xor(order_ref[0], step + part * half)
            if kind == 1:
                place = place // 8 * 8 + place // 2 % 2 * 4 + place // 4 % 2 * 2 + place % 2
            start = pl.multiple_of(place * BLOCK, BLOCK)
            block = rows_ref[kind, pl.ds(start, BLOCK)].astype(F32)
            out = outs[kind * 2 + part]
            if part == 0:
                out[0] = block
            else:
                for c in range(out.shape[1]):
                    out[0, c] = block[:, c * D : (c + 1) * D]


def expert_outputs(depth, order, residual, core, earlier):
    width = residual[0].shape[1]
    half = D // BLOCK
    count = width // D
    up = jax.ShapeDtypeStruct((LAYERS, D, width), F32)
    down = jax.ShapeDtypeStruct((LAYERS, count, D, D), F32)
    up_spec = pl.BlockSpec((1, BLOCK, width), lambda i: (depth, i, 0))
    down_spec = pl.BlockSpec((1, count, BLOCK, D), lambda i: (depth, 0, i, 0))
    pieces = residual + core
    earlier = list(earlier or [])
    return pl.pallas_call(
        partial(expert_outputs_kernel, bool(earlier)),
        grid=(half,),
        in_specs=[pl.BlockSpec(memory_space=pltpu.SMEM)]
        + [whole(p.shape) for p in pieces]
        + [pl.BlockSpec(memory_space=pl.ANY)] * len(earlier),
        out_specs=[up_spec, down_spec] * 2,
        out_shape=[up, down] * 2,
        scratch_shapes=[pltpu.VMEM((2, 2 * D, width), BF16)],
        input_output_aliases={9 + i: i for i in range(len(earlier))},
        compiler_params=pltpu.CompilerParams(vmem_limit_bytes=32 * 1024 * 1024),
        cost_estimate=cost(4),
        name="expert_outputs",
    )(order, *pieces, *earlier)


def attend_outputs_kernel(earlier, order_ref, *refs):
    pieces, refs = refs[:2], refs[2:]
    refs = refs[2 if earlier else 0 :]
    attend_ref, out_ref, rows_ref = refs
    half = pieces[0].shape[0]
    for r in range(2):
        rows_ref[r * half : (r + 1) * half] = pieces[r][...].astype(F32)
    for j in range(D // BLOCK):
        place = jnp.bitwise_xor(order_ref[0], j)
        place = place // 4 * 4 + place % 2 * 2 + place // 2 % 2
        block = rows_ref[pl.ds(pl.multiple_of(place * BLOCK, BLOCK), BLOCK)]
        attend_ref[0, j * BLOCK : (j + 1) * BLOCK] = block[:, : 3 * D]
        out_ref[0, j * BLOCK : (j + 1) * BLOCK] = block[:, 3 * D :]


def attend_outputs(depth, order, pieces, earlier):
    earlier = list(earlier or [])
    shapes = [(LAYERS, D, 3 * D), (LAYERS, D, D)]
    return pl.pallas_call(
        partial(attend_outputs_kernel, bool(earlier)),
        grid=(1,),
        in_specs=[pl.BlockSpec(memory_space=pltpu.SMEM)]
        + [whole(p.shape) for p in pieces]
        + [pl.BlockSpec(memory_space=pl.ANY)] * len(earlier),
        out_specs=[layer_of(shape, depth) for shape in shapes],
        out_shape=[jax.ShapeDtypeStruct(shape, F32) for shape in shapes],
        scratch_shapes=[pltpu.VMEM((D, 4 * D), F32)],
        input_output_aliases={3 + i: i for i in range(len(earlier))},
        compiler_params=pltpu.CompilerParams(vmem_limit_bytes=24 * 1024 * 1024),
        cost_estimate=cost(2),
        name="attend_outputs",
    )(order, *pieces, *earlier)


CORE, ROW = ("dp", 1), ("dp", 2)
NEAR_X, NEAR_Z, FAR_Z = ("expert", 1), ("expert", 2), ("expert", 4)


def place_order(steps):
    order = 0
    for step in steps:
        order = order * 2 + bit_at(step)
    return jnp.full((1,), order, jnp.int32)


class ExpertSum:
    def __init__(self, keep, send):
        self.keep, self.send = keep, send

    def core(self):
        rows = self.keep.shape[0] // 2
        cuts = ((0, rows), (rows, 2 * rows))
        self.keep, self.send = add_rows(self.keep, swap(self.send, CORE), cuts)
        return [self.keep, self.send]

    def row(self):
        self.own, self.partner, self.core_keep, self.core_send = add_last(
            self.keep, swap(self.send, ROW)
        )
        return [self.own, self.partner, self.core_keep, self.core_send]

    def join(self):
        rows = self.own.shape[0]
        (self.mine,) = add_rows(self.own, swap(self.partner, FAR_Z), ((0, rows),))
        return [self.mine]

    def residual_row(self):
        self.mine_row = swap(self.mine, ROW)
        return [self.mine_row]

    def residual_core(self):
        self.residual = [self.mine, self.mine_row, swap(self.mine, CORE), swap(self.mine_row, CORE)]
        return self.residual

    def near_x(self):
        rows = self.core_send.shape[0]
        cuts = ((0, rows // 2), (rows // 2, rows))
        got = swap(self.core_send, NEAR_X)
        self.core_keep, self.core_send = add_rows(self.core_keep, got, cuts)
        return [self.core_keep, self.core_send]

    def near_z(self):
        rows = self.core_send.shape[0]
        (self.total,) = add_rows(self.core_keep, swap(self.core_send, NEAR_Z), ((0, rows),))
        return [self.total]

    def far_z(self):
        rows = self.total.shape[0]
        (self.total,) = add_rows(self.total, swap(self.total, FAR_Z), ((0, rows),))
        return [self.total]

    def back_z(self):
        self.total = join_rows(self.total, swap(self.total, NEAR_Z))
        return [self.total]

    def back_row(self):
        self.total = join_rows(self.total, swap(self.total, ROW))
        return [self.total]

    def back_x(self):
        self.total_x = swap(self.total, NEAR_X)
        return [self.total_x]

    def back_core(self):
        self.whole = [self.total, self.total_x, swap(self.total, CORE), swap(self.total_x, CORE)]
        return self.whole

    def run(self, *steps):
        done = []
        for step in steps:
            done = done + getattr(self, step)()
        return done


class AttendSum:
    def __init__(self, keep, send):
        self.keep, self.send = keep, send
        self.steps = iter(
            [lambda step=step: self.halve(step) for step in (CORE, ROW, NEAR_X)]
            + [lambda step=step: self.add(step) for step in (NEAR_Z, FAR_Z)]
            + [lambda step=step: self.join(step) for step in (ROW, NEAR_X)]
            + [self.last]
        )

    def run(self, count):
        for _ in range(count):
            next(self.steps)()
        return self.done

    def halve(self, step):
        rows = self.send.shape[0]
        got = swap(self.send, step)
        if step == NEAR_X:
            (self.keep,) = add_rows(self.keep, got, ((0, rows),))
            self.done = [self.keep]
        else:
            cuts = ((0, rows // 2), (rows // 2, rows))
            self.keep, self.send = add_rows(self.keep, got, cuts)
            self.done = [self.keep, self.send]

    def add(self, step):
        (self.keep,) = add_rows(self.keep, swap(self.keep, step), ((0, self.keep.shape[0]),))
        self.done = [self.keep]

    def join(self, step):
        self.keep = join_rows(self.keep, swap(self.keep, step))
        self.done = [self.keep]

    def last(self):
        self.pieces = [self.keep, swap(self.keep, CORE)]
        self.done = self.pieces


def after(value, *done):
    return lax.optimization_barrier((value,) + done)[0]


def body(
    block_input,
    routes,
    first_gain,
    first_shift,
    attend_weight,
    bias_table,
    output_weight,
    second_gain,
    second_shift,
    router_weight,
    core_up,
    core_down,
    residual_up,
    residual_down,
    cotangent,
):
    groups = lax.axis_size("expert")
    slices = groups // EXPERTS
    group_part = lax.axis_index("expert") % slices
    images = block_input.shape[0]
    width = residual_up.shape[2]

    routes_rows = jnp.pad(
        routes.reshape(LAYERS, images, HW), ((0, 0), (0, 0), (0, TPAD - HW)), constant_values=-1
    )
    alone = slices == 1
    half = lax.axis_index("expert") // TEAM
    ups, downs, quarters = [], [], []
    dp_order = place_order((CORE, ROW)) if alone else None
    for d in range(LAYERS):
        if not alone:
            up = lax.dynamic_slice_in_dim(core_up[d], group_part * width, width, 1)
            down = lax.dynamic_slice_in_dim(core_down[d], group_part * width, width, 0)
            ups.append((up.astype(F32) + residual_up[d].astype(F32)).astype(BF16)[None])
            downs.append((down.astype(F32) + residual_down[d].astype(F32)).astype(BF16)[None])

    def pack(d, core_up):
        up, down, quarter = pack_weights(
            d, dp_order, core_up, residual_up, core_down, residual_down
        )
        ups.append(up)
        downs.append(down)
        quarters.append(quarter)

    if alone:
        pack(0, core_up)
        routes_rows, bias_table = after((routes_rows, bias_table), quarters[0])
    targets = run_routing(routes_rows, jnp.full((1,), half, jnp.int32), alone)

    table_index = jnp.asarray(offset_table(), jnp.int32)
    picker = (jnp.arange(OFFSETS, dtype=jnp.int32)[:, None] == table_index[None, :]).astype(F32)
    flat_table = bias_table.transpose(0, 2, 1).reshape(LAYERS * HEADS, OFFSETS)
    bias = jnp.dot(flat_table, picker, precision=lax.Precision.HIGHEST)
    bias = (
        bias.reshape(LAYERS, HEADS, LPAD, LPAD)
        .transpose(0, 2, 1, 3)
        .reshape(LAYERS, LPAD, HEADS * LPAD)
    )
    offsets = [SHIFT * (depth % 2) for depth in range(LAYERS)]
    shared = {
        "first_gain": first_gain,
        "first_shift": first_shift,
        "second_gain": second_gain,
        "second_shift": second_shift,
        "attend_weight": attend_weight,
        "output_weight": output_weight,
        "router": jnp.pad(router_weight, ((0, 0), (0, 0), (0, LANES - EXPERTS))),
        "bias": [bias[depth] for depth in range(LAYERS)],
        "mask": [jnp.asarray(score_mask(o)) for o in offsets],
        "perm": [jnp.asarray(permutation(o), BF16) for o in offsets],
        "perm_back": [jnp.asarray(permutation(o).T, BF16) for o in offsets],
    }
    route_rows = [routes_rows[d].reshape(images, 1, TPAD) for d in range(LAYERS)]
    target_rows = [targets[d].reshape(images, 1, TPAD) for d in range(LAYERS)]
    target_all = [targets[d].reshape(1, images * TPAD) for d in range(LAYERS)]
    picked_type = BF16 if slices == 1 else F32
    saved, inner, gates, xs, picks = [], [], [], [block_input], []
    x, earlier = block_input, None
    dy_arrived = None
    def in_parts(rows):
        return [rows[i : i + PART] for i in range(0, rows.shape[0], PART)]

    first = [swap(quarters[0], FAR_Z)] if alone else []
    for d in range(LAYERS):
        if alone:
            x = after(x, quarters[d])
        outs, outgoing = run_forward(
            d, x, earlier, cotangent, route_rows[d], target_rows[d], target_all[d], shared
        )
        qkv, a, mixed, mid, n, probs, gate = outs[:7]
        if d:
            xs.append(outs[7])
            picks.append(outs[8])
        if alone:
            outgoing = after(outgoing, first[d])
            second = swap(first[d], ROW)
            if d == 0:
                pack(1, after(core_up, outgoing))
        arrived = to_experts(outgoing, slices)
        if alone:
            if d == 0:
                first.append(swap(after(quarters[1], second), FAR_Z))
            pieces = [first[d], second, swap(first[d], CORE), swap(second, CORE)]
            ups[d], downs[d] = unpack_weights(dp_order, pieces, ups[d], downs[d])
        if d < LAYERS - 1:
            y = run_expert_forward(arrived, ups[d], downs[d])
            back = from_experts(y, slices)
            earlier = (back, gate, target_rows[d], picked_type)
        x = mid
        gates.append(gate)
        saved.append([xs[d], qkv, a, mixed, mid, n, probs, gate])
        inner.append(arrived)

    grad = cotangent
    vecs, tables = [None] * 2, [None] * 2
    block_output = None
    expert_order = place_order((CORE, ROW, NEAR_X, NEAR_Z)) if alone else None
    attend_order = place_order((CORE, ROW, NEAR_X)) if alone else None
    expert_sums, attend_sums = [None] * 2, [None] * 2
    dy_arrived = None
    for d in reversed(range(LAYERS)):
        arrived = inner[d]
        if alone and d == 0:
            dy_arrived = after(dy_arrived, *attend_sums[1].run(1))
        rows_out, hidden, du = run_expert_both(arrived, dy_arrived, ups[d], downs[d])
        if alone and d == 0:
            rows_out = after(
                rows_out, *expert_sums[1].run("join", "near_x"), *attend_sums[1].run(1)
            )
        back = from_experts(rows_out, slices)
        grads = run_expert_weights(arrived, dy_arrived, hidden, du, expert_order)
        if alone:
            expert_sums[d] = ExpertSum(*grads)
            done = expert_sums[d].run("core")
            if d == 0:
                done = done + expert_sums[1].run("residual_row", "near_z", "far_z")
            grad = after(grad, *done)
        else:
            expert_sums[d] = grads
        if d == LAYERS - 1:
            extra = (gates[d - 1], target_all[d - 1])
        else:
            extra = picks[d]
        outs = run_backward(
            d,
            grad,
            back,
            extra,
            saved[d],
            route_rows[d],
            target_rows[d],
            shared,
            attend_order,
        )
        if alone:
            grad, keep, send, vecs[d], tables[d] = outs[:5]
            attend_sums[d] = AttendSum(keep, send)
            outs = outs[5:]
        else:
            grad, attend_sums[d], vecs[d], tables[d] = outs[:4]
            outs = outs[4:]
        if d == LAYERS - 1:
            block_output, dy_out = outs
            if alone:
                dy_out = after(dy_out, *expert_sums[1].run("row"))
            dy_arrived = to_experts(dy_out, slices)
    input_grad = grad

    dp_steps = bits_of("dp", 1, lax.axis_size("dp"))
    slice_steps = bits_of("expert", 1, slices)
    sum_steps = bits_of("expert", slices, groups)
    all_steps = dp_steps + slice_steps + sum_steps
    if alone:
        experts, full = None, None
        for d in reversed(range(LAYERS)):
            sums, attend = expert_sums[d], attend_sums[d]
            if d:
                sums.run("residual_core")
            else:
                sums.run("row", "join", "near_x", "near_z", "far_z")
                sums.run("residual_row", "residual_core")
            sums.run("back_z", "back_row", "back_x", "back_core")
            attend.run(6 if d else 8)
            experts = expert_outputs(d, expert_order, sums.residual, sums.whole, experts)
            full = attend_outputs(d, attend_order, attend.pieces, full)
        residual_up_grad, residual_down_grad, core_up_grad, core_down_grad = experts
        residual_down_grad = residual_down_grad.reshape(LAYERS, width, D)
        core_down_grad = core_down_grad.reshape(LAYERS, width, D)
        attend_weight_grad, output_weight_grad = full
    else:
        residual, core, full = [], [], []
        for d in range(LAYERS):
            part = scatter_sum(expert_sums[d], dp_steps)
            residual.append(gather_all(part, dp_steps))
            total = gather_all(sum_over(part, sum_steps), dp_steps)
            core.append(gather_all(total, slice_steps, dim=1))
            full.append(sum_over(attend_sums[d], all_steps))
        full = jnp.stack(full).astype(F32)
        attend_weight_grad, output_weight_grad = full[:, :, : 3 * D], full[:, :, 3 * D :]
        residual_up_grad = jnp.stack([r[:D] for r in residual]).astype(F32)
        residual_down_grad = jnp.stack([unpack_down(r[D:]) for r in residual]).astype(F32)
        core_up_grad = jnp.stack([c[:D] for c in core]).astype(F32)
        core_down_grad = jnp.stack([unpack_down(c[D:]) for c in core]).astype(F32)
    table_grad = jnp.stack(tables).reshape(LAYERS, LPAD, HEADS, LPAD).transpose(0, 2, 1, 3)
    table_grad = jnp.dot(
        table_grad.reshape(LAYERS * HEADS, LPAD * LPAD), picker.T, precision=lax.Precision.HIGHEST
    )
    small = jnp.concatenate(
        [
            jnp.stack(vecs).reshape(LAYERS * 16, D),
            jnp.pad(table_grad, ((0, 0), (0, D - OFFSETS))),
        ],
        axis=0,
    )
    small = sum_all(small, all_steps)
    vec = small[: LAYERS * 16].reshape(LAYERS, 16, D)
    table = small[LAYERS * 16 :, :OFFSETS].reshape(LAYERS, HEADS, OFFSETS).transpose(0, 2, 1)
    return (
        block_output,
        input_grad,
        vec[:, 0],
        vec[:, 1],
        attend_weight_grad,
        table,
        output_weight_grad,
        vec[:, 2],
        vec[:, 3],
        vec[:, 8:16].transpose(0, 2, 1),
        core_up_grad,
        core_down_grad,
        residual_up_grad,
        residual_down_grad,
    )


def solution(mesh):
    placed = (
        P(("dp", "expert"), None, None),
        P(None, ("dp", "expert"), None, None),
        P(),
        P(),
        P(),
        P(),
        P(),
        P(),
        P(),
        P(),
        P(),
        P(),
        P(None, None, "expert"),
        P(None, "expert", None),
        P(("dp", "expert"), None, None),
    )
    return jax.shard_map(
        body,
        mesh=mesh,
        in_specs=placed,
        out_specs=(
            P(("dp", "expert"), None, None),
            P(("dp", "expert"), None, None),
            P(),
            P(),
            P(),
            P(),
            P(),
            P(),
            P(),
            P(),
            P(),
            P(),
            P(None, None, "expert"),
            P(None, "expert", None),
        ),
        check_vma=False,
    )
```

```python
from functools import partial

import jax
import jax.numpy as jnp
import numpy as np
from jax import lax
from jax.experimental import pallas as pl
from jax.experimental.pallas import tpu as pltpu
from jax.sharding import PartitionSpec as P

D = 384
HEADS = 12
HD = 32
FF = 1536
EXPERTS = 8
WIN = 7
SIDE = 14
SHIFT = 3
LAYERS = 2
HW = 196
CAP = 184
OFFSETS = 169
ROWS = 192
SLOTS = EXPERTS * ROWS

WINDOWS = (SIDE // WIN) * (SIDE // WIN)
LENGTH = WIN * WIN
LPAD = 64
WROWS = WINDOWS * LPAD
TPAD = 256
LANES = 128
GROUP = LANES // HD
GROUPS = HEADS // GROUP
GW = GROUP * LPAD
FCHUNK = 384
SOURCES = 2
FTILE = 512
EXPERT_VMEM = 32 * 1024 * 1024
BLOCK = 48
PAIRS_AT_ONCE = 2
TEAM = 4
BACKWARD_CALLS = 1
STEP_IMAGES = 3

F32 = jnp.float32
BF16 = jnp.bfloat16
eps_norm = 1e-05
mask_fill = -100.0
pad_fill = -1e30
score_scale = HD ** (-0.5)
VMEM_BYTES = 56 * 1024 * 1024

NN = (((1,), (0,)), ((), ()))
NT = (((1,), (1,)), ((), ()))
TN = (((0,), (0,)), ((), ()))


def mm(a, b, dims=NN):
    return lax.dot_general(a, b, dims, preferred_element_type=F32)


def window_tokens(offset):
    rows = np.full((WINDOWS, LPAD), -1, np.int64)
    per_side = SIDE // WIN
    for w in range(WINDOWS):
        for i in range(LENGTH):
            r = (w // per_side) * WIN + i // WIN
            c = (w % per_side) * WIN + i % WIN
            rows[w, i] = ((r + offset) % SIDE) * SIDE + (c + offset) % SIDE
    return rows.reshape(-1)


def permutation(offset):
    rows = window_tokens(offset)
    return (rows[:, None] == np.arange(HW)[None, :]).astype(np.float32)


def score_mask(offset):
    coords = np.arange(SIDE)
    bands = (coords >= SIDE - WIN).astype(int) + (coords >= SIDE - offset).astype(int)
    labels = bands[:, None] * 3 + bands[None, :]
    per_side = SIDE // WIN
    out = np.zeros((WINDOWS, LPAD, LPAD), np.float32)
    for w in range(WINDOWS):
        r0, c0 = (w // per_side) * WIN, (w % per_side) * WIN
        flat = labels[r0 : r0 + WIN, c0 : c0 + WIN].reshape(-1)
        out[w, :LENGTH, :LENGTH] = np.where(flat[:, None] == flat[None, :], 0.0, mask_fill)
        out[w, LENGTH:, :] = pad_fill
    return np.tile(out, (1, 1, GROUP))


def offset_table():
    i = np.arange(LENGTH)
    r, c = i // WIN, i % WIN
    index = np.full((LPAD, LPAD), -1, np.int64)
    index[:LENGTH, :LENGTH] = (
        (r[None, :] - r[:, None] + WIN - 1) * (2 * WIN - 1) + c[None, :] - c[:, None] + WIN - 1
    )
    return index.reshape(-1)


def norm_parts(x):
    centred = x - jnp.mean(x, axis=-1, keepdims=True)
    inverse = lax.rsqrt(jnp.mean(centred * centred, axis=-1, keepdims=True) + eps_norm)
    return centred * inverse, inverse


def norm_back(grad, unit, inverse, gain):
    scaled = grad * gain
    return inverse * (
        scaled
        - jnp.mean(scaled, axis=-1, keepdims=True)
        - unit * jnp.mean(scaled * unit, axis=-1, keepdims=True)
    )


def one_hot(cond):
    return jnp.where(cond, 1.0, 0.0).astype(BF16)


def head_masks():
    lane = lax.broadcasted_iota(jnp.int32, (1, LANES), 1) // HD
    return [jnp.where(lane == h, 1.0, 0.0) for h in range(GROUP)]


def spread_heads(block, masks):
    return jnp.concatenate([block * m.astype(BF16) for m in masks], axis=0)


def fold_heads(tall, masks):
    total = tall[0:LPAD] * masks[0]
    for h in range(1, GROUP):
        total = total + tall[h * LPAD : (h + 1) * LPAD] * masks[h]
    return total


def as_column(row, count):
    wide = jnp.broadcast_to(row.astype(F32), (8, TPAD))
    return wide.T[:count, 0:1].astype(jnp.int32)


def pick_rows(target_row, *arrays):
    column = as_column(target_row, HW)
    place = one_hot(lax.broadcasted_iota(jnp.int32, (HW, SLOTS), 1) == column)
    picked = []
    for rows_ref in arrays:
        total = mm(place, rows_ref[0])
        for k in range(1, rows_ref.shape[0]):
            total = total + mm(place, rows_ref[k])
        picked.append(total)
    return picked


def send_rows(out_refs, target_all, rows):
    step = SLOTS // 4
    for c in range(4):
        slot = lax.broadcasted_iota(jnp.int32, (step, rows.shape[0]), 0) + c * step
        block = mm(one_hot(slot == target_all), rows).astype(BF16)
        for at, ref in enumerate(out_refs):
            ref[c * step : (c + 1) * step] = block[:, at * D : (at + 1) * D]


def gelu_parts(u):
    cdf = 0.5 + 0.5 * lax.erf(u * (0.5**0.5))
    bell = jnp.exp(-0.5 * u * u)
    return u * cdf, cdf + u * (bell * 0.3989422804014327)


def in_hbm(shape, dtype):
    return pltpu.HBM(tuple(shape), dtype)


def from_hbm(array):
    return pltpu.with_memory_space_constraint(array, pltpu.HBM)


def cost(microseconds):
    return pl.CostEstimate(
        flops=int(microseconds * 9e8), bytes_accessed=1000, transcendentals=0
    )


def routing_kernel(paired, half_ref, routes_ref, target_ref):
    before = one_hot(
        lax.broadcasted_iota(jnp.int32, (TPAD, TPAD), 0)
        <= lax.broadcasted_iota(jnp.int32, (TPAD, TPAD), 1)
    )
    expert = lax.broadcasted_iota(jnp.int32, (16, TPAD), 0)
    for depth in range(LAYERS):
        carry = jnp.zeros((16, 1), F32)
        for i in range(routes_ref.shape[1]):
            row = routes_ref[depth, i : i + 1, :]
            chosen = jnp.where(expert == row, 1.0, 0.0)
            counts = mm(chosen.astype(BF16), before) + carry
            carry = counts[:, TPAD - 1 : TPAD]
            slot = jnp.sum(chosen * counts, axis=0, keepdims=True).astype(jnp.int32) - 1
            kept = (slot >= 0) & (slot < CAP)
            place = row
            if paired[depth]:
                place = (row % TEAM) * 2 + jnp.bitwise_xor(row // TEAM, half_ref[0])
            target_ref[depth, i : i + 1, :] = jnp.where(kept, place * ROWS + slot, -1)


def run_routing(routes, half, paired):
    return pl.pallas_call(
        partial(routing_kernel, paired),
        in_specs=[
            pl.BlockSpec(memory_space=pltpu.SMEM),
            pl.BlockSpec(memory_space=pltpu.VMEM),
        ],
        out_shape=jax.ShapeDtypeStruct(routes.shape, jnp.int32),
        name="routing",
    )(half, routes)


def group_cols(part, g):
    return slice(part * D + g * LANES, part * D + (g + 1) * LANES)


def softmax_down(scores):
    raised = jnp.exp(scores - jnp.max(scores, axis=0, keepdims=True))
    return raised * (1.0 / jnp.sum(raised, axis=0, keepdims=True))


def window_items(some):
    pairs = [(w, g) for w in range(WINDOWS) for g in range(GROUPS)]
    runs = []
    for first in range(0, len(pairs), PAIRS_AT_ONCE):
        runs.append([(w, g, b) for w, g in pairs[first : first + PAIRS_AT_ONCE] for b in some])
    return runs


def raw_scores(qkv_ref, items, masks):
    wide, scores = [], []
    for w, g, b in items:
        rows = slice(w * LPAD, (w + 1) * LPAD)
        wide.append(spread_heads(qkv_ref[b, rows, group_cols(0, g)], masks))
    for (w, g, b), q_wide in zip(items, wide):
        rows = slice(w * LPAD, (w + 1) * LPAD)
        scores.append(mm(qkv_ref[b, rows, group_cols(1, g)], q_wide, NT))
    return wide, scores


def to_probs(items, scores, bias_ref, mask_ref):
    probs = []
    for (w, g, b), score in zip(items, scores):
        probs.append(
            softmax_down(
                score * score_scale + bias_ref[:, g * GW : (g + 1) * GW] + mask_ref[w]
            )
        )
    return probs


def forward_kernel(depth, images, *refs):
    last = depth == LAYERS - 1
    refs = list(refs)
    take = lambda: refs.pop(0)
    x_ref = take()
    if depth:
        back_ref, gate_in_ref, target_in_ref = take(), take(), take()
    if last:
        cot_ref = take()
    (route_ref, target_ref, g1_ref, s1_ref, g2_ref, s2_ref, attend_ref, out_w_ref) = refs[:8]
    (router_ref, bias_ref, mask_ref, perm_ref, perm_back_ref) = refs[8:13]
    refs = refs[13:]
    (qkv_ref, a_ref, mixed_ref, mid_ref, n_ref, probs_ref, gate_ref) = refs[:7]
    refs = refs[7:]
    if depth:
        x_out_ref, picked_ref = take(), take()
    out_refs = [take() for _ in range(2 if last else 1)]
    rows_ref = take()

    step = pl.program_id(0)

    @pl.when(step == 0)
    def _():
        rows_ref[...] = jnp.zeros_like(rows_ref)

    some = range(x_ref.shape[0])
    xs = []
    for b in some:
        x = x_ref[b].astype(F32)
        if depth:
            (picked,) = pick_rows(target_in_ref[b], back_ref)
            picked_ref[b] = picked.astype(picked_ref.dtype)
            x = x + gate_in_ref[b][:, 0:1] * picked
            x_out_ref[b] = x
        xs.append(x)
    for b in some:
        unit, _ = norm_parts(xs[b])
        normed = (unit * g1_ref[depth : depth + 1] + s1_ref[depth : depth + 1]).astype(BF16)
        a_ref[b] = mm(perm_ref[...], normed).astype(BF16)
    qkv = mm(a_ref[...].reshape(len(some) * WROWS, D), attend_ref[0]).astype(BF16)
    qkv_ref[...] = qkv.reshape(len(some), WROWS, 3 * D)
    masks = head_masks()
    runs = window_items(some)
    ready = raw_scores(qkv_ref, runs[0], masks)
    for at, items in enumerate(runs):
        _, scores = ready
        if at + 1 < len(runs):
            ready = raw_scores(qkv_ref, runs[at + 1], masks)
        probs = to_probs(items, scores, bias_ref, mask_ref)
        tall = []
        for (w, g, b), p in zip(items, probs):
            rows = slice(w * LPAD, (w + 1) * LPAD)
            tall.append(mm(p.astype(BF16), qkv_ref[b, rows, group_cols(2, g)], TN))
        for (w, g, b), t in zip(items, tall):
            rows = slice(w * LPAD, (w + 1) * LPAD)
            mixed_ref[b, rows, group_cols(0, g)] = fold_heads(t, masks).astype(BF16)
    lane = lax.broadcasted_iota(jnp.int32, (HW, LANES), 1)
    for b in some:
        mixed = mm(perm_back_ref[...], mixed_ref[b]).astype(BF16)
        mid = xs[b] + mm(mixed, out_w_ref[0])
        mid_ref[b] = mid
        unit, _ = norm_parts(mid)
        n = (unit * g2_ref[depth : depth + 1] + s2_ref[depth : depth + 1]).astype(BF16)
        n_ref[b] = n
        logits = jnp.where(lane < EXPERTS, mm(n, router_ref[0]), pad_fill)
        raised = jnp.exp(logits - jnp.max(logits, axis=-1, keepdims=True))
        router = raised / jnp.sum(raised, axis=-1, keepdims=True)
        probs_ref[b] = router
        chosen = lane == as_column(route_ref[b], HW)
        gate = jnp.sum(jnp.where(chosen, router, 0.0), axis=-1, keepdims=True)
        gate_ref[b] = jnp.broadcast_to(gate, (HW, LANES))
        at = step * len(some) + b
        rows_ref[pl.ds(at, 1), 0:HW, 0:D] = n[None]
        if last:
            dy = (gate * cot_ref[b].astype(F32)).astype(BF16)
            rows_ref[pl.ds(at, 1), 0:HW, D : 2 * D] = dy[None]

    @pl.when(step == pl.num_programs(0) - 1)
    def _():
        rows = rows_ref[...].reshape(images * TPAD, rows_ref.shape[2])
        send_rows(out_refs, target_ref[...], rows)


def whole(shape):
    return pl.BlockSpec(shape, lambda i: (0,) * len(shape))


def images_of(images):
    return STEP_IMAGES if images % STEP_IMAGES == 0 else 1


def by_image(shape):
    return pl.BlockSpec(
        (images_of(shape[0]),) + shape[1:], lambda i: (i,) + (0,) * (len(shape) - 1)
    )


def layer_of(shape, depth):
    return pl.BlockSpec((1,) + shape[1:], lambda i: (depth,) + (0,) * (len(shape) - 1))


def run_forward(depth, x, earlier, cotangent, route_rows, target_rows, target_all, shared):
    images = x.shape[0]
    last = depth == LAYERS - 1
    args, specs = [x], [by_image(x.shape)]
    if depth:
        back, gate_in, target_in, picked_type = earlier
        args += [back, gate_in, target_in]
        specs += [whole(back.shape), by_image(gate_in.shape), by_image(target_in.shape)]
    if last:
        args.append(cotangent)
        specs.append(by_image(cotangent.shape))
    args += [route_rows, target_all]
    specs += [by_image(route_rows.shape), whole(target_all.shape)]
    for name in ("first_gain", "first_shift", "second_gain", "second_shift"):
        args.append(shared[name])
        specs.append(whole(shared[name].shape))
    for name in ("attend_weight", "output_weight", "router"):
        args.append(shared[name])
        specs.append(layer_of(shared[name].shape, depth))
    for name in ("bias", "mask", "perm", "perm_back"):
        args.append(shared[name][depth])
        specs.append(whole(shared[name][depth].shape))
    outs = [
        ((images, WROWS, 3 * D), BF16),
        ((images, WROWS, D), BF16),
        ((images, WROWS, D), BF16),
        ((images, HW, D), F32),
        ((images, HW, D), BF16),
        ((images, HW, LANES), F32),
        ((images, HW, LANES), F32),
    ]
    out_specs = [by_image(s) for s, _ in outs]
    if depth:
        outs += [((images, HW, D), F32), ((images, HW, D), picked_type)]
        out_specs += [by_image((images, HW, D))] * 2
    count = 2 if last else 1
    sent = count * D
    outs += [((SLOTS, D), BF16)] * count
    out_specs += [whole((SLOTS, D))] * count
    scratch = [pltpu.VMEM((images, TPAD, sent), BF16)]
    results = pl.pallas_call(
        partial(forward_kernel, depth, images),
        grid=(images // images_of(images),),
        in_specs=specs,
        out_specs=out_specs,
        out_shape=[in_hbm(s, t) for s, t in outs[:-count]]
        + [jax.ShapeDtypeStruct(s, t) for s, t in outs[-count:]],
        scratch_shapes=scratch,
        compiler_params=pltpu.CompilerParams(vmem_limit_bytes=VMEM_BYTES),
        cost_estimate=cost(24 if last else 18),
        name="forward_%d" % depth,
    )(*args)
    return results[:-count], results[-count:]


def joined(ref, columns=slice(None)):
    return jnp.concatenate([ref[s, 0, :, columns] for s in range(ref.shape[0])], axis=0)


def spread(ref, value, columns=slice(None)):
    for s in range(ref.shape[0]):
        ref[s, 0, :, columns] = value[s * ROWS : (s + 1) * ROWS]


def hidden_tiles(width):
    tile = FTILE if width % FTILE == 0 else FCHUNK
    return [slice(f, f + tile) for f in range(0, width, tile)]


def expert_forward_kernel(aliased, n_ref, up_ref, down_ref, *refs):
    y_ref, hidden_ref = refs[aliased:]
    n = joined(n_ref)
    tiles = hidden_tiles(up_ref.shape[2])
    ready = mm(n, up_ref[0, :, tiles[0]])
    for at, tile in enumerate(tiles):
        u = ready
        if at + 1 < len(tiles):
            ready = mm(n, up_ref[0, :, tiles[at + 1]])
        hidden_ref[:, tile] = gelu_parts(u)[0].astype(BF16)
    spread(y_ref, mm(hidden_ref[...], down_ref[0]).astype(BF16))


def by_expert(shape):
    return pl.BlockSpec((1,) + shape[1:], lambda k, i: (k,) + (0,) * (len(shape) - 1))


def by_sources(array, first=0):
    return pl.BlockSpec((SOURCES, 1) + array.shape[2:], lambda k, i: (i, first + k, 0, 0))


def run_expert_forward(arrived, up, down, which=None, earlier=None):
    total, width = up.shape[0], up.shape[2]
    first = which or 0
    weight_spec = lambda shape: pl.BlockSpec(
        (1,) + shape[1:], lambda k, i: ((first if total > 1 else 0) + k, 0, 0)
    )
    args = [arrived, from_hbm(up), from_hbm(down)]
    specs = [by_sources(arrived, first), weight_spec(up.shape), weight_spec(down.shape)]
    aliases = {}
    if earlier is not None:
        args.append(earlier)
        specs.append(pl.BlockSpec(memory_space=pl.ANY))
        aliases = {3: 0}
    steps = total if which is None else 1
    return pl.pallas_call(
        partial(expert_forward_kernel, len(aliases)),
        grid=(steps, arrived.shape[0] // SOURCES),
        in_specs=specs,
        out_specs=by_sources(arrived, first),
        out_shape=jax.ShapeDtypeStruct(arrived.shape, BF16),
        scratch_shapes=[pltpu.VMEM((SOURCES * ROWS, width), BF16)],
        input_output_aliases=aliases,
        compiler_params=pltpu.CompilerParams(vmem_limit_bytes=EXPERT_VMEM),
        cost_estimate=cost(4 * steps),
        name="expert_forward",
    )(*args)


def expert_both_kernel(n_ref, dy_ref, up_ref, down_ref, dn_ref, hidden_ref, du_ref):
    n, dy = joined(n_ref), joined(dy_ref)
    tiles = hidden_tiles(up_ref.shape[2])

    def first(tile):
        return mm(n, up_ref[0, :, tile]), mm(dy, down_ref[0, tile], NT)

    ready = first(tiles[0])
    for at, tile in enumerate(tiles):
        u, dh = ready
        if at + 1 < len(tiles):
            ready = first(tiles[at + 1])
        value, slope = gelu_parts(u)
        hidden_ref[0, :, tile] = value.astype(BF16)
        du_ref[0, :, tile] = (dh * slope).astype(BF16)
    spread(dn_ref, mm(du_ref[0], up_ref[0], NT).astype(BF16))


def run_expert_both(n, dy, up, down):
    total, width = up.shape[0], up.shape[2]
    wide = in_hbm((total, n.shape[0] * ROWS, width), BF16)
    wide_spec = pl.BlockSpec((1, SOURCES * ROWS, width), lambda k, i: (k, i, 0))
    return pl.pallas_call(
        expert_both_kernel,
        grid=(total, n.shape[0] // SOURCES),
        in_specs=[by_sources(n), by_sources(dy), by_expert(up.shape), by_expert(down.shape)],
        out_specs=[by_sources(n), wide_spec, wide_spec],
        out_shape=[jax.ShapeDtypeStruct(n.shape, BF16), wide, wide],
        compiler_params=pltpu.CompilerParams(vmem_limit_bytes=EXPERT_VMEM),
        cost_estimate=cost(6 * total),
        name="expert_both",
    )(n, dy, from_hbm(up), from_hbm(down))


def expert_weights_kernel(order, *refs):
    if order:
        order_ref, refs = refs[0], refs[1:]
    n_ref, dy_ref, hidden_ref, du_ref, refs = *refs[:4], refs[4:]
    if order:
        keep_ref, send_ref, refs = refs[0], refs[1], refs[2:]
    else:
        out_ref, refs = refs[0], refs[1:]
    n_rows, dy_rows, sum_ref = refs
    k = pl.program_id(1)

    @pl.when(pl.program_id(0) == 0)
    def _():
        for s in range(n_ref.shape[0]):
            rows = slice(s * ROWS, (s + 1) * ROWS)
            n_rows[k, rows] = n_ref[s, k]
            dy_rows[k, rows] = dy_ref[s, k]

    up = mm(n_rows[k], du_ref[0], TN)
    down = mm(hidden_ref[0], dy_rows[k], TN)
    sum_ref[0:D] = up
    sum_ref[D : 2 * D] = down
    if order:
        spread_experts(order_ref, sum_ref, keep_ref, send_ref)
    else:
        out_ref[0] = sum_ref[...].astype(BF16)


def spread_experts(order_ref, sum_ref, keep_ref, send_ref):
    run = sum_ref.shape[0] // BLOCK // 4
    for j in range(4 * run):
        start = pl.multiple_of(jnp.bitwise_xor(order_ref[0], j) * BLOCK, BLOCK)
        block = sum_ref[pl.ds(start, BLOCK)].astype(BF16)
        ref = keep_ref if j < 2 * run else send_ref
        at = j % run * BLOCK
        ref[j // run % 2, 0, at : at + BLOCK] = block


def spread_blocks(order_ref, sum_ref, keep_ref, send_ref, columns):
    count = sum_ref.shape[0] // BLOCK
    for j in range(count):
        start = pl.multiple_of(jnp.bitwise_xor(order_ref[0], j) * BLOCK, BLOCK)
        block = sum_ref[pl.ds(start, BLOCK)].astype(BF16)
        ref = keep_ref if j < count // 2 else send_ref
        at = (j % (count // 2)) * BLOCK
        ref[at : at + BLOCK, columns] = block


def run_expert_weights(n, dy, hidden, du, order=None):
    total, rows, width = hidden.shape
    specs = [
        pl.BlockSpec(array.shape, lambda f, k: (0, 0, 0, 0), pipeline_mode=pl.Buffered(1))
        for array in (n, dy)
    ]
    if order is None:
        shape = [jax.ShapeDtypeStruct((total, 2 * D, width), BF16)]
        out_specs = [pl.BlockSpec((1, 2 * D, FCHUNK), lambda f, k: (k, 0, f))]
        leading = []
    else:
        shape = [jax.ShapeDtypeStruct((2, total, D // 2, width), BF16)] * 2
        out_specs = [pl.BlockSpec((2, 1, D // 2, FCHUNK), lambda f, k: (0, k, 0, f))] * 2
        leading = [order]
    wide_spec = pl.BlockSpec((1, rows, FCHUNK), lambda f, k: (k, 0, f))
    results = pl.pallas_call(
        partial(expert_weights_kernel, order is not None),
        grid=(width // FCHUNK, total),
        in_specs=[pl.BlockSpec(memory_space=pltpu.SMEM)] * len(leading)
        + specs
        + [wide_spec] * 2,
        out_specs=out_specs,
        out_shape=shape,
        scratch_shapes=[pltpu.VMEM((total, rows, D), BF16)] * 2
        + [pltpu.VMEM((2 * D, FCHUNK), F32)],
        compiler_params=pltpu.CompilerParams(vmem_limit_bytes=EXPERT_VMEM + 8 * 1024 * 1024),
        cost_estimate=cost(4 * total),
        name="expert_weights",
    )(*leading, n, dy, from_hbm(hidden), from_hbm(du))
    if order is None:
        return results[0][0]
    return [r.reshape(total * D, width) for r in results]


def backward_kernel(depth, images, order, part, parts, *refs):
    last = depth == LAYERS - 1
    refs = list(refs)
    take = lambda: refs.pop(0)
    if order:
        order_ref = take()
    g_ref, back_ref = take(), take()
    if last:
        y_ref = take()
        before_gate_ref, before_target_ref = take(), take()
    else:
        picked_ref = take()
    (x_ref, qkv_ref, a_ref, mixed_ref, mid_ref, n_ref, probs_ref, gate_ref) = refs[:8]
    (route_ref, target_ref, g1_ref, g2_ref, attend_ref, out_w_ref) = refs[8:14]
    (router_ref, bias_ref, mask_ref, perm_ref, perm_back_ref) = refs[14:19]
    refs = refs[19:]
    earlier = {}
    if part:
        earlier["mats"] = [take() for _ in range(2 if order else 1)]
        earlier["sums"] = [take(), take()]
        if last:
            earlier["dy"] = [take() for _ in range(part)]
        take()
        if last:
            take()
    g_out_ref = take()
    mats_refs = [take() for _ in range(2 if order else 1)]
    vecs_ref, table_ref = take(), take()
    if last:
        result_ref, dy_out_ref = take(), take()
    attend_acc, out_acc, dqkv_ref, dz_ref = (take() for _ in range(4))
    if last:
        dy_rows_ref = take()

    step = pl.program_id(0)

    @pl.when(step == 0)
    def _():
        attend_acc[...] = jnp.zeros_like(attend_acc)
        out_acc[...] = jnp.zeros_like(out_acc)
        if part:
            vecs_ref[...] = earlier["sums"][0][...]
            table_ref[...] = earlier["sums"][1][...]
        else:
            vecs_ref[...] = jnp.zeros_like(vecs_ref)
            table_ref[...] = jnp.zeros_like(table_ref)
        if last:
            dy_rows_ref[...] = jnp.zeros_like(dy_rows_ref)

    some = range(g_ref.shape[0])
    lane = lax.broadcasted_iota(jnp.int32, (HW, LANES), 1)
    grad_mids, dmixed_all = [], []
    for b in some:
        grad = g_ref[b].astype(F32)
        mid = mid_ref[b]
        gate = gate_ref[b][:, 0:1]
        if last:
            rows_back, picked = pick_rows(target_ref[b], back_ref, y_ref)
            result_ref[b] = (mid + gate * picked).astype(BF16)
        else:
            (rows_back,) = pick_rows(target_ref[b], back_ref)
            picked = picked_ref[b].astype(F32)
        gate_grad = jnp.sum(grad * picked, axis=-1, keepdims=True)
        chosen = jnp.where(lane == as_column(route_ref[b], HW), 1.0, 0.0)
        logit_grad = ((gate * gate_grad) * (chosen - probs_ref[b])).astype(BF16)
        router_grad = mm(logit_grad, n_ref[b], TN)
        grad_n = rows_back + mm(logit_grad, router_ref[0], NT)
        unit, inverse = norm_parts(mid)
        vecs_ref[2:3] += jnp.sum(grad_n * unit, axis=0, keepdims=True)
        vecs_ref[3:4] += jnp.sum(grad_n, axis=0, keepdims=True)
        vecs_ref[8:16] += router_grad[0:8]
        grad_mid = grad + norm_back(grad_n, unit, inverse, g2_ref[depth : depth + 1])
        grad_mids.append(grad_mid)
        dz = mm(perm_ref[...], grad_mid.astype(BF16)).astype(BF16)
        dz_ref[b] = dz
    dz = dz_ref[...].reshape(len(some) * WROWS, D)
    out_acc[...] += mm(mixed_ref[...].reshape(len(some) * WROWS, D), dz, TN)
    dmixed_all = mm(dz, out_w_ref[0], NT).astype(BF16)
    masks = head_masks()
    def first_part(items):
        dm_wide, dprobs = [], []
        for w, g, b in items:
            start = b * WROWS + w * LPAD
            dm_wide.append(
                spread_heads(dmixed_all[start : start + LPAD, group_cols(0, g)], masks)
            )
        for (w, g, b), dm in zip(items, dm_wide):
            rows = slice(w * LPAD, (w + 1) * LPAD)
            dprobs.append(mm(qkv_ref[b, rows, group_cols(2, g)], dm, NT))
        return raw_scores(qkv_ref, items, masks) + (dm_wide, dprobs)

    runs = window_items(some)
    ready = first_part(runs[0])
    for at, items in enumerate(runs):
        places = [(b, slice(w * LPAD, (w + 1) * LPAD), g) for w, g, b in items]
        q_wide, scores, dm_wide, dprobs = ready
        if at + 1 < len(runs):
            ready = first_part(runs[at + 1])
        probs = to_probs(items, scores, bias_ref, mask_ref)
        dscores, tables = [], {}
        for (b, rows, g), p, dp in zip(places, probs, dprobs):
            row_dot = jnp.sum(p * dp, axis=0, keepdims=True)
            dscores.append((p * (dp - row_dot)).astype(BF16))
            wide = dscores[-1].astype(F32)
            tables[g] = tables[g] + wide if g in tables else wide
        for g, total in tables.items():
            table_ref[:, g * GW : (g + 1) * GW] += total
        dv, dk, tall = [], [], []
        for p, dm in zip(probs, dm_wide):
            dv.append(mm(p.astype(BF16), dm))
        for ds, q in zip(dscores, q_wide):
            dk.append(mm(ds, q))
        for (b, rows, g), ds in zip(places, dscores):
            tall.append(mm(ds, qkv_ref[b, rows, group_cols(1, g)], TN))
        for i, (b, rows, g) in enumerate(places):
            dq = fold_heads(tall[i], masks) * score_scale
            dqkv_ref[b, rows, group_cols(0, g)] = dq.astype(BF16)
            dqkv_ref[b, rows, group_cols(1, g)] = (dk[i] * score_scale).astype(BF16)
            dqkv_ref[b, rows, group_cols(2, g)] = dv[i].astype(BF16)
    dqkv = dqkv_ref[...].reshape(len(some) * WROWS, 3 * D)
    attend_acc[...] += mm(a_ref[...].reshape(len(some) * WROWS, D), dqkv, TN)
    for b in some:
        dqkv_tokens = mm(perm_back_ref[...], dqkv_ref[b]).astype(BF16)
        grad_normed = mm(dqkv_tokens, attend_ref[0], NT)
        unit, inverse = norm_parts(x_ref[b].astype(F32))
        vecs_ref[0:1] += jnp.sum(grad_normed * unit, axis=0, keepdims=True)
        vecs_ref[1:2] += jnp.sum(grad_normed, axis=0, keepdims=True)
        grad_x = grad_mids[b] + norm_back(grad_normed, unit, inverse, g1_ref[depth : depth + 1])
        g_out_ref[b] = grad_x.astype(g_out_ref.dtype)
        if last:
            dy = (before_gate_ref[b][:, 0:1] * grad_x).astype(BF16)
            dy_rows_ref[pl.ds(step * len(some) + b, 1), 0:HW, :] = dy[None]

    @pl.when(step == pl.num_programs(0) - 1)
    def _():
        for acc, columns in ((attend_acc, slice(0, 3 * D)), (out_acc, slice(3 * D, 4 * D))):
            if order:
                spread_blocks(order_ref, acc, *mats_refs, columns)
            else:
                mats_refs[0][:, columns] = acc[...].astype(BF16)
        if part:
            for mats_ref, before in zip(mats_refs, earlier["mats"]):
                total = mats_ref[...].astype(F32) + before[...].astype(F32)
                mats_ref[...] = total.astype(BF16)
        if last:
            if part < parts - 1:
                dy_out_ref[...] = dy_rows_ref[...]
            else:
                runs = [ref[...] for ref in earlier.get("dy", [])] + [dy_rows_ref[...]]
                rows = jnp.concatenate([run.reshape(-1, D) for run in runs], axis=0)
                send_rows([dy_out_ref], before_target_ref[...], rows)


def run_backward(
    depth, grad, back, extra, saved, route_rows, target_rows, shared, order=None, before=()
):
    images = grad.shape[0]
    some = images_of(images)
    part, parts = len(before), BACKWARD_CALLS
    steps = images // some // parts
    last = depth == LAYERS - 1

    def by_image(shape):
        return pl.BlockSpec(
            (some,) + shape[1:], lambda i: (part * steps + i,) + (0,) * (len(shape) - 1)
        )

    args, specs = [], []
    if order is not None:
        args.append(order)
        specs.append(pl.BlockSpec(memory_space=pltpu.SMEM))
    args += [grad, back]
    specs += [by_image(grad.shape), whole(back.shape)]
    if last:
        y_back, before_gate, before_target = extra
        args += [y_back, before_gate, before_target]
        specs += [whole(y_back.shape), by_image(before_gate.shape), whole(before_target.shape)]
    else:
        args.append(extra)
        specs.append(by_image(extra.shape))
    for array in saved + [route_rows, target_rows]:
        args.append(array)
        specs.append(by_image(array.shape))
    for name in ("first_gain", "second_gain"):
        args.append(shared[name])
        specs.append(whole(shared[name].shape))
    for name in ("attend_weight", "output_weight", "router"):
        args.append(shared[name])
        specs.append(layer_of(shared[name].shape, depth))
    for name in ("bias", "mask", "perm", "perm_back"):
        args.append(shared[name][depth])
        specs.append(whole(shared[name][depth].shape))
    token_shape = (images, HW, D)
    outs = [(token_shape, F32 if last else BF16, by_image(token_shape))]
    if order is None:
        outs.append(((D, 4 * D), BF16, whole((D, 4 * D))))
    else:
        outs += [((D // 2, 4 * D), BF16, whole((D // 2, 4 * D)))] * 2
    mats = len(outs) - 1
    outs += [
        ((16, D), F32, whole((16, D))),
        ((LPAD, GROUPS * GW), F32, whole((LPAD, GROUPS * GW))),
    ]
    aliases = {}
    if last:
        outs.append((token_shape, BF16, by_image(token_shape)))
        shape = (SLOTS, D) if part == parts - 1 else (steps * some, TPAD, D)
        outs.append((shape, BF16, whole(shape)))
    if part:
        near = before[-1]
        plain = list(near[1 : 3 + mats])
        if last:
            plain += [results[-1] for results in before]
        args += plain
        specs += [whole(array.shape) for array in plain]
        for at in (0, 3 + mats) if last else (0,):
            aliases[len(args)] = at
            args.append(near[at])
            specs.append(pl.BlockSpec(memory_space=pl.ANY))
    scratch = [
        pltpu.VMEM((D, 3 * D), F32),
        pltpu.VMEM((D, D), F32),
        pltpu.VMEM((some, WROWS, 3 * D), BF16),
        pltpu.VMEM((some, WROWS, D), BF16),
    ]
    if last:
        scratch.append(pltpu.VMEM((steps * some, TPAD, D), BF16))
    return pl.pallas_call(
        partial(backward_kernel, depth, images, order is not None, part, parts),
        grid=(steps,),
        in_specs=specs,
        out_specs=[o[2] for o in outs],
        out_shape=[jax.ShapeDtypeStruct(o[0], o[1]) for o in outs],
        scratch_shapes=scratch,
        input_output_aliases=aliases,
        compiler_params=pltpu.CompilerParams(vmem_limit_bytes=VMEM_BYTES),
        cost_estimate=cost((33 if last else 24) / parts),
        name="backward_%d" % depth,
    )(*args)


def bits_of(axis, low, high):
    steps = []
    bit = low
    while bit < high:
        steps.append((axis, bit))
        bit *= 2
    return steps


def swap(x, step):
    axis, bit = step
    size = lax.axis_size(axis)
    return lax.ppermute(x, axis, [(i, i ^ bit) for i in range(size)])


def bit_at(step):
    axis, bit = step
    return (lax.axis_index(axis) // bit) % 2


def halved(rows, steps, least):
    count = 0
    while count < len(steps) and rows % 2 == 0 and rows // 2 >= least:
        rows //= 2
        count += 1
    return count


def sum_over(x, steps, least=24):
    count = halved(x.shape[0], steps, least)
    x = sum_all(scatter_sum(x, steps[:count]), steps[count:])
    return gather_all(x, steps[:count])


def scatter_sum(x, steps):
    for step in steps:
        half = x.shape[0] // 2
        mine = bit_at(step)
        keep = lax.dynamic_slice_in_dim(x, mine * half, half, 0)
        away = lax.dynamic_slice_in_dim(x, (1 - mine) * half, half, 0)
        x = (keep.astype(F32) + swap(away, step).astype(F32)).astype(x.dtype)
    return x


def gather_all(x, steps, dim=0):
    for step in reversed(steps):
        other = swap(x, step)
        mine = bit_at(step)
        first = jnp.where(mine == 0, x, other)
        second = jnp.where(mine == 0, other, x)
        x = jnp.concatenate([first, second], axis=dim)
    return x


def sum_all(x, steps):
    for step in steps:
        x = (x.astype(F32) + swap(x, step).astype(F32)).astype(x.dtype)
    return x


def exchange(rows, team):
    groups = lax.axis_size("expert")
    teams, size = None, groups
    if team:
        teams = [list(range(first, first + team)) for first in range(0, groups, team)]
        size = team
    width = rows.shape[-1]
    runs = rows.reshape(size, -1, width)
    runs = lax.all_to_all(
        runs, "expert", split_axis=0, concat_axis=0, tiled=True, axis_index_groups=teams
    )
    return runs.reshape(size, -1, ROWS, width)


def to_experts(rows, slices, team):
    if slices > 1:
        runs = rows.reshape(EXPERTS, ROWS, rows.shape[1])
        rows = jnp.repeat(runs, slices, axis=0)
    return exchange(rows, team)


def from_experts(rows, slices, team):
    width = rows.shape[-1]
    rows = exchange(rows, team).reshape(EXPERTS, slices, ROWS, width)
    return rows.transpose(1, 0, 2, 3).reshape(slices, SLOTS, width)


def unpack_down(packed):
    width = packed.shape[1]
    return jnp.concatenate(
        [packed[:, j * D : (j + 1) * D] for j in range(width // D)], axis=0
    )


def add_kernel(cuts, keep_ref, got_ref, *outs):
    total = keep_ref[...].astype(F32) + got_ref[...].astype(F32)
    for (start, stop), out in zip(cuts, outs):
        out[...] = total[start:stop].astype(out.dtype)


def add_rows(keep, got, cuts):
    rows, width = got.shape
    return pl.pallas_call(
        partial(add_kernel, cuts),
        grid=(1,),
        in_specs=[pl.BlockSpec((rows, width), lambda i: (0, 0))] * 2,
        out_specs=[pl.BlockSpec((b - a, width), lambda i: (0, 0)) for a, b in cuts],
        out_shape=[jax.ShapeDtypeStruct((b - a, width), keep.dtype) for a, b in cuts],
        compiler_params=pltpu.CompilerParams(vmem_limit_bytes=12 * 1024 * 1024),
        cost_estimate=cost(1),
        name="add_rows",
    )(keep, got)


def add_pair_kernel(keep_ref, got_ref, low_ref, high_ref, own_ref, first_ref, second_ref):
    own = (keep_ref[...].astype(F32) + got_ref[...].astype(F32)).astype(BF16)
    own_ref[...] = own
    rows = low_ref.shape[0]
    for at, other, out in ((0, low_ref, first_ref), (rows, high_ref, second_ref)):
        total = own[at : at + rows].astype(F32) + other[...].astype(F32)
        out[...] = total.astype(BF16)


def add_pair(keep, got, low, high):
    return pl.pallas_call(
        add_pair_kernel,
        out_shape=[jax.ShapeDtypeStruct(a.shape, BF16) for a in (keep, low, high)],
        compiler_params=pltpu.CompilerParams(vmem_limit_bytes=12 * 1024 * 1024),
        cost_estimate=cost(1),
        name="add_pair",
    )(keep, got, low, high)


def add_halves_kernel(own_ref, low_ref, high_ref, out_ref):
    rows = low_ref.shape[0]
    for at, other in ((0, low_ref), (rows, high_ref)):
        total = own_ref[at : at + rows].astype(F32) + other[...].astype(F32)
        out_ref[at : at + rows] = total.astype(BF16)


def add_halves(own, low, high):
    return pl.pallas_call(
        add_halves_kernel,
        out_shape=jax.ShapeDtypeStruct(own.shape, BF16),
        compiler_params=pltpu.CompilerParams(vmem_limit_bytes=12 * 1024 * 1024),
        cost_estimate=cost(1),
        name="add_halves",
    )(own, low, high)


def join_kernel(first_ref, second_ref, out_ref):
    rows = first_ref.shape[0]
    out_ref[0:rows] = first_ref[...]
    out_ref[rows:] = second_ref[...]


def join_rows(first, second):
    rows, width = first.shape
    return pl.pallas_call(
        join_kernel,
        out_shape=jax.ShapeDtypeStruct((2 * rows, width), first.dtype),
        compiler_params=pltpu.CompilerParams(vmem_limit_bytes=8 * 1024 * 1024),
        cost_estimate=cost(1),
        name="join_rows",
    )(first, second)


def pack_kernel(order_ref, up_a, up_b, down_a, down_b, up_ref, down_ref, quarter_ref, rows_ref):
    up = (up_a[0].astype(F32) + up_b[0].astype(F32)).astype(BF16)
    down = (down_a[0].astype(F32) + down_b[0].astype(F32)).astype(BF16)
    up_ref[...] = up
    down_ref[...] = down
    step, steps = pl.program_id(0), pl.num_programs(0)
    some, width = up.shape
    rows_ref[pl.ds(pl.multiple_of(step * some, some), some)] = up
    for c in range(down.shape[0] // D):
        rows_ref[D : 2 * D, c * D : (c + 1) * D] = down[c * D : (c + 1) * D]

    @pl.when(step == steps - 1)
    def _():
        quarter = quarter_ref.shape[0]
        start = pl.multiple_of(order_ref[0] * quarter, quarter)
        quarter_ref[...] = rows_ref[pl.ds(start, quarter)]


def pack_weights(depth, order, core_up, residual_up, core_down, residual_down):
    width = residual_up.shape[2]
    arrays = [core_up, residual_up, core_down, residual_down]
    shapes = [(D, width), (width, D), (D // 2, width)]
    return pl.pallas_call(
        pack_kernel,
        grid=(1,),
        in_specs=[pl.BlockSpec(memory_space=pltpu.SMEM)]
        + [layer_of(array.shape, depth) for array in arrays],
        out_specs=[whole(shape) for shape in shapes],
        out_shape=[in_hbm(shape, BF16) for shape in shapes],
        scratch_shapes=[pltpu.VMEM((2 * D, width), BF16)],
        compiler_params=pltpu.CompilerParams(vmem_limit_bytes=VMEM_BYTES),
        cost_estimate=cost(4),
        name="pack_weights",
    )(order, *map(from_hbm, arrays))


def unpack_kernel(order_ref, *refs):
    pieces, (own_up, own_down, up_ref, down_ref, rows_ref) = refs[:4], refs[4:]
    quarter = pieces[0].shape[0]
    for r, piece in enumerate(pieces):
        start = pl.multiple_of(jnp.bitwise_xor(order_ref[0], r) * quarter, quarter)
        rows_ref[pl.ds(start, quarter)] = piece[...]
    up_ref[0] = own_up[...]
    down_ref[0] = own_down[...]
    up_ref[1] = rows_ref[0:D]
    for c in range(down_ref.shape[1] // D):
        down_ref[1, c * D : (c + 1) * D] = rows_ref[D : 2 * D, c * D : (c + 1) * D]


def unpack_weights(order, pieces, own_up, own_down):
    width = pieces[0].shape[1]
    shapes = [(2, D, width), (2, width, D)]
    args = [*pieces, from_hbm(own_up), from_hbm(own_down)]
    return pl.pallas_call(
        unpack_kernel,
        grid=(1,),
        in_specs=[pl.BlockSpec(memory_space=pltpu.SMEM)] + [whole(a.shape) for a in args],
        out_specs=[whole(shape) for shape in shapes],
        out_shape=[in_hbm(shape, BF16) for shape in shapes],
        scratch_shapes=[pltpu.VMEM((2 * D, width), BF16)],
        compiler_params=pltpu.CompilerParams(vmem_limit_bytes=EXPERT_VMEM),
        cost_estimate=cost(3),
        name="unpack_weights",
    )(order, *args)


def expert_outputs_kernel(earlier, plain, order_ref, *refs):
    pieces, refs = refs[:8], refs[8:]
    refs = refs[4 if earlier else 0 :]
    outs, (rows_ref,) = refs[:4], refs[4:]
    step = pl.program_id(0)
    quarter = pieces[0].shape[0]

    @pl.when(step == 0)
    def _():
        for kind in range(2):
            for r in range(4):
                rows_ref[kind, r * quarter : (r + 1) * quarter] = pieces[kind * 4 + r][...]

    half = pl.num_programs(0)
    for kind in range(2):
        for part in range(2):
            place = jnp.bitwise_xor(order_ref[0], step + part * half)
            if kind == 1 and not plain:
                place = place // 8 * 8 + place // 2 % 2 * 4 + place // 4 % 2 * 2 + place % 2
            start = pl.multiple_of(place * BLOCK, BLOCK)
            block = rows_ref[kind, pl.ds(start, BLOCK)].astype(F32)
            out = outs[kind * 2 + part]
            if part == 0:
                out[0] = block
            else:
                for c in range(out.shape[1]):
                    out[0, c] = block[:, c * D : (c + 1) * D]


def expert_outputs(depth, order, residual, core, earlier, plain=False):
    width = residual[0].shape[1]
    half = D // BLOCK
    count = width // D
    up = jax.ShapeDtypeStruct((LAYERS, D, width), F32)
    down = jax.ShapeDtypeStruct((LAYERS, count, D, D), F32)
    up_spec = pl.BlockSpec((1, BLOCK, width), lambda i: (depth, i, 0))
    down_spec = pl.BlockSpec((1, count, BLOCK, D), lambda i: (depth, 0, i, 0))
    pieces = residual + core
    specs = [pl.BlockSpec(residual[0].shape, lambda i: (0, 0))] * len(pieces)
    earlier = list(earlier or [])
    return pl.pallas_call(
        partial(expert_outputs_kernel, bool(earlier), plain),
        grid=(half,),
        in_specs=[pl.BlockSpec(memory_space=pltpu.SMEM)]
        + specs
        + [pl.BlockSpec(memory_space=pl.ANY)] * len(earlier),
        out_specs=[up_spec, down_spec] * 2,
        out_shape=[up, down] * 2,
        scratch_shapes=[pltpu.VMEM((2, 2 * D, width), BF16)],
        input_output_aliases={9 + i: i for i in range(len(earlier))},
        compiler_params=pltpu.CompilerParams(vmem_limit_bytes=32 * 1024 * 1024),
        cost_estimate=cost(4),
        name="expert_outputs",
    )(order, *pieces, *earlier)


def attend_outputs_kernel(earlier, order_ref, *refs):
    pieces, refs = refs[:2], refs[2:]
    refs = refs[2 if earlier else 0 :]
    attend_ref, out_ref, rows_ref = refs
    half = pieces[0].shape[0]
    for r in range(2):
        rows_ref[r * half : (r + 1) * half] = pieces[r][...].astype(F32)
    for j in range(D // BLOCK):
        start = pl.multiple_of(jnp.bitwise_xor(order_ref[0], j) * BLOCK, BLOCK)
        block = rows_ref[pl.ds(start, BLOCK)]
        attend_ref[0, j * BLOCK : (j + 1) * BLOCK] = block[:, : 3 * D]
        out_ref[0, j * BLOCK : (j + 1) * BLOCK] = block[:, 3 * D :]


def attend_outputs(depth, order, pieces, earlier):
    earlier = list(earlier or [])
    shapes = [(LAYERS, D, 3 * D), (LAYERS, D, D)]
    return pl.pallas_call(
        partial(attend_outputs_kernel, bool(earlier)),
        grid=(1,),
        in_specs=[pl.BlockSpec(memory_space=pltpu.SMEM)]
        + [whole(p.shape) for p in pieces]
        + [pl.BlockSpec(memory_space=pl.ANY)] * len(earlier),
        out_specs=[layer_of(shape, depth) for shape in shapes],
        out_shape=[jax.ShapeDtypeStruct(shape, F32) for shape in shapes],
        scratch_shapes=[pltpu.VMEM((D, 4 * D), F32)],
        input_output_aliases={3 + i: i for i in range(len(earlier))},
        compiler_params=pltpu.CompilerParams(vmem_limit_bytes=24 * 1024 * 1024),
        cost_estimate=cost(2),
        name="attend_outputs",
    )(order, *pieces, *earlier)


CORE, ROW = ("dp", 1), ("dp", 2)
NEAR_X, NEAR_Z, FAR_Z = ("expert", 1), ("expert", 2), ("expert", 4)


def place_order(steps):
    order = 0
    for step in steps:
        order = order * 2 + bit_at(step)
    return jnp.full((1,), order, jnp.int32)


class Steps:
    def run(self, *steps):
        for step in steps:
            getattr(self, step)()


class PairSum(Steps):
    def __init__(self, keep, send):
        self.keep, self.send = keep, send

    def core(self):
        self.send = swap(self.send, CORE)

    def add_core(self):
        rows = self.keep.shape[0] // 4
        cuts = tuple((i * rows, (i + 1) * rows) for i in range(4))
        self.own, self.partner, self.send, self.send_partner = add_rows(
            self.keep, self.send, cuts
        )
        del self.keep

    def row_own(self):
        self.send = swap(self.send, ROW)

    def row_partner(self):
        self.send_partner = swap(self.send_partner, ROW)

    def add_partner(self):
        rows = self.partner.shape[0] // 2
        cuts = ((0, rows), (rows, 2 * rows))
        self.partner_low, self.partner_high = add_rows(
            self.partner, self.send_partner, cuts
        )
        del self.partner, self.send_partner

    def add_own(self):
        self.own, self.total, self.send = add_pair(
            self.own, self.send, self.partner_low, self.partner_high
        )

    def far_low(self):
        self.partner_low = swap(self.partner_low, FAR_Z)

    def far_high(self):
        self.partner_high = swap(self.partner_high, FAR_Z)

    def add_far(self):
        self.mine = add_halves(self.own, self.partner_low, self.partner_high)
        del self.own, self.partner_low, self.partner_high

    def residual_row(self):
        self.mine_row = swap(self.mine, ROW)

    def residual_core(self):
        self.mine_core = swap(self.mine, CORE)
        self.row_core = swap(self.mine_row, CORE)

    def residual_pieces(self):
        return [self.mine, self.mine_row, self.mine_core, self.row_core]

    def near_x(self):
        self.send = swap(self.send, NEAR_X)

    def add_near_x(self):
        rows = self.send.shape[0]
        cuts = ((0, rows // 2), (rows // 2, rows))
        self.total, self.send = add_rows(self.total, self.send, cuts)

    def near_z(self):
        self.send = swap(self.send, NEAR_Z)

    def add_near_z(self):
        (self.total,) = add_rows(self.total, self.send, ((0, self.send.shape[0]),))
        self.send = self.total

    def far_z(self):
        self.send = swap(self.send, FAR_Z)

    def add_far_z(self):
        (self.total,) = add_rows(self.total, self.send, ((0, self.send.shape[0]),))

    def back_z(self):
        self.send = swap(self.total, NEAR_Z)

    def back_row(self):
        self.total = join_rows(self.total, self.send)
        self.send = swap(self.total, ROW)

    def back_x(self):
        self.total = join_rows(self.total, self.send)
        self.send = swap(self.total, NEAR_X)

    def back_core(self):
        self.total_core = swap(self.total, CORE)
        self.send_core = swap(self.send, CORE)

    def core_pieces(self):
        return [self.total, self.send, self.total_core, self.send_core]


class AttendSum(Steps):
    def __init__(self, keep, send):
        self.keep, self.send = keep, send

    def core(self):
        self.send = swap(self.send, CORE)

    def add_half(self):
        rows = self.send.shape[0] // 2
        cuts = ((0, rows), (rows, 2 * rows))
        self.keep, self.send = add_rows(self.keep, self.send, cuts)

    def row(self):
        self.send = swap(self.send, ROW)

    def near_x(self):
        self.send = swap(self.send, NEAR_X)

    def add(self):
        (self.keep,) = add_rows(self.keep, self.send, ((0, self.send.shape[0]),))
        self.send = self.keep

    def near_z(self):
        self.send = swap(self.send, NEAR_Z)

    def far_z(self):
        self.send = swap(self.send, FAR_Z)

    def back_x(self):
        self.send = swap(self.keep, NEAR_X)

    def back_row(self):
        self.keep = join_rows(self.keep, self.send)
        self.send = swap(self.keep, ROW)

    def back_core(self):
        self.keep = join_rows(self.keep, self.send)
        self.send = swap(self.keep, CORE)

    def pieces(self):
        return [self.keep, self.send]


class SmallSum(Steps):
    def __init__(self, value):
        self.value = value

    def swap(self, step):
        self.send = swap(self.value, step)

    def add(self):
        self.value = self.value + self.send


def at_once(values, *objects):
    fields = [
        (o, name)
        for o in objects
        for name, field in vars(o).items()
        if isinstance(field, jax.Array)
    ]
    held = [getattr(o, name) for o, name in fields]
    values, held = lax.optimization_barrier((tuple(values), held))
    for (o, name), field in zip(fields, held):
        setattr(o, name, field)
    return values


def after(value, *done):
    return lax.optimization_barrier((value,) + done)[0]


def body(
    block_input,
    routes,
    first_gain,
    first_shift,
    attend_weight,
    bias_table,
    output_weight,
    second_gain,
    second_shift,
    router_weight,
    core_up,
    core_down,
    residual_up,
    residual_down,
    cotangent,
):
    groups = lax.axis_size("expert")
    slices = groups // EXPERTS
    group_part = lax.axis_index("expert") % slices
    images = block_input.shape[0]
    width = residual_up.shape[2]

    routes_rows = jnp.pad(
        routes.reshape(LAYERS, images, HW), ((0, 0), (0, 0), (0, TPAD - HW)), constant_values=-1
    )
    alone = slices == 1
    half = lax.axis_index("expert") // TEAM
    ups, downs, quarters = [], [], []
    dp_order = place_order((CORE, ROW)) if alone else None
    for d in range(LAYERS):
        if not alone:
            up = lax.dynamic_slice_in_dim(core_up[d], group_part * width, width, 1)
            down = lax.dynamic_slice_in_dim(core_down[d], group_part * width, width, 0)
            ups.append((up.astype(F32) + residual_up[d].astype(F32)).astype(BF16)[None])
            downs.append((down.astype(F32) + residual_down[d].astype(F32)).astype(BF16)[None])

    def pack(d, core_up):
        up, down, quarter = pack_weights(
            d, dp_order, core_up, residual_up, core_down, residual_down
        )
        ups.append(up)
        downs.append(down)
        quarters.append(quarter)

    teams = [TEAM if alone else 0] * LAYERS
    if alone:
        pack(0, core_up)
        routes_rows, bias_table = after((routes_rows, bias_table), quarters[0])
    targets = run_routing(routes_rows, jnp.full((1,), half, jnp.int32), teams)

    table_index = jnp.asarray(offset_table(), jnp.int32)
    picker = (jnp.arange(OFFSETS, dtype=jnp.int32)[:, None] == table_index[None, :]).astype(F32)
    flat_table = bias_table.transpose(0, 2, 1).reshape(LAYERS * HEADS, OFFSETS)
    bias = jnp.dot(flat_table, picker, precision=lax.Precision.HIGHEST)
    bias = (
        bias.reshape(LAYERS, HEADS, LPAD, LPAD)
        .transpose(0, 2, 1, 3)
        .reshape(LAYERS, LPAD, HEADS * LPAD)
    )
    offsets = [SHIFT * (depth % 2) for depth in range(LAYERS)]
    shared = {
        "first_gain": first_gain,
        "first_shift": first_shift,
        "second_gain": second_gain,
        "second_shift": second_shift,
        "attend_weight": attend_weight,
        "output_weight": output_weight,
        "router": jnp.pad(router_weight, ((0, 0), (0, 0), (0, LANES - EXPERTS))),
        "bias": [bias[depth] for depth in range(LAYERS)],
        "mask": [jnp.asarray(score_mask(o)) for o in offsets],
        "perm": [jnp.asarray(permutation(o), BF16) for o in offsets],
        "perm_back": [jnp.asarray(permutation(o).T, BF16) for o in offsets],
    }
    route_rows = [routes_rows[d].reshape(images, 1, TPAD) for d in range(LAYERS)]
    target_rows = [targets[d].reshape(images, 1, TPAD) for d in range(LAYERS)]
    target_all = [targets[d].reshape(1, images * TPAD) for d in range(LAYERS)]
    picked_type = BF16 if slices == 1 else F32
    saved, inner, gates, xs, picks = [], [], [], [block_input], []
    x, earlier = block_input, None
    dy_arrived = None
    def in_parts(rows):
        return [rows[i : i + PART] for i in range(0, rows.shape[0], PART)]

    for d in range(LAYERS):
        if alone:
            quarter = quarters[d]
            if d:
                quarter, back = lax.optimization_barrier((quarter, back))
                earlier = (back,) + earlier[1:]
            far = swap(quarter, FAR_Z)
            x = after(x, quarter)
        outs, outgoing = run_forward(
            d, x, earlier, cotangent, route_rows[d], target_rows[d], target_all[d], shared
        )
        qkv, a, mixed, mid, n, probs, gate = outs[:7]
        if d:
            xs.append(outs[7])
            picks.append(outs[8])
        if alone:
            *outgoing, far = lax.optimization_barrier((*outgoing, far))
            far_row = swap(far, ROW)
        arrived = to_experts(outgoing[0], slices, teams[d])
        if alone and d == 0:
            pack(1, after(core_up, outgoing[0]))
        if d == LAYERS - 1:
            dy_arrived = to_experts(outgoing[1], slices, teams[d])
        if alone:
            arrived, far, far_row = lax.optimization_barrier((arrived, far, far_row))
            pieces = [far, far_row, swap(far, CORE), swap(far_row, CORE)]
            y = run_expert_forward(arrived, ups[d][None], downs[d][None], 0)
            ups[d], downs[d] = unpack_weights(dp_order, pieces, ups[d], downs[d])
            y = run_expert_forward(arrived, ups[d], downs[d], 1, y)
        else:
            y = run_expert_forward(arrived, ups[d], downs[d])
        if d == LAYERS - 1:
            y, dy_arrived = lax.optimization_barrier((y, dy_arrived))
        back = y_back = from_experts(y, slices, teams[d])
        earlier = (back, gate, target_rows[d], picked_type)
        x = mid
        gates.append(gate)
        saved.append([xs[d], qkv, a, mixed, mid, n, probs, gate])
        inner.append(arrived)

    grad = cotangent
    vecs, tables = [None] * 2, [None] * 2
    block_output = None
    expert_order = place_order((CORE, ROW, NEAR_X, NEAR_Z)) if alone else None
    attend_order = place_order((CORE, ROW, NEAR_X)) if alone else None
    expert_sums, attend_sums = [None] * 2, [None] * 2
    for d in reversed(range(LAYERS)):
        arrived = inner[d]
        dn, hidden, du = run_expert_both(arrived, dy_arrived, ups[d], downs[d])
        if alone:
            sums = [] if d else [expert_sums[1], attend_sums[1]]
            dn, hidden, du, y_back = at_once((dn, hidden, du, y_back), *sums)
        back = from_experts(dn, slices, teams[d])
        grads = run_expert_weights(arrived, dy_arrived, hidden, du, expert_order)
        expert_sums[d] = grads
        if alone:
            expert_sums[d] = PairSum(*grads)
        if alone and d == 0:
            expert_sums[0].run("core")
            expert_sums[1].run("add_own", "near_x")
            attend_sums[1].run("add_half", "row")
        if d == LAYERS - 1:
            extra = (y_back, gates[d - 1], target_all[d - 1])
        else:
            extra = picks[d]
        before = []
        for part in range(BACKWARD_CALLS):
            if alone:
                sums = expert_sums[1:] if d else expert_sums + [attend_sums[1]]
                grad, back, before = at_once((grad, back, before), *sums)
                if d:
                    expert_sums[1].run("core")
                else:
                    expert_sums[0].run("add_core", "row_partner", "row_own")
                    expert_sums[1].run("far_low", "far_high", "add_near_x", "near_z")
                    attend_sums[1].run("add_half", "near_x")
            before = before + [
                run_backward(
                    d,
                    grad,
                    back,
                    extra,
                    saved[d],
                    route_rows[d],
                    target_rows[d],
                    shared,
                    attend_order,
                    before,
                )
            ]
        outs = before[-1]
        if alone:
            grad, keep, send, vecs[d], tables[d] = outs[:5]
            attend_sums[d] = AttendSum(keep, send)
            outs = outs[5:]
        else:
            grad, attend_sums[d], vecs[d], tables[d] = outs[:4]
            outs = outs[4:]
        if d == LAYERS - 1:
            block_output, dy_out = outs
            if alone:
                (dy_out,) = at_once((dy_out,), expert_sums[1], attend_sums[1])
                expert_sums[1].run("add_core", "row_partner")
                attend_sums[1].run("core")
            dy_arrived = to_experts(dy_out, slices, teams[0])
            if alone:
                (dy_arrived,) = at_once((dy_arrived,), expert_sums[1], attend_sums[1])
                expert_sums[1].run("add_partner", "row_own")
        elif alone:
            at_once((), *expert_sums, *attend_sums)
    input_grad = grad

    dp_steps = bits_of("dp", 1, lax.axis_size("dp"))
    slice_steps = bits_of("expert", 1, slices)
    sum_steps = bits_of("expert", slices, groups)
    all_steps = dp_steps + slice_steps + sum_steps
    table_grad = jnp.stack(tables).reshape(LAYERS, LPAD, HEADS, LPAD).transpose(0, 2, 1, 3)
    table_grad = jnp.dot(
        table_grad.reshape(LAYERS * HEADS, LPAD * LPAD), picker.T, precision=lax.Precision.HIGHEST
    )
    small = jnp.concatenate(
        [
            jnp.stack(vecs).reshape(LAYERS * 16, D),
            jnp.pad(table_grad, ((0, 0), (0, D - OFFSETS))),
        ],
        axis=0,
    )
    if alone:
        experts, full = None, None
        sums, sums_before = expert_sums
        attend, attend_before = attend_sums
        tiny = SmallSum(small)
        attend.run("core")
        sums.run("add_partner", "add_own", "far_low", "near_x")
        sums_before.run("add_far", "residual_row", "add_near_z", "far_z")
        attend_before.run("add", "near_z")
        at_once((), attend, sums, sums_before, attend_before)
        attend.run("add_half", "row")
        sums.run("far_high", "add_near_x", "near_z")
        sums_before.run("residual_core", "add_far_z", "back_z")
        at_once((), attend, sums, sums_before, attend_before, tiny)
        attend.run("add_half", "near_x", "add", "near_z", "add", "far_z")
        attend.run("add", "back_x", "back_row", "back_core")
        sums.run("add_near_z", "far_z", "add_far_z", "add_far", "residual_row")
        sums.run("back_z", "back_row", "back_x", "back_core", "residual_core")
        sums_before.run("back_row", "back_x", "back_core")
        attend_before.run("add", "far_z", "add", "back_x", "back_row", "back_core")
        for step in all_steps:
            tiny.swap(step)
            tiny.add()
        small = tiny.value
        experts = expert_outputs(
            1, expert_order, sums_before.residual_pieces(), sums_before.core_pieces(), None
        )
        experts = expert_outputs(
            0, expert_order, sums.residual_pieces(), sums.core_pieces(), experts
        )
        full = attend_outputs(1, attend_order, attend_before.pieces(), None)
        full = attend_outputs(0, attend_order, attend.pieces(), full)
        residual_up_grad, residual_down_grad, core_up_grad, core_down_grad = experts
        residual_down_grad = residual_down_grad.reshape(LAYERS, width, D)
        core_down_grad = core_down_grad.reshape(LAYERS, width, D)
        attend_weight_grad, output_weight_grad = full
    else:
        small = sum_all(small, all_steps)
        residual, core, full = [], [], []
        for d in range(LAYERS):
            part = scatter_sum(expert_sums[d], dp_steps)
            residual.append(gather_all(part, dp_steps))
            total = gather_all(sum_over(part, sum_steps), dp_steps)
            core.append(gather_all(total, slice_steps, dim=1))
            full.append(sum_over(attend_sums[d], all_steps))
        full = jnp.stack(full).astype(F32)
        attend_weight_grad, output_weight_grad = full[:, :, : 3 * D], full[:, :, 3 * D :]
        residual_up_grad = jnp.stack([r[:D] for r in residual]).astype(F32)
        residual_down_grad = jnp.stack([unpack_down(r[D:]) for r in residual]).astype(F32)
        core_up_grad = jnp.stack([c[:D] for c in core]).astype(F32)
        core_down_grad = jnp.stack([unpack_down(c[D:]) for c in core]).astype(F32)
    vec = small[: LAYERS * 16].reshape(LAYERS, 16, D)
    table = small[LAYERS * 16 :, :OFFSETS].reshape(LAYERS, HEADS, OFFSETS).transpose(0, 2, 1)
    return (
        block_output,
        input_grad,
        vec[:, 0],
        vec[:, 1],
        attend_weight_grad,
        table,
        output_weight_grad,
        vec[:, 2],
        vec[:, 3],
        vec[:, 8:16].transpose(0, 2, 1),
        core_up_grad,
        core_down_grad,
        residual_up_grad,
        residual_down_grad,
    )


def solution(mesh):
    placed = (
        P(("dp", "expert"), None, None),
        P(None, ("dp", "expert"), None, None),
        P(),
        P(),
        P(),
        P(),
        P(),
        P(),
        P(),
        P(),
        P(),
        P(),
        P(None, None, "expert"),
        P(None, "expert", None),
        P(("dp", "expert"), None, None),
    )
    return jax.shard_map(
        body,
        mesh=mesh,
        in_specs=placed,
        out_specs=(
            P(("dp", "expert"), None, None),
            P(("dp", "expert"), None, None),
            P(),
            P(),
            P(),
            P(),
            P(),
            P(),
            P(),
            P(),
            P(),
            P(),
            P(None, None, "expert"),
            P(None, "expert", None),
        ),
        check_vma=False,
    )
```

```python
from functools import partial

import jax
import jax.numpy as jnp
import numpy as np
from jax import lax
from jax.experimental import pallas as pl
from jax.experimental.pallas import tpu as pltpu
from jax.sharding import PartitionSpec as P

D = 384
HEADS = 12
HD = 32
FF = 1536
EXPERTS = 8
WIN = 7
SIDE = 14
SHIFT = 3
LAYERS = 2
HW = 196
CAP = 184
OFFSETS = 169
ROWS = 192
SLOTS = EXPERTS * ROWS

WINDOWS = (SIDE // WIN) * (SIDE // WIN)
LENGTH = WIN * WIN
LPAD = 64
WROWS = WINDOWS * LPAD
TPAD = 256
LANES = 128
GROUP = LANES // HD
GROUPS = HEADS // GROUP
GW = GROUP * LPAD
FCHUNK = 384
SOURCES = 2
FTILE = 512
EXPERT_VMEM = 32 * 1024 * 1024
BLOCK = 48
PAIRS_AT_ONCE = 2
TEAM = 4
BACKWARD_CALLS = 1
STEP_IMAGES = 3

F32 = jnp.float32
BF16 = jnp.bfloat16
eps_norm = 1e-05
mask_fill = -100.0
pad_fill = -1e30
score_scale = HD ** (-0.5)
VMEM_BYTES = 56 * 1024 * 1024

NN = (((1,), (0,)), ((), ()))
NT = (((1,), (1,)), ((), ()))
TN = (((0,), (0,)), ((), ()))


def mm(a, b, dims=NN):
    return lax.dot_general(a, b, dims, preferred_element_type=F32)


def window_tokens(offset):
    rows = np.full((WINDOWS, LPAD), -1, np.int64)
    per_side = SIDE // WIN
    for w in range(WINDOWS):
        for i in range(LENGTH):
            r = (w // per_side) * WIN + i // WIN
            c = (w % per_side) * WIN + i % WIN
            rows[w, i] = ((r + offset) % SIDE) * SIDE + (c + offset) % SIDE
    return rows.reshape(-1)


def permutation(offset):
    rows = window_tokens(offset)
    return (rows[:, None] == np.arange(HW)[None, :]).astype(np.float32)


def score_mask(offset):
    coords = np.arange(SIDE)
    bands = (coords >= SIDE - WIN).astype(int) + (coords >= SIDE - offset).astype(int)
    labels = bands[:, None] * 3 + bands[None, :]
    per_side = SIDE // WIN
    out = np.zeros((WINDOWS, LPAD, LPAD), np.float32)
    for w in range(WINDOWS):
        r0, c0 = (w // per_side) * WIN, (w % per_side) * WIN
        flat = labels[r0 : r0 + WIN, c0 : c0 + WIN].reshape(-1)
        out[w, :LENGTH, :LENGTH] = np.where(flat[:, None] == flat[None, :], 0.0, mask_fill)
        out[w, LENGTH:, :] = pad_fill
    return np.tile(out, (1, 1, GROUP))


def offset_table():
    i = np.arange(LENGTH)
    r, c = i // WIN, i % WIN
    index = np.full((LPAD, LPAD), -1, np.int64)
    index[:LENGTH, :LENGTH] = (
        (r[None, :] - r[:, None] + WIN - 1) * (2 * WIN - 1) + c[None, :] - c[:, None] + WIN - 1
    )
    return index.reshape(-1)


def norm_parts(x):
    centred = x - jnp.mean(x, axis=-1, keepdims=True)
    inverse = lax.rsqrt(jnp.mean(centred * centred, axis=-1, keepdims=True) + eps_norm)
    return centred * inverse, inverse


def norm_back(grad, unit, inverse, gain):
    scaled = grad * gain
    return inverse * (
        scaled
        - jnp.mean(scaled, axis=-1, keepdims=True)
        - unit * jnp.mean(scaled * unit, axis=-1, keepdims=True)
    )


def one_hot(cond):
    return jnp.where(cond, 1.0, 0.0).astype(BF16)


def head_masks():
    lane = lax.broadcasted_iota(jnp.int32, (1, LANES), 1) // HD
    return [jnp.where(lane == h, 1.0, 0.0) for h in range(GROUP)]


def spread_heads(block, masks):
    return jnp.concatenate([block * m.astype(BF16) for m in masks], axis=0)


def fold_heads(tall, masks):
    total = tall[0:LPAD] * masks[0]
    for h in range(1, GROUP):
        total = total + tall[h * LPAD : (h + 1) * LPAD] * masks[h]
    return total


def as_column(row, count):
    wide = jnp.broadcast_to(row.astype(F32), (8, TPAD))
    return wide.T[:count, 0:1].astype(jnp.int32)


def pick_rows(target_row, *arrays):
    column = as_column(target_row, HW)
    place = one_hot(lax.broadcasted_iota(jnp.int32, (HW, SLOTS), 1) == column)
    picked = []
    for rows_ref in arrays:
        total = mm(place, rows_ref[0])
        for k in range(1, rows_ref.shape[0]):
            total = total + mm(place, rows_ref[k])
        picked.append(total)
    return picked


def send_rows(out_refs, target_all, rows):
    step = SLOTS // 4
    for c in range(4):
        slot = lax.broadcasted_iota(jnp.int32, (step, rows.shape[0]), 0) + c * step
        block = mm(one_hot(slot == target_all), rows).astype(BF16)
        for at, ref in enumerate(out_refs):
            ref[c * step : (c + 1) * step] = block[:, at * D : (at + 1) * D]


def gelu_parts(u):
    cdf = 0.5 + 0.5 * lax.erf(u * (0.5**0.5))
    bell = jnp.exp(-0.5 * u * u)
    return u * cdf, cdf + u * (bell * 0.3989422804014327)


def in_hbm(shape, dtype):
    return pltpu.HBM(tuple(shape), dtype)


def from_hbm(array):
    return pltpu.with_memory_space_constraint(array, pltpu.HBM)


def cost(microseconds):
    return pl.CostEstimate(
        flops=int(microseconds * 9e8), bytes_accessed=1000, transcendentals=0
    )


def routing_kernel(paired, half_ref, routes_ref, target_ref):
    before = one_hot(
        lax.broadcasted_iota(jnp.int32, (TPAD, TPAD), 0)
        <= lax.broadcasted_iota(jnp.int32, (TPAD, TPAD), 1)
    )
    expert = lax.broadcasted_iota(jnp.int32, (16, TPAD), 0)
    for depth in range(LAYERS):
        carry = jnp.zeros((16, 1), F32)
        for i in range(routes_ref.shape[1]):
            row = routes_ref[depth, i : i + 1, :]
            chosen = jnp.where(expert == row, 1.0, 0.0)
            counts = mm(chosen.astype(BF16), before) + carry
            carry = counts[:, TPAD - 1 : TPAD]
            slot = jnp.sum(chosen * counts, axis=0, keepdims=True).astype(jnp.int32) - 1
            kept = (slot >= 0) & (slot < CAP)
            place = row
            if paired[depth]:
                place = (row % TEAM) * 2 + jnp.bitwise_xor(row // TEAM, half_ref[0])
            target_ref[depth, i : i + 1, :] = jnp.where(kept, place * ROWS + slot, -1)


def run_routing(routes, half, paired):
    return pl.pallas_call(
        partial(routing_kernel, paired),
        in_specs=[
            pl.BlockSpec(memory_space=pltpu.SMEM),
            pl.BlockSpec(memory_space=pltpu.VMEM),
        ],
        out_shape=jax.ShapeDtypeStruct(routes.shape, jnp.int32),
        name="routing",
    )(half, routes)


def group_cols(part, g):
    return slice(part * D + g * LANES, part * D + (g + 1) * LANES)


def softmax_down(scores):
    raised = jnp.exp(scores - jnp.max(scores, axis=0, keepdims=True))
    return raised * (1.0 / jnp.sum(raised, axis=0, keepdims=True))


def window_items(some):
    pairs = [(w, g) for w in range(WINDOWS) for g in range(GROUPS)]
    runs = []
    for first in range(0, len(pairs), PAIRS_AT_ONCE):
        runs.append([(w, g, b) for w, g in pairs[first : first + PAIRS_AT_ONCE] for b in some])
    return runs


def raw_scores(qkv_ref, items, masks):
    wide, scores = [], []
    for w, g, b in items:
        rows = slice(w * LPAD, (w + 1) * LPAD)
        wide.append(spread_heads(qkv_ref[b, rows, group_cols(0, g)], masks))
    for (w, g, b), q_wide in zip(items, wide):
        rows = slice(w * LPAD, (w + 1) * LPAD)
        scores.append(mm(qkv_ref[b, rows, group_cols(1, g)], q_wide, NT))
    return wide, scores


def to_probs(items, scores, bias_ref, mask_ref):
    probs = []
    for (w, g, b), score in zip(items, scores):
        probs.append(
            softmax_down(
                score * score_scale + bias_ref[:, g * GW : (g + 1) * GW] + mask_ref[w]
            )
        )
    return probs


def forward_kernel(depth, images, *refs):
    last = depth == LAYERS - 1
    refs = list(refs)
    take = lambda: refs.pop(0)
    x_ref = take()
    if depth:
        back_ref, gate_in_ref, target_in_ref = take(), take(), take()
    if last:
        cot_ref = take()
    (route_ref, target_ref, g1_ref, s1_ref, g2_ref, s2_ref, attend_ref, out_w_ref) = refs[:8]
    (router_ref, bias_ref, mask_ref, perm_ref, perm_back_ref) = refs[8:13]
    refs = refs[13:]
    (qkv_ref, a_ref, mixed_ref, mid_ref, n_ref, probs_ref, gate_ref) = refs[:7]
    refs = refs[7:]
    if depth:
        x_out_ref, picked_ref = take(), take()
    out_refs = [take() for _ in range(2 if last else 1)]
    rows_ref = take()

    step = pl.program_id(0)

    @pl.when(step == 0)
    def _():
        rows_ref[...] = jnp.zeros_like(rows_ref)

    some = range(x_ref.shape[0])
    xs = []
    for b in some:
        x = x_ref[b].astype(F32)
        if depth:
            (picked,) = pick_rows(target_in_ref[b], back_ref)
            picked_ref[b] = picked.astype(picked_ref.dtype)
            x = x + gate_in_ref[b][:, 0:1] * picked
            x_out_ref[b] = x
        xs.append(x)
    for b in some:
        unit, _ = norm_parts(xs[b])
        normed = (unit * g1_ref[depth : depth + 1] + s1_ref[depth : depth + 1]).astype(BF16)
        a_ref[b] = mm(perm_ref[...], normed).astype(BF16)
    qkv = mm(a_ref[...].reshape(len(some) * WROWS, D), attend_ref[0]).astype(BF16)
    qkv_ref[...] = qkv.reshape(len(some), WROWS, 3 * D)
    masks = head_masks()
    runs = window_items(some)
    ready = raw_scores(qkv_ref, runs[0], masks)
    for at, items in enumerate(runs):
        _, scores = ready
        if at + 1 < len(runs):
            ready = raw_scores(qkv_ref, runs[at + 1], masks)
        probs = to_probs(items, scores, bias_ref, mask_ref)
        tall = []
        for (w, g, b), p in zip(items, probs):
            rows = slice(w * LPAD, (w + 1) * LPAD)
            tall.append(mm(p.astype(BF16), qkv_ref[b, rows, group_cols(2, g)], TN))
        for (w, g, b), t in zip(items, tall):
            rows = slice(w * LPAD, (w + 1) * LPAD)
            mixed_ref[b, rows, group_cols(0, g)] = fold_heads(t, masks).astype(BF16)
    lane = lax.broadcasted_iota(jnp.int32, (HW, LANES), 1)
    for b in some:
        mixed = mm(perm_back_ref[...], mixed_ref[b]).astype(BF16)
        mid = xs[b] + mm(mixed, out_w_ref[0])
        mid_ref[b] = mid
        unit, _ = norm_parts(mid)
        n = (unit * g2_ref[depth : depth + 1] + s2_ref[depth : depth + 1]).astype(BF16)
        n_ref[b] = n
        logits = jnp.where(lane < EXPERTS, mm(n, router_ref[0]), pad_fill)
        raised = jnp.exp(logits - jnp.max(logits, axis=-1, keepdims=True))
        router = raised / jnp.sum(raised, axis=-1, keepdims=True)
        probs_ref[b] = router
        chosen = lane == as_column(route_ref[b], HW)
        gate = jnp.sum(jnp.where(chosen, router, 0.0), axis=-1, keepdims=True)
        gate_ref[b] = jnp.broadcast_to(gate, (HW, LANES))
        at = step * len(some) + b
        rows_ref[pl.ds(at, 1), 0:HW, 0:D] = n[None]
        if last:
            dy = (gate * cot_ref[b].astype(F32)).astype(BF16)
            rows_ref[pl.ds(at, 1), 0:HW, D : 2 * D] = dy[None]

    @pl.when(step == pl.num_programs(0) - 1)
    def _():
        rows = rows_ref[...].reshape(images * TPAD, rows_ref.shape[2])
        send_rows(out_refs, target_ref[...], rows)


def whole(shape):
    return pl.BlockSpec(shape, lambda i: (0,) * len(shape))


def images_of(images):
    return STEP_IMAGES if images % STEP_IMAGES == 0 else 1


def by_image(shape):
    return pl.BlockSpec(
        (images_of(shape[0]),) + shape[1:], lambda i: (i,) + (0,) * (len(shape) - 1)
    )


def layer_of(shape, depth):
    return pl.BlockSpec((1,) + shape[1:], lambda i: (depth,) + (0,) * (len(shape) - 1))


def run_forward(depth, x, earlier, cotangent, route_rows, target_rows, target_all, shared):
    images = x.shape[0]
    last = depth == LAYERS - 1
    args, specs = [x], [by_image(x.shape)]
    if depth:
        back, gate_in, target_in, picked_type = earlier
        args += [back, gate_in, target_in]
        specs += [whole(back.shape), by_image(gate_in.shape), by_image(target_in.shape)]
    if last:
        args.append(cotangent)
        specs.append(by_image(cotangent.shape))
    args += [route_rows, target_all]
    specs += [by_image(route_rows.shape), whole(target_all.shape)]
    for name in ("first_gain", "first_shift", "second_gain", "second_shift"):
        args.append(shared[name])
        specs.append(whole(shared[name].shape))
    for name in ("attend_weight", "output_weight", "router"):
        args.append(shared[name])
        specs.append(layer_of(shared[name].shape, depth))
    for name in ("bias", "mask", "perm", "perm_back"):
        args.append(shared[name][depth])
        specs.append(whole(shared[name][depth].shape))
    outs = [
        ((images, WROWS, 3 * D), BF16),
        ((images, WROWS, D), BF16),
        ((images, WROWS, D), BF16),
        ((images, HW, D), F32),
        ((images, HW, D), BF16),
        ((images, HW, LANES), F32),
        ((images, HW, LANES), F32),
    ]
    out_specs = [by_image(s) for s, _ in outs]
    if depth:
        outs += [((images, HW, D), F32), ((images, HW, D), picked_type)]
        out_specs += [by_image((images, HW, D))] * 2
    count = 2 if last else 1
    sent = count * D
    outs += [((SLOTS, D), BF16)] * count
    out_specs += [whole((SLOTS, D))] * count
    scratch = [pltpu.VMEM((images, TPAD, sent), BF16)]
    results = pl.pallas_call(
        partial(forward_kernel, depth, images),
        grid=(images // images_of(images),),
        in_specs=specs,
        out_specs=out_specs,
        out_shape=[in_hbm(s, t) for s, t in outs[:-count]]
        + [jax.ShapeDtypeStruct(s, t) for s, t in outs[-count:]],
        scratch_shapes=scratch,
        compiler_params=pltpu.CompilerParams(vmem_limit_bytes=VMEM_BYTES),
        cost_estimate=cost(24 if last else 18),
        name="forward_%d" % depth,
    )(*args)
    return results[:-count], results[-count:]


def joined(ref, columns=slice(None)):
    return jnp.concatenate([ref[s, 0, :, columns] for s in range(ref.shape[0])], axis=0)


def spread(ref, value, columns=slice(None)):
    for s in range(ref.shape[0]):
        ref[s, 0, :, columns] = value[s * ROWS : (s + 1) * ROWS]


def hidden_tiles(width):
    tile = FTILE if width % FTILE == 0 else FCHUNK
    return [slice(f, f + tile) for f in range(0, width, tile)]


def expert_forward_kernel(aliased, n_ref, up_ref, down_ref, *refs):
    y_ref, hidden_ref = refs[aliased:]
    n = joined(n_ref)
    tiles = hidden_tiles(up_ref.shape[2])
    ready = mm(n, up_ref[0, :, tiles[0]])
    for at, tile in enumerate(tiles):
        u = ready
        if at + 1 < len(tiles):
            ready = mm(n, up_ref[0, :, tiles[at + 1]])
        hidden_ref[:, tile] = gelu_parts(u)[0].astype(BF16)
    spread(y_ref, mm(hidden_ref[...], down_ref[0]).astype(BF16))


def by_sources(array, first=0):
    return pl.BlockSpec((SOURCES, 1) + array.shape[2:], lambda k, i: (i, first + k, 0, 0))


def run_expert_forward(arrived, up, down, which=None, earlier=None):
    total, width = up.shape[0], up.shape[2]
    first = which or 0
    weight_spec = lambda shape: pl.BlockSpec((1,) + shape[1:], lambda k, i: (k, 0, 0))
    args = [arrived, from_hbm(up), from_hbm(down)]
    specs = [by_sources(arrived, first), weight_spec(up.shape), weight_spec(down.shape)]
    aliases = {}
    if earlier is not None:
        args.append(earlier)
        specs.append(pl.BlockSpec(memory_space=pl.ANY))
        aliases = {3: 0}
    steps = total if which is None else 1
    return pl.pallas_call(
        partial(expert_forward_kernel, len(aliases)),
        grid=(steps, arrived.shape[0] // SOURCES),
        in_specs=specs,
        out_specs=by_sources(arrived, first),
        out_shape=jax.ShapeDtypeStruct(arrived.shape, BF16),
        scratch_shapes=[pltpu.VMEM((SOURCES * ROWS, width), BF16)],
        input_output_aliases=aliases,
        compiler_params=pltpu.CompilerParams(vmem_limit_bytes=EXPERT_VMEM),
        cost_estimate=cost(4 * steps),
        name="expert_forward",
    )(*args)


def expert_both_kernel(total, *refs):
    n_ref, dy_ref, ups, downs = refs[0], refs[1], refs[2 : 2 + total], refs[2 + total : 2 + 2 * total]
    dn_ref, hidden_ref, du_ref = refs[2 + 2 * total :]

    def work(up_ref, down_ref):
        n, dy = joined(n_ref), joined(dy_ref)
        tiles = hidden_tiles(up_ref.shape[2])

        def first(tile):
            return mm(n, up_ref[0, :, tile]), mm(dy, down_ref[0, tile], NT)

        ready = first(tiles[0])
        for at, tile in enumerate(tiles):
            u, dh = ready
            if at + 1 < len(tiles):
                ready = first(tiles[at + 1])
            value, slope = gelu_parts(u)
            hidden_ref[0, :, tile] = value.astype(BF16)
            du_ref[0, :, tile] = (dh * slope).astype(BF16)
        spread(dn_ref, mm(du_ref[0], up_ref[0], NT).astype(BF16))

    if total == 1:
        work(ups[0], downs[0])
    else:
        for k in range(total):
            pl.when(pl.program_id(0) == k)(partial(work, ups[k], downs[k]))


def run_expert_both(n, dy, ups, downs):
    total, width = len(ups), ups[0].shape[2]
    wide = in_hbm((total, n.shape[0] * ROWS, width), BF16)
    wide_spec = pl.BlockSpec((1, SOURCES * ROWS, width), lambda k, i: (k, i, 0))
    weights = [*ups, *downs]
    return pl.pallas_call(
        partial(expert_both_kernel, total),
        grid=(total, n.shape[0] // SOURCES),
        in_specs=[by_sources(n), by_sources(dy)]
        + [
            pl.BlockSpec(w.shape, lambda k, i: (0, 0, 0), pipeline_mode=pl.Buffered(1))
            for w in weights
        ],
        out_specs=[by_sources(n), wide_spec, wide_spec],
        out_shape=[jax.ShapeDtypeStruct(n.shape, BF16), wide, wide],
        compiler_params=pltpu.CompilerParams(vmem_limit_bytes=EXPERT_VMEM),
        cost_estimate=cost(6 * total),
        name="expert_both",
    )(n, dy, *weights)


def expert_weights_kernel(order, *refs):
    if order:
        order_ref, refs = refs[0], refs[1:]
    n_ref, dy_ref, hidden_ref, du_ref, refs = *refs[:4], refs[4:]
    if order:
        keep_ref, send_ref, refs = refs[0], refs[1], refs[2:]
    else:
        out_ref, refs = refs[0], refs[1:]
    n_rows, dy_rows, sum_ref = refs
    k = pl.program_id(1)

    @pl.when(pl.program_id(0) == 0)
    def _():
        for s in range(n_ref.shape[0]):
            rows = slice(s * ROWS, (s + 1) * ROWS)
            n_rows[k, rows] = n_ref[s, k]
            dy_rows[k, rows] = dy_ref[s, k]

    up = mm(n_rows[k], du_ref[0], TN)
    down = mm(hidden_ref[0], dy_rows[k], TN)
    sum_ref[0:D] = up
    sum_ref[D : 2 * D] = down
    if order:
        spread_experts(order_ref, sum_ref, keep_ref, send_ref)
    else:
        out_ref[0] = sum_ref[...].astype(BF16)


def spread_experts(order_ref, sum_ref, keep_ref, send_ref):
    run = sum_ref.shape[0] // BLOCK // 4
    for j in range(4 * run):
        start = pl.multiple_of(jnp.bitwise_xor(order_ref[0], j) * BLOCK, BLOCK)
        block = sum_ref[pl.ds(start, BLOCK)].astype(BF16)
        ref = keep_ref if j < 2 * run else send_ref
        at = j % run * BLOCK
        ref[j // run % 2, 0, at : at + BLOCK] = block


def spread_blocks(order_ref, sum_ref, keep_ref, send_ref, columns):
    count = sum_ref.shape[0] // BLOCK
    for j in range(count):
        start = pl.multiple_of(jnp.bitwise_xor(order_ref[0], j) * BLOCK, BLOCK)
        block = sum_ref[pl.ds(start, BLOCK)].astype(BF16)
        ref = keep_ref if j < count // 2 else send_ref
        at = (j % (count // 2)) * BLOCK
        ref[at : at + BLOCK, columns] = block


def run_expert_weights(n, dy, hidden, du, order=None):
    total, rows, width = hidden.shape
    specs = [
        pl.BlockSpec(array.shape, lambda f, k: (0, 0, 0, 0), pipeline_mode=pl.Buffered(1))
        for array in (n, dy)
    ]
    if order is None:
        shape = [jax.ShapeDtypeStruct((total, 2 * D, width), BF16)]
        out_specs = [pl.BlockSpec((1, 2 * D, FCHUNK), lambda f, k: (k, 0, f))]
        leading = []
    else:
        shape = [jax.ShapeDtypeStruct((2, total, D // 2, width), BF16)] * 2
        out_specs = [pl.BlockSpec((2, 1, D // 2, FCHUNK), lambda f, k: (0, k, 0, f))] * 2
        leading = [order]
    wide_spec = pl.BlockSpec((1, rows, FCHUNK), lambda f, k: (k, 0, f))
    results = pl.pallas_call(
        partial(expert_weights_kernel, order is not None),
        grid=(width // FCHUNK, total),
        in_specs=[pl.BlockSpec(memory_space=pltpu.SMEM)] * len(leading)
        + specs
        + [wide_spec] * 2,
        out_specs=out_specs,
        out_shape=shape,
        scratch_shapes=[pltpu.VMEM((total, rows, D), BF16)] * 2
        + [pltpu.VMEM((2 * D, FCHUNK), F32)],
        compiler_params=pltpu.CompilerParams(vmem_limit_bytes=EXPERT_VMEM + 8 * 1024 * 1024),
        cost_estimate=cost(4 * total),
        name="expert_weights",
    )(*leading, n, dy, from_hbm(hidden), from_hbm(du))
    if order is None:
        return results[0][0]
    return [r.reshape(total * D, width) for r in results]


def backward_kernel(depth, images, order, part, parts, *refs):
    last = depth == LAYERS - 1
    refs = list(refs)
    take = lambda: refs.pop(0)
    if order:
        order_ref = take()
    g_ref, back_ref = take(), take()
    if last:
        y_ref = take()
        before_gate_ref, before_target_ref = take(), take()
    else:
        picked_ref = take()
    (x_ref, qkv_ref, a_ref, mixed_ref, mid_ref, n_ref, probs_ref, gate_ref) = refs[:8]
    (route_ref, target_ref, g1_ref, g2_ref, attend_ref, out_w_ref) = refs[8:14]
    (router_ref, bias_ref, mask_ref, perm_ref, perm_back_ref) = refs[14:19]
    refs = refs[19:]
    earlier = {}
    if part:
        earlier["mats"] = [take() for _ in range(2 if order else 1)]
        earlier["sums"] = [take(), take()]
        if last:
            earlier["dy"] = [take() for _ in range(part)]
        take()
        if last:
            take()
    g_out_ref = take()
    mats_refs = [take() for _ in range(2 if order else 1)]
    vecs_ref, table_ref = take(), take()
    if last:
        result_ref, dy_out_ref = take(), take()
    attend_acc, out_acc, dqkv_ref, dz_ref = (take() for _ in range(4))
    if last:
        dy_rows_ref = take()

    step = pl.program_id(0)

    @pl.when(step == 0)
    def _():
        attend_acc[...] = jnp.zeros_like(attend_acc)
        out_acc[...] = jnp.zeros_like(out_acc)
        if part:
            vecs_ref[...] = earlier["sums"][0][...]
            table_ref[...] = earlier["sums"][1][...]
        else:
            vecs_ref[...] = jnp.zeros_like(vecs_ref)
            table_ref[...] = jnp.zeros_like(table_ref)
        if last:
            dy_rows_ref[...] = jnp.zeros_like(dy_rows_ref)

    some = range(g_ref.shape[0])
    lane = lax.broadcasted_iota(jnp.int32, (HW, LANES), 1)
    grad_mids, dmixed_all = [], []
    for b in some:
        grad = g_ref[b].astype(F32)
        mid = mid_ref[b]
        gate = gate_ref[b][:, 0:1]
        if last:
            rows_back, picked = pick_rows(target_ref[b], back_ref, y_ref)
            result_ref[b] = (mid + gate * picked).astype(BF16)
        else:
            (rows_back,) = pick_rows(target_ref[b], back_ref)
            picked = picked_ref[b].astype(F32)
        gate_grad = jnp.sum(grad * picked, axis=-1, keepdims=True)
        chosen = jnp.where(lane == as_column(route_ref[b], HW), 1.0, 0.0)
        logit_grad = ((gate * gate_grad) * (chosen - probs_ref[b])).astype(BF16)
        router_grad = mm(logit_grad, n_ref[b], TN)
        grad_n = rows_back + mm(logit_grad, router_ref[0], NT)
        unit, inverse = norm_parts(mid)
        vecs_ref[2:3] += jnp.sum(grad_n * unit, axis=0, keepdims=True)
        vecs_ref[3:4] += jnp.sum(grad_n, axis=0, keepdims=True)
        vecs_ref[8:16] += router_grad[0:8]
        grad_mid = grad + norm_back(grad_n, unit, inverse, g2_ref[depth : depth + 1])
        grad_mids.append(grad_mid)
        dz = mm(perm_ref[...], grad_mid.astype(BF16)).astype(BF16)
        dz_ref[b] = dz
    dz = dz_ref[...].reshape(len(some) * WROWS, D)
    out_acc[...] += mm(mixed_ref[...].reshape(len(some) * WROWS, D), dz, TN)
    dmixed_all = mm(dz, out_w_ref[0], NT).astype(BF16)
    masks = head_masks()
    def first_part(items):
        dm_wide, dprobs = [], []
        for w, g, b in items:
            start = b * WROWS + w * LPAD
            dm_wide.append(
                spread_heads(dmixed_all[start : start + LPAD, group_cols(0, g)], masks)
            )
        for (w, g, b), dm in zip(items, dm_wide):
            rows = slice(w * LPAD, (w + 1) * LPAD)
            dprobs.append(mm(qkv_ref[b, rows, group_cols(2, g)], dm, NT))
        return raw_scores(qkv_ref, items, masks) + (dm_wide, dprobs)

    runs = window_items(some)
    ready = first_part(runs[0])
    for at, items in enumerate(runs):
        places = [(b, slice(w * LPAD, (w + 1) * LPAD), g) for w, g, b in items]
        q_wide, scores, dm_wide, dprobs = ready
        if at + 1 < len(runs):
            ready = first_part(runs[at + 1])
        probs = to_probs(items, scores, bias_ref, mask_ref)
        dscores, tables = [], {}
        for (b, rows, g), p, dp in zip(places, probs, dprobs):
            row_dot = jnp.sum(p * dp, axis=0, keepdims=True)
            dscores.append((p * (dp - row_dot)).astype(BF16))
            wide = dscores[-1].astype(F32)
            tables[g] = tables[g] + wide if g in tables else wide
        for g, total in tables.items():
            table_ref[:, g * GW : (g + 1) * GW] += total
        dv, dk, tall = [], [], []
        for p, dm in zip(probs, dm_wide):
            dv.append(mm(p.astype(BF16), dm))
        for ds, q in zip(dscores, q_wide):
            dk.append(mm(ds, q))
        for (b, rows, g), ds in zip(places, dscores):
            tall.append(mm(ds, qkv_ref[b, rows, group_cols(1, g)], TN))
        for i, (b, rows, g) in enumerate(places):
            dq = fold_heads(tall[i], masks) * score_scale
            dqkv_ref[b, rows, group_cols(0, g)] = dq.astype(BF16)
            dqkv_ref[b, rows, group_cols(1, g)] = (dk[i] * score_scale).astype(BF16)
            dqkv_ref[b, rows, group_cols(2, g)] = dv[i].astype(BF16)
    dqkv = dqkv_ref[...].reshape(len(some) * WROWS, 3 * D)
    attend_acc[...] += mm(a_ref[...].reshape(len(some) * WROWS, D), dqkv, TN)
    for b in some:
        dqkv_tokens = mm(perm_back_ref[...], dqkv_ref[b]).astype(BF16)
        grad_normed = mm(dqkv_tokens, attend_ref[0], NT)
        unit, inverse = norm_parts(x_ref[b].astype(F32))
        vecs_ref[0:1] += jnp.sum(grad_normed * unit, axis=0, keepdims=True)
        vecs_ref[1:2] += jnp.sum(grad_normed, axis=0, keepdims=True)
        grad_x = grad_mids[b] + norm_back(grad_normed, unit, inverse, g1_ref[depth : depth + 1])
        g_out_ref[b] = grad_x.astype(g_out_ref.dtype)
        if last:
            dy = (before_gate_ref[b][:, 0:1] * grad_x).astype(BF16)
            dy_rows_ref[pl.ds(step * len(some) + b, 1), 0:HW, :] = dy[None]

    @pl.when(step == pl.num_programs(0) - 1)
    def _():
        for acc, columns in ((attend_acc, slice(0, 3 * D)), (out_acc, slice(3 * D, 4 * D))):
            if order:
                spread_blocks(order_ref, acc, *mats_refs, columns)
            else:
                mats_refs[0][:, columns] = acc[...].astype(BF16)
        if part:
            for mats_ref, before in zip(mats_refs, earlier["mats"]):
                total = mats_ref[...].astype(F32) + before[...].astype(F32)
                mats_ref[...] = total.astype(BF16)
        if last:
            if part < parts - 1:
                dy_out_ref[...] = dy_rows_ref[...]
            else:
                runs = [ref[...] for ref in earlier.get("dy", [])] + [dy_rows_ref[...]]
                rows = jnp.concatenate([run.reshape(-1, D) for run in runs], axis=0)
                send_rows([dy_out_ref], before_target_ref[...], rows)


def run_backward(
    depth, grad, back, extra, saved, route_rows, target_rows, shared, order=None, before=()
):
    images = grad.shape[0]
    some = images_of(images)
    part, parts = len(before), BACKWARD_CALLS
    steps = images // some // parts
    last = depth == LAYERS - 1

    def by_image(shape):
        return pl.BlockSpec(
            (some,) + shape[1:], lambda i: (part * steps + i,) + (0,) * (len(shape) - 1)
        )

    args, specs = [], []
    if order is not None:
        args.append(order)
        specs.append(pl.BlockSpec(memory_space=pltpu.SMEM))
    args += [grad, back]
    specs += [by_image(grad.shape), whole(back.shape)]
    if last:
        y_back, before_gate, before_target = extra
        args += [y_back, before_gate, before_target]
        specs += [whole(y_back.shape), by_image(before_gate.shape), whole(before_target.shape)]
    else:
        args.append(extra)
        specs.append(by_image(extra.shape))
    for array in saved + [route_rows, target_rows]:
        args.append(array)
        specs.append(by_image(array.shape))
    for name in ("first_gain", "second_gain"):
        args.append(shared[name])
        specs.append(whole(shared[name].shape))
    for name in ("attend_weight", "output_weight", "router"):
        args.append(shared[name])
        specs.append(layer_of(shared[name].shape, depth))
    for name in ("bias", "mask", "perm", "perm_back"):
        args.append(shared[name][depth])
        specs.append(whole(shared[name][depth].shape))
    token_shape = (images, HW, D)
    outs = [(token_shape, F32 if last else BF16, by_image(token_shape))]
    if order is None:
        outs.append(((D, 4 * D), BF16, whole((D, 4 * D))))
    else:
        outs += [((D // 2, 4 * D), BF16, whole((D // 2, 4 * D)))] * 2
    mats = len(outs) - 1
    outs += [
        ((16, D), F32, whole((16, D))),
        ((LPAD, GROUPS * GW), F32, whole((LPAD, GROUPS * GW))),
    ]
    aliases = {}
    if last:
        outs.append((token_shape, BF16, by_image(token_shape)))
        shape = (SLOTS, D) if part == parts - 1 else (steps * some, TPAD, D)
        outs.append((shape, BF16, whole(shape)))
    if part:
        near = before[-1]
        plain = list(near[1 : 3 + mats])
        if last:
            plain += [results[-1] for results in before]
        args += plain
        specs += [whole(array.shape) for array in plain]
        for at in (0, 3 + mats) if last else (0,):
            aliases[len(args)] = at
            args.append(near[at])
            specs.append(pl.BlockSpec(memory_space=pl.ANY))
    scratch = [
        pltpu.VMEM((D, 3 * D), F32),
        pltpu.VMEM((D, D), F32),
        pltpu.VMEM((some, WROWS, 3 * D), BF16),
        pltpu.VMEM((some, WROWS, D), BF16),
    ]
    if last:
        scratch.append(pltpu.VMEM((steps * some, TPAD, D), BF16))
    return pl.pallas_call(
        partial(backward_kernel, depth, images, order is not None, part, parts),
        grid=(steps,),
        in_specs=specs,
        out_specs=[o[2] for o in outs],
        out_shape=[jax.ShapeDtypeStruct(o[0], o[1]) for o in outs],
        scratch_shapes=scratch,
        input_output_aliases=aliases,
        compiler_params=pltpu.CompilerParams(vmem_limit_bytes=VMEM_BYTES),
        cost_estimate=cost((33 if last else 24) / parts),
        name="backward_%d" % depth,
    )(*args)


def bits_of(axis, low, high):
    steps = []
    bit = low
    while bit < high:
        steps.append((axis, bit))
        bit *= 2
    return steps


def swap(x, step):
    axis, bit = step
    size = lax.axis_size(axis)
    return lax.ppermute(x, axis, [(i, i ^ bit) for i in range(size)])


def bit_at(step):
    axis, bit = step
    return (lax.axis_index(axis) // bit) % 2


def halved(rows, steps, least):
    count = 0
    while count < len(steps) and rows % 2 == 0 and rows // 2 >= least:
        rows //= 2
        count += 1
    return count


def sum_over(x, steps, least=24):
    count = halved(x.shape[0], steps, least)
    x = sum_all(scatter_sum(x, steps[:count]), steps[count:])
    return gather_all(x, steps[:count])


def scatter_sum(x, steps):
    for step in steps:
        half = x.shape[0] // 2
        mine = bit_at(step)
        keep = lax.dynamic_slice_in_dim(x, mine * half, half, 0)
        away = lax.dynamic_slice_in_dim(x, (1 - mine) * half, half, 0)
        x = (keep.astype(F32) + swap(away, step).astype(F32)).astype(x.dtype)
    return x


def gather_all(x, steps, dim=0):
    for step in reversed(steps):
        other = swap(x, step)
        mine = bit_at(step)
        first = jnp.where(mine == 0, x, other)
        second = jnp.where(mine == 0, other, x)
        x = jnp.concatenate([first, second], axis=dim)
    return x


def sum_all(x, steps):
    for step in steps:
        x = (x.astype(F32) + swap(x, step).astype(F32)).astype(x.dtype)
    return x


def exchange(rows, team):
    groups = lax.axis_size("expert")
    teams, size = None, groups
    if team:
        teams = [list(range(first, first + team)) for first in range(0, groups, team)]
        size = team
    width = rows.shape[-1]
    runs = rows.reshape(size, -1, width)
    runs = lax.all_to_all(
        runs, "expert", split_axis=0, concat_axis=0, tiled=True, axis_index_groups=teams
    )
    return runs.reshape(size, -1, ROWS, width)


def to_experts(rows, slices, team):
    if slices > 1:
        runs = rows.reshape(EXPERTS, ROWS, rows.shape[1])
        rows = jnp.repeat(runs, slices, axis=0)
    return exchange(rows, team)


def from_experts(rows, slices, team):
    width = rows.shape[-1]
    rows = exchange(rows, team).reshape(EXPERTS, slices, ROWS, width)
    return rows.transpose(1, 0, 2, 3).reshape(slices, SLOTS, width)


def unpack_down(packed):
    width = packed.shape[1]
    return jnp.concatenate(
        [packed[:, j * D : (j + 1) * D] for j in range(width // D)], axis=0
    )


def add_kernel(cuts, keep_ref, got_ref, *outs):
    total = keep_ref[...].astype(F32) + got_ref[...].astype(F32)
    for (start, stop), out in zip(cuts, outs):
        out[...] = total[start:stop].astype(out.dtype)


def add_rows(keep, got, cuts):
    rows, width = got.shape
    return pl.pallas_call(
        partial(add_kernel, cuts),
        grid=(1,),
        in_specs=[pl.BlockSpec((rows, width), lambda i: (0, 0))] * 2,
        out_specs=[pl.BlockSpec((b - a, width), lambda i: (0, 0)) for a, b in cuts],
        out_shape=[jax.ShapeDtypeStruct((b - a, width), keep.dtype) for a, b in cuts],
        compiler_params=pltpu.CompilerParams(vmem_limit_bytes=12 * 1024 * 1024),
        cost_estimate=cost(1),
        name="add_rows",
    )(keep, got)


def add_pair_kernel(keep_ref, got_ref, partner_ref, own_ref, first_ref, second_ref):
    own = (keep_ref[...].astype(F32) + got_ref[...].astype(F32)).astype(BF16)
    own_ref[...] = own
    total = (own.astype(F32) + partner_ref[...].astype(F32)).astype(BF16)
    rows = first_ref.shape[0]
    first_ref[...] = total[0:rows]
    second_ref[...] = total[rows:]


def add_pair(keep, got, partner):
    rows, width = keep.shape
    return pl.pallas_call(
        add_pair_kernel,
        out_shape=[
            jax.ShapeDtypeStruct((count, width), BF16) for count in (rows, rows // 2, rows // 2)
        ],
        compiler_params=pltpu.CompilerParams(vmem_limit_bytes=12 * 1024 * 1024),
        cost_estimate=cost(1),
        name="add_pair",
    )(keep, got, partner)


def add_halves_kernel(own_ref, low_ref, high_ref, out_ref):
    rows = low_ref.shape[0]
    for at, other in ((0, low_ref), (rows, high_ref)):
        total = own_ref[at : at + rows].astype(F32) + other[...].astype(F32)
        out_ref[at : at + rows] = total.astype(BF16)


def add_halves(own, low, high):
    return pl.pallas_call(
        add_halves_kernel,
        out_shape=jax.ShapeDtypeStruct(own.shape, BF16),
        compiler_params=pltpu.CompilerParams(vmem_limit_bytes=12 * 1024 * 1024),
        cost_estimate=cost(1),
        name="add_halves",
    )(own, low, high)


def join_kernel(first_ref, second_ref, out_ref):
    rows = first_ref.shape[0]
    out_ref[0:rows] = first_ref[...]
    out_ref[rows:] = second_ref[...]


def join_rows(first, second):
    rows, width = first.shape
    return pl.pallas_call(
        join_kernel,
        out_shape=jax.ShapeDtypeStruct((2 * rows, width), first.dtype),
        compiler_params=pltpu.CompilerParams(vmem_limit_bytes=8 * 1024 * 1024),
        cost_estimate=cost(1),
        name="join_rows",
    )(first, second)


def pack_kernel(order_ref, up_a, up_b, down_a, down_b, up_ref, down_ref, quarter_ref, rows_ref):
    up = (up_a[0].astype(F32) + up_b[0].astype(F32)).astype(BF16)
    down = (down_a[0].astype(F32) + down_b[0].astype(F32)).astype(BF16)
    up_ref[...] = up
    down_ref[...] = down
    step, steps = pl.program_id(0), pl.num_programs(0)
    some, width = up.shape
    rows_ref[pl.ds(pl.multiple_of(step * some, some), some)] = up
    for c in range(down.shape[0] // D):
        rows_ref[D : 2 * D, c * D : (c + 1) * D] = down[c * D : (c + 1) * D]

    @pl.when(step == steps - 1)
    def _():
        quarter = quarter_ref.shape[0]
        start = pl.multiple_of(order_ref[0] * quarter, quarter)
        quarter_ref[...] = rows_ref[pl.ds(start, quarter)]


def pack_weights(depth, order, core_up, residual_up, core_down, residual_down):
    width = residual_up.shape[2]
    arrays = [core_up, residual_up, core_down, residual_down]
    shapes = [(D, width), (width, D), (D // 2, width)]
    return pl.pallas_call(
        pack_kernel,
        grid=(1,),
        in_specs=[pl.BlockSpec(memory_space=pltpu.SMEM)]
        + [layer_of(array.shape, depth) for array in arrays],
        out_specs=[whole(shape) for shape in shapes],
        out_shape=[in_hbm(shape, BF16) for shape in shapes],
        scratch_shapes=[pltpu.VMEM((2 * D, width), BF16)],
        compiler_params=pltpu.CompilerParams(vmem_limit_bytes=VMEM_BYTES),
        cost_estimate=cost(4),
        name="pack_weights",
    )(order, *map(from_hbm, arrays))


def unpack_kernel(order_ref, *refs):
    pieces, (up_ref, down_ref, rows_ref) = refs[:4], refs[4:]
    quarter = pieces[0].shape[0]
    for r, piece in enumerate(pieces):
        start = pl.multiple_of(jnp.bitwise_xor(order_ref[0], r) * quarter, quarter)
        rows_ref[pl.ds(start, quarter)] = piece[...]
    up_ref[0] = rows_ref[0:D]
    for c in range(down_ref.shape[1] // D):
        down_ref[0, c * D : (c + 1) * D] = rows_ref[D : 2 * D, c * D : (c + 1) * D]


def unpack_weights(order, pieces):
    width = pieces[0].shape[1]
    shapes = [(1, D, width), (1, width, D)]
    return pl.pallas_call(
        unpack_kernel,
        grid=(1,),
        in_specs=[pl.BlockSpec(memory_space=pltpu.SMEM)] + [whole(a.shape) for a in pieces],
        out_specs=[whole(shape) for shape in shapes],
        out_shape=[in_hbm(shape, BF16) for shape in shapes],
        scratch_shapes=[pltpu.VMEM((2 * D, width), BF16)],
        compiler_params=pltpu.CompilerParams(vmem_limit_bytes=EXPERT_VMEM),
        cost_estimate=cost(5),
        name="unpack_weights",
    )(order, *pieces)


def expert_outputs_kernel(earlier, plain, order_ref, *refs):
    pieces, refs = refs[:8], refs[8:]
    refs = refs[4 if earlier else 0 :]
    outs, (rows_ref,) = refs[:4], refs[4:]
    step = pl.program_id(0)
    quarter = pieces[0].shape[0]

    @pl.when(step == 0)
    def _():
        for kind in range(2):
            for r in range(4):
                rows_ref[kind, r * quarter : (r + 1) * quarter] = pieces[kind * 4 + r][...]

    half = pl.num_programs(0)
    for kind in range(2):
        for part in range(2):
            place = jnp.bitwise_xor(order_ref[0], step + part * half)
            if kind == 1 and not plain:
                place = place // 8 * 8 + place // 2 % 2 * 4 + place // 4 % 2 * 2 + place % 2
            start = pl.multiple_of(place * BLOCK, BLOCK)
            block = rows_ref[kind, pl.ds(start, BLOCK)].astype(F32)
            out = outs[kind * 2 + part]
            if part == 0:
                out[0] = block
            else:
                for c in range(out.shape[1]):
                    out[0, c] = block[:, c * D : (c + 1) * D]


def expert_outputs(depth, order, residual, core, earlier, plain=False):
    width = residual[0].shape[1]
    half = D // BLOCK
    count = width // D
    up = jax.ShapeDtypeStruct((LAYERS, D, width), F32)
    down = jax.ShapeDtypeStruct((LAYERS, count, D, D), F32)
    up_spec = pl.BlockSpec((1, BLOCK, width), lambda i: (depth, i, 0))
    down_spec = pl.BlockSpec((1, count, BLOCK, D), lambda i: (depth, 0, i, 0))
    pieces = residual + core
    specs = [pl.BlockSpec(residual[0].shape, lambda i: (0, 0))] * len(pieces)
    earlier = list(earlier or [])
    return pl.pallas_call(
        partial(expert_outputs_kernel, bool(earlier), plain),
        grid=(half,),
        in_specs=[pl.BlockSpec(memory_space=pltpu.SMEM)]
        + specs
        + [pl.BlockSpec(memory_space=pl.ANY)] * len(earlier),
        out_specs=[up_spec, down_spec] * 2,
        out_shape=[up, down] * 2,
        scratch_shapes=[pltpu.VMEM((2, 2 * D, width), BF16)],
        input_output_aliases={9 + i: i for i in range(len(earlier))},
        compiler_params=pltpu.CompilerParams(vmem_limit_bytes=32 * 1024 * 1024),
        cost_estimate=cost(4),
        name="expert_outputs",
    )(order, *pieces, *earlier)


def attend_outputs_kernel(earlier, order_ref, *refs):
    pieces, refs = refs[:2], refs[2:]
    refs = refs[2 if earlier else 0 :]
    attend_ref, out_ref, rows_ref = refs
    half = pieces[0].shape[0]
    for r in range(2):
        rows_ref[r * half : (r + 1) * half] = pieces[r][...].astype(F32)
    for j in range(D // BLOCK):
        start = pl.multiple_of(jnp.bitwise_xor(order_ref[0], j) * BLOCK, BLOCK)
        block = rows_ref[pl.ds(start, BLOCK)]
        attend_ref[0, j * BLOCK : (j + 1) * BLOCK] = block[:, : 3 * D]
        out_ref[0, j * BLOCK : (j + 1) * BLOCK] = block[:, 3 * D :]


def attend_outputs(depth, order, pieces, earlier):
    earlier = list(earlier or [])
    shapes = [(LAYERS, D, 3 * D), (LAYERS, D, D)]
    return pl.pallas_call(
        partial(attend_outputs_kernel, bool(earlier)),
        grid=(1,),
        in_specs=[pl.BlockSpec(memory_space=pltpu.SMEM)]
        + [whole(p.shape) for p in pieces]
        + [pl.BlockSpec(memory_space=pl.ANY)] * len(earlier),
        out_specs=[layer_of(shape, depth) for shape in shapes],
        out_shape=[jax.ShapeDtypeStruct(shape, F32) for shape in shapes],
        scratch_shapes=[pltpu.VMEM((D, 4 * D), F32)],
        input_output_aliases={3 + i: i for i in range(len(earlier))},
        compiler_params=pltpu.CompilerParams(vmem_limit_bytes=24 * 1024 * 1024),
        cost_estimate=cost(2),
        name="attend_outputs",
    )(order, *pieces, *earlier)


CORE, ROW = ("dp", 1), ("dp", 2)
NEAR_X, NEAR_Z, FAR_Z = ("expert", 1), ("expert", 2), ("expert", 4)


def place_order(steps):
    order = 0
    for step in steps:
        order = order * 2 + bit_at(step)
    return jnp.full((1,), order, jnp.int32)


class Steps:
    def run(self, *steps):
        for step in steps:
            getattr(self, step)()


class PairSum(Steps):
    def __init__(self, keep, send):
        self.keep, self.send = keep, send

    def core(self):
        self.send = swap(self.send, CORE)

    def add_core(self):
        rows = self.keep.shape[0] // 4
        cuts = tuple((i * rows, (i + 1) * rows) for i in range(4))
        self.own, self.partner, self.send, self.send_partner = add_rows(
            self.keep, self.send, cuts
        )
        del self.keep

    def row_own(self):
        self.send = swap(self.send, ROW)

    def row_partner(self):
        self.send_partner = swap(self.send_partner, ROW)

    def add_partner(self):
        rows = self.partner.shape[0]
        (self.partner,) = add_rows(self.partner, self.send_partner, ((0, rows),))
        del self.send_partner

    def add_own(self):
        self.own, self.total, self.send = add_pair(self.own, self.send, self.partner)

    def far(self):
        self.partner = swap(self.partner, FAR_Z)

    def add_far(self):
        (self.mine,) = add_rows(self.own, self.partner, ((0, self.own.shape[0]),))
        del self.own, self.partner

    def far_low(self):
        half = self.partner.shape[0] // 2
        self.got_low = swap(self.partner[:half], FAR_Z)

    def far_high(self):
        half = self.partner.shape[0] // 2
        self.got_high = swap(self.partner[half:], FAR_Z)

    def add_far_halves(self):
        self.mine = add_halves(self.own, self.got_low, self.got_high)
        del self.own, self.partner, self.got_low, self.got_high

    def residual_row(self):
        self.mine_row = swap(self.mine, ROW)

    def residual_core(self):
        self.mine_core = swap(self.mine, CORE)
        self.row_core = swap(self.mine_row, CORE)

    def residual_pieces(self):
        return [self.mine, self.mine_row, self.mine_core, self.row_core]

    def near_x(self):
        self.send = swap(self.send, NEAR_X)

    def add_near_x(self):
        rows = self.send.shape[0]
        cuts = ((0, rows // 2), (rows // 2, rows))
        self.total, self.send = add_rows(self.total, self.send, cuts)

    def near_z(self):
        self.send = swap(self.send, NEAR_Z)

    def add_near_z(self):
        (self.total,) = add_rows(self.total, self.send, ((0, self.send.shape[0]),))
        self.send = self.total

    def far_z(self):
        self.send = swap(self.send, FAR_Z)

    def add_far_z(self):
        (self.total,) = add_rows(self.total, self.send, ((0, self.send.shape[0]),))

    def back_z(self):
        self.send = swap(self.total, NEAR_Z)

    def back_row(self):
        self.total = join_rows(self.total, self.send)
        self.send = swap(self.total, ROW)

    def back_x(self):
        self.total = join_rows(self.total, self.send)
        self.send = swap(self.total, NEAR_X)

    def back_core(self):
        self.total_core = swap(self.total, CORE)
        self.send_core = swap(self.send, CORE)

    def core_pieces(self):
        return [self.total, self.send, self.total_core, self.send_core]


class AttendSum(Steps):
    def __init__(self, keep, send):
        self.keep, self.send = keep, send

    def core(self):
        self.send = swap(self.send, CORE)

    def add_half(self):
        rows = self.send.shape[0] // 2
        cuts = ((0, rows), (rows, 2 * rows))
        self.keep, self.send = add_rows(self.keep, self.send, cuts)

    def row(self):
        self.send = swap(self.send, ROW)

    def near_x(self):
        self.send = swap(self.send, NEAR_X)

    def add(self):
        (self.keep,) = add_rows(self.keep, self.send, ((0, self.send.shape[0]),))
        self.send = self.keep

    def near_z(self):
        self.send = swap(self.send, NEAR_Z)

    def far_z(self):
        self.send = swap(self.send, FAR_Z)

    def back_x(self):
        self.send = swap(self.keep, NEAR_X)

    def back_row(self):
        self.keep = join_rows(self.keep, self.send)
        self.send = swap(self.keep, ROW)

    def back_core(self):
        self.keep = join_rows(self.keep, self.send)
        self.send = swap(self.keep, CORE)

    def pieces(self):
        return [self.keep, self.send]


class SmallSum(Steps):
    def __init__(self, value):
        self.value = value

    def swap(self, step):
        self.send = swap(self.value, step)

    def add(self):
        self.value = self.value + self.send


def at_once(values, *objects):
    fields = [
        (o, name)
        for o in objects
        for name, field in vars(o).items()
        if isinstance(field, jax.Array)
    ]
    held = [getattr(o, name) for o, name in fields]
    values, held = lax.optimization_barrier((tuple(values), held))
    for (o, name), field in zip(fields, held):
        setattr(o, name, field)
    return values


def after(value, *done):
    return lax.optimization_barrier((value,) + done)[0]


def body(
    block_input,
    routes,
    first_gain,
    first_shift,
    attend_weight,
    bias_table,
    output_weight,
    second_gain,
    second_shift,
    router_weight,
    core_up,
    core_down,
    residual_up,
    residual_down,
    cotangent,
):
    groups = lax.axis_size("expert")
    slices = groups // EXPERTS
    group_part = lax.axis_index("expert") % slices
    images = block_input.shape[0]
    width = residual_up.shape[2]

    routes_rows = jnp.pad(
        routes.reshape(LAYERS, images, HW), ((0, 0), (0, 0), (0, TPAD - HW)), constant_values=-1
    )
    alone = slices == 1
    half = lax.axis_index("expert") // TEAM
    ups, downs, quarters = [], [], []
    dp_order = place_order((CORE, ROW)) if alone else None
    for d in range(LAYERS):
        if not alone:
            up = lax.dynamic_slice_in_dim(core_up[d], group_part * width, width, 1)
            down = lax.dynamic_slice_in_dim(core_down[d], group_part * width, width, 0)
            ups.append((up.astype(F32) + residual_up[d].astype(F32)).astype(BF16)[None])
            downs.append((down.astype(F32) + residual_down[d].astype(F32)).astype(BF16)[None])

    def pack(d, core_up):
        up, down, quarter = pack_weights(
            d, dp_order, core_up, residual_up, core_down, residual_down
        )
        ups.append(up)
        downs.append(down)
        quarters.append(quarter)

    teams = [TEAM if alone else 0] * LAYERS
    if alone:
        pack(0, core_up)
        routes_rows, bias_table = after((routes_rows, bias_table), quarters[0])
    targets = run_routing(routes_rows, jnp.full((1,), half, jnp.int32), teams)

    table_index = jnp.asarray(offset_table(), jnp.int32)
    picker = (jnp.arange(OFFSETS, dtype=jnp.int32)[:, None] == table_index[None, :]).astype(F32)
    flat_table = bias_table.transpose(0, 2, 1).reshape(LAYERS * HEADS, OFFSETS)
    bias = jnp.dot(flat_table, picker, precision=lax.Precision.HIGHEST)
    bias = (
        bias.reshape(LAYERS, HEADS, LPAD, LPAD)
        .transpose(0, 2, 1, 3)
        .reshape(LAYERS, LPAD, HEADS * LPAD)
    )
    offsets = [SHIFT * (depth % 2) for depth in range(LAYERS)]
    shared = {
        "first_gain": first_gain,
        "first_shift": first_shift,
        "second_gain": second_gain,
        "second_shift": second_shift,
        "attend_weight": attend_weight,
        "output_weight": output_weight,
        "router": jnp.pad(router_weight, ((0, 0), (0, 0), (0, LANES - EXPERTS))),
        "bias": [bias[depth] for depth in range(LAYERS)],
        "mask": [jnp.asarray(score_mask(o)) for o in offsets],
        "perm": [jnp.asarray(permutation(o), BF16) for o in offsets],
        "perm_back": [jnp.asarray(permutation(o).T, BF16) for o in offsets],
    }
    route_rows = [routes_rows[d].reshape(images, 1, TPAD) for d in range(LAYERS)]
    target_rows = [targets[d].reshape(images, 1, TPAD) for d in range(LAYERS)]
    target_all = [targets[d].reshape(1, images * TPAD) for d in range(LAYERS)]
    picked_type = BF16 if slices == 1 else F32
    saved, inner, gates, xs, picks = [], [], [], [block_input], []
    x, earlier = block_input, None
    dy_arrived = None
    def in_parts(rows):
        return [rows[i : i + PART] for i in range(0, rows.shape[0], PART)]

    for d in range(LAYERS):
        if alone:
            quarter = quarters[d]
            if d:
                quarter, back = lax.optimization_barrier((quarter, back))
                earlier = (back,) + earlier[1:]
            far = swap(quarter, FAR_Z)
            x = after(x, quarter)
        outs, outgoing = run_forward(
            d, x, earlier, cotangent, route_rows[d], target_rows[d], target_all[d], shared
        )
        qkv, a, mixed, mid, n, probs, gate = outs[:7]
        if d:
            xs.append(outs[7])
            picks.append(outs[8])
        if alone:
            *outgoing, far = lax.optimization_barrier((*outgoing, far))
            far_row = swap(far, ROW)
        arrived = to_experts(outgoing[0], slices, teams[d])
        if alone and d == 0:
            pack(1, after(core_up, outgoing[0]))
        if d == LAYERS - 1:
            dy_arrived = to_experts(outgoing[1], slices, teams[d])
        if alone:
            arrived, far, far_row = lax.optimization_barrier((arrived, far, far_row))
            pieces = [far, far_row, swap(far, CORE), swap(far_row, CORE)]
            ups[d], downs[d] = [ups[d][None]], [downs[d][None]]
            y = run_expert_forward(arrived, ups[d][0], downs[d][0], 0)
            up, down = unpack_weights(dp_order, pieces)
            ups[d].append(up)
            downs[d].append(down)
            y = run_expert_forward(arrived, up, down, 1, y)
        else:
            ups[d], downs[d] = [ups[d]], [downs[d]]
            y = run_expert_forward(arrived, ups[d][0], downs[d][0])
        if d == LAYERS - 1:
            y, dy_arrived = lax.optimization_barrier((y, dy_arrived))
        back = y_back = from_experts(y, slices, teams[d])
        earlier = (back, gate, target_rows[d], picked_type)
        x = mid
        gates.append(gate)
        saved.append([xs[d], qkv, a, mixed, mid, n, probs, gate])
        inner.append(arrived)

    grad = cotangent
    vecs, tables = [None] * 2, [None] * 2
    block_output = None
    expert_order = place_order((CORE, ROW, NEAR_X, NEAR_Z)) if alone else None
    attend_order = place_order((CORE, ROW, NEAR_X)) if alone else None
    expert_sums, attend_sums = [None] * 2, [None] * 2
    for d in reversed(range(LAYERS)):
        arrived = inner[d]
        dn, hidden, du = run_expert_both(arrived, dy_arrived, ups[d], downs[d])
        if alone:
            sums = [] if d else [expert_sums[1], attend_sums[1]]
            dn, hidden, du, y_back = at_once((dn, hidden, du, y_back), *sums)
        back = from_experts(dn, slices, teams[d])
        grads = run_expert_weights(arrived, dy_arrived, hidden, du, expert_order)
        expert_sums[d] = grads
        if alone:
            expert_sums[d] = PairSum(*grads)
        if alone and d == 0:
            expert_sums[0].run("core")
            expert_sums[1].run("add_own", "near_x")
            attend_sums[1].run("add_half", "row")
        if d == LAYERS - 1:
            extra = (y_back, gates[d - 1], target_all[d - 1])
        else:
            extra = picks[d]
        before = []
        for part in range(BACKWARD_CALLS):
            if alone:
                sums = expert_sums[1:] if d else expert_sums + [attend_sums[1]]
                grad, back, before = at_once((grad, back, before), *sums)
                if d:
                    expert_sums[1].run("core")
                else:
                    expert_sums[0].run("add_core", "row_partner", "row_own")
                    expert_sums[1].run("far", "add_near_x", "near_z")
                    attend_sums[1].run("add_half", "near_x")
            before = before + [
                run_backward(
                    d,
                    grad,
                    back,
                    extra,
                    saved[d],
                    route_rows[d],
                    target_rows[d],
                    shared,
                    attend_order,
                    before,
                )
            ]
        outs = before[-1]
        if alone:
            grad, keep, send, vecs[d], tables[d] = outs[:5]
            attend_sums[d] = AttendSum(keep, send)
            outs = outs[5:]
        else:
            grad, attend_sums[d], vecs[d], tables[d] = outs[:4]
            outs = outs[4:]
        if d == LAYERS - 1:
            block_output, dy_out = outs
            if alone:
                (dy_out,) = at_once((dy_out,), expert_sums[1], attend_sums[1])
                expert_sums[1].run("add_core", "row_partner")
                attend_sums[1].run("core")
            dy_arrived = to_experts(dy_out, slices, teams[0])
            if alone:
                (dy_arrived,) = at_once((dy_arrived,), expert_sums[1], attend_sums[1])
                expert_sums[1].run("add_partner", "row_own")
        elif alone:
            at_once((), *expert_sums, *attend_sums)
    input_grad = grad

    dp_steps = bits_of("dp", 1, lax.axis_size("dp"))
    slice_steps = bits_of("expert", 1, slices)
    sum_steps = bits_of("expert", slices, groups)
    all_steps = dp_steps + slice_steps + sum_steps
    table_grad = jnp.stack(tables).reshape(LAYERS, LPAD, HEADS, LPAD).transpose(0, 2, 1, 3)
    table_grad = jnp.dot(
        table_grad.reshape(LAYERS * HEADS, LPAD * LPAD), picker.T, precision=lax.Precision.HIGHEST
    )
    small = jnp.concatenate(
        [
            jnp.stack(vecs).reshape(LAYERS * 16, D),
            jnp.pad(table_grad, ((0, 0), (0, D - OFFSETS))),
        ],
        axis=0,
    )
    if alone:
        experts, full = None, None
        sums, sums_before = expert_sums
        attend, attend_before = attend_sums
        tiny = SmallSum(small)
        attend.run("core")
        sums.run("add_partner", "add_own", "far_low", "near_x")
        sums_before.run("add_far", "residual_row", "add_near_z", "far_z")
        attend_before.run("add", "near_z")
        at_once((), attend, sums, sums_before, attend_before)
        attend.run("add_half", "row")
        sums.run("far_high", "add_near_x", "near_z")
        sums_before.run("residual_core", "add_far_z", "back_z")
        at_once((), attend, sums, sums_before, attend_before, tiny)
        attend.run("add_half", "near_x", "add", "near_z", "add", "far_z")
        attend.run("add", "back_x", "back_row")
        sums.run("add_near_z", "far_z", "add_far_z", "add_far_halves", "residual_row")
        sums.run("back_z", "back_row", "back_x", "back_core", "residual_core")
        sums_before.run("back_row", "back_x", "back_core")
        attend_before.run("add", "far_z", "add", "back_x", "back_row", "back_core")
        for step in all_steps:
            tiny.swap(step)
            tiny.add()
        small = tiny.value
        experts = expert_outputs(
            1, expert_order, sums_before.residual_pieces(), sums_before.core_pieces(), None
        )
        full = attend_outputs(1, attend_order, attend_before.pieces(), None)
        experts, full = at_once((experts, full), attend)
        attend.run("back_core")
        experts = expert_outputs(
            0, expert_order, sums.residual_pieces(), sums.core_pieces(), experts
        )
        full = attend_outputs(0, attend_order, attend.pieces(), full)
        residual_up_grad, residual_down_grad, core_up_grad, core_down_grad = experts
        residual_down_grad = residual_down_grad.reshape(LAYERS, width, D)
        core_down_grad = core_down_grad.reshape(LAYERS, width, D)
        attend_weight_grad, output_weight_grad = full
    else:
        small = sum_all(small, all_steps)
        residual, core, full = [], [], []
        for d in range(LAYERS):
            part = scatter_sum(expert_sums[d], dp_steps)
            residual.append(gather_all(part, dp_steps))
            total = gather_all(sum_over(part, sum_steps), dp_steps)
            core.append(gather_all(total, slice_steps, dim=1))
            full.append(sum_over(attend_sums[d], all_steps))
        full = jnp.stack(full).astype(F32)
        attend_weight_grad, output_weight_grad = full[:, :, : 3 * D], full[:, :, 3 * D :]
        residual_up_grad = jnp.stack([r[:D] for r in residual]).astype(F32)
        residual_down_grad = jnp.stack([unpack_down(r[D:]) for r in residual]).astype(F32)
        core_up_grad = jnp.stack([c[:D] for c in core]).astype(F32)
        core_down_grad = jnp.stack([unpack_down(c[D:]) for c in core]).astype(F32)
    vec = small[: LAYERS * 16].reshape(LAYERS, 16, D)
    table = small[LAYERS * 16 :, :OFFSETS].reshape(LAYERS, HEADS, OFFSETS).transpose(0, 2, 1)
    return (
        block_output,
        input_grad,
        vec[:, 0],
        vec[:, 1],
        attend_weight_grad,
        table,
        output_weight_grad,
        vec[:, 2],
        vec[:, 3],
        vec[:, 8:16].transpose(0, 2, 1),
        core_up_grad,
        core_down_grad,
        residual_up_grad,
        residual_down_grad,
    )


def solution(mesh):
    placed = (
        P(("dp", "expert"), None, None),
        P(None, ("dp", "expert"), None, None),
        P(),
        P(),
        P(),
        P(),
        P(),
        P(),
        P(),
        P(),
        P(),
        P(),
        P(None, None, "expert"),
        P(None, "expert", None),
        P(("dp", "expert"), None, None),
    )
    return jax.shard_map(
        body,
        mesh=mesh,
        in_specs=placed,
        out_specs=(
            P(("dp", "expert"), None, None),
            P(("dp", "expert"), None, None),
            P(),
            P(),
            P(),
            P(),
            P(),
            P(),
            P(),
            P(),
            P(),
            P(),
            P(None, None, "expert"),
            P(None, "expert", None),
        ),
        check_vma=False,
    )
```
